32 devices in a mesh: band: 4 (over x, core), tile: 8 (over z, y).
Axes of the slice: x: 2, y: 2, z: 4, core: 2. Of those that a mesh axis runs over, the one named last changes fastest.
Arguments:
- raw_traces: bfloat16 [8, 1024, 2048], P('tile', 'band'), may hold values from -6 to 6
- bin_owner: int32 [8, 1024, 1], P('tile'), may hold values from 0 to 7; in each aligned block of 1024 rows (0 to 1023, 1024 to 2047, ..., all dimensions but the last counted through in order) at most 256 rows name the same one
- bin_offset: int32 [8, 1024], P('tile'), may hold values from 0 to 32767
Outputs:
- multiples: float32 [40, 2, 512, 512], P('band', None, 'tile')
The draws below stay inside these ranges and needn't reach their ends.
Inputs may be any that keep to these rules, and one draw needn't show every extreme that they name: `bin_owner`: in each tile's list of 1024 traces at most 256 are binned into one tile, and some tile receives exactly 256.
All inputs are finite; a program needn't handle non-finite values.
Results may differ from the reference program's by a relative error of at most 0.0067.
Values may be sent and summed in bfloat16 or wider, within the bound.
No kernel may reach another device: no remote copies, remote signals or barrier semaphores. Data moves between devices by JAX's collectives and lax.ppermute only.
A program may use at most 128 MiB of HBM per device.

```python
import math
import jax
import jax.numpy as jnp
import numpy as np
from jax import lax

NG = 512
NT = 2048
FB = 10
NF = 40
TILES = 8
TR_TILE = 1024
CAP = 256
CELLS_DEV = 32768
N_BAND = 4
N_TILE = 8


def plant(entries, own_key, low, high):
    longest = entries.shape.index(max(entries.shape))
    spots = []
    for shift in (0, 1):
        where = [jax.random.randint(jax.random.fold_in(own_key, axis), (), 0, length) for axis, length in enumerate(entries.shape)]
        where[longest] = (where[longest] + shift) % entries.shape[longest]
        spots.append(tuple(where))
    return entries.at[spots[0]].set(low).at[spots[1]].set(high)


def level_of(key, extent, cuts, least, top_value):
    def one(position, parts):
        heights = jax.random.uniform(jax.random.fold_in(jax.random.fold_in(key, 6), position), (parts,), jnp.float32, least / len(cuts), top_value / len(cuts))
        return jnp.repeat(jnp.exp(heights), extent[position] // parts).reshape((-1,) + (1,) * (len(extent) - position - 1))

    level = one(*cuts[0])
    for cut in cuts[1:]:
        level = level * one(*cut)
    return level


def shared_out(key, own, number, rows, count, top, reach, skew):
    ranking = jax.random.permutation(key, count)
    crowded, usual = shares(count, rows * top, reach, skew, True), shares(count, rows * top, reach, skew, False)
    places = jnp.arange(count)

    def named(lengths, turn):
        used = int((lengths > 0).sum())
        fixed = max(1, used // 4)
        passed = fixed + (places - fixed + turn * (used - fixed)) % max(1, count - fixed)
        return jnp.zeros((count,), jnp.int32).at[ranking[jnp.where(places < fixed, places, passed)]].set(jnp.asarray(lengths, jnp.int32))

    lengths = jnp.where(number % 4 == 0, named(crowded, number // 4), named(usual, number - number // 4 - 1))
    mixed = jax.random.permutation(jax.random.fold_in(own, 3), count)
    source_of, taker = mixed[0:count // 2 * 2:2], mixed[1:count // 2 * 2:2]
    margin = jnp.minimum(lengths[source_of] - 1, reach - lengths[taker]) // 2
    margin = jnp.where((source_of == ranking[0]) | (taker == ranking[0]) | (lengths[taker] == 0), 0, jnp.maximum(margin, 0))
    passed = jax.random.randint(jax.random.fold_in(own, 4), (count // 2,), 0, 1 << 20) % (margin + 1)
    lengths = lengths.at[source_of].add(-passed).at[taker].add(passed)
    members = jnp.searchsorted(jnp.cumsum(lengths), jnp.arange(rows * top), side="right").astype(jnp.int32)
    grid = members.reshape(top, rows).T
    grid = grid[jax.random.permutation(jax.random.fold_in(own, 1), rows)]
    turn = jax.random.randint(jax.random.fold_in(own, 2), (rows, 1), 0, top)
    return jnp.take_along_axis(grid, (jnp.arange(top)[None, :] + turn) % top, axis=1)


def shares(amount, total, limit, slope, full):
    weights = [(1 << 20) // math.isqrt(standing ** slope) + 1 for standing in range(1, amount + 1)]
    largest = limit if full else min(limit, max(-(-total // amount), total * weights[0] // sum(weights)))
    least = 1 if total - largest >= amount - 1 else 0
    given, rest = [largest] + [least] * (amount - 1), total - largest - least * (amount - 1)
    while rest > 0:
        movable = [i for i in range(1, amount) if given[i] < largest] or [i for i in range(1, amount) if given[i] < limit]
        whole, remaining = sum([weights[i] for i in movable]), rest
        for i in movable:
            more = min(limit - given[i], max(1, remaining * weights[i] // whole), rest)
            given[i] = given[i] + more
            rest = rest - more
    return np.array(given)


def centred(stream_key, shape, scale, most, split=(), kind=jnp.bfloat16):
    level = level_of(stream_key, shape, split, -0.22, 0.18) if split else 1.0
    result = jax.random.normal(stream_key, shape, jnp.float32) * scale * level
    return jnp.minimum(jnp.maximum(result, -most), most).astype(kind)


def setup_inputs(seed: int = 0) -> dict:
    splits = jax.random.split(jax.random.key(seed), 4)
    raw_traces = centred(splits[0], (TILES, TR_TILE, NT), 1.0, 6.0, ((0, 8), (1, 4)))
    bin_owner_keys = jax.random.split(jax.random.fold_in(splits[1], 1), TILES * TR_TILE // TR_TILE)
    bin_owner_turns = jax.random.permutation(jax.random.fold_in(splits[1], 3), TILES * TR_TILE // TR_TILE)
    bin_owner = jax.vmap(lambda own, number: shared_out(jax.random.fold_in(splits[1], 2), own, number, TR_TILE, N_TILE, 1, CAP, 2))(bin_owner_keys, bin_owner_turns).reshape((TILES, TR_TILE, 1))
    bin_offset = plant(jax.random.randint(splits[2], (TILES, TR_TILE), 0, CELLS_DEV), jax.random.fold_in(splits[2], 1), 0, CELLS_DEV - 1).astype(jnp.int32)
    return {"raw_traces": raw_traces, "bin_owner": bin_owner, "bin_offset": bin_offset}


def twiddle_band(first_freq, freq_count):
    time_index = jnp.arange(NT, dtype=jnp.int32)
    freq_index = jnp.arange(freq_count, dtype=jnp.int32) + first_freq + 1
    phase_angle = (time_index[:, None] * freq_index[None, :] % NT).astype(jnp.float32) * (2.0 * math.pi / NT)
    norm_factor = 1.0 / math.sqrt(NT)
    return jnp.concatenate([jnp.cos(phase_angle) * norm_factor, -jnp.sin(phase_angle) * norm_factor], axis=1).astype(jnp.bfloat16)

def reference(raw_traces, bin_owner, bin_offset):
    traces = raw_traces.reshape(TILES * TR_TILE, NT)
    cell_index = (bin_owner[:, :, 0] * CELLS_DEV + bin_offset).reshape(-1).astype(jnp.int32)
    counts = jax.ops.segment_sum(jnp.ones(cell_index.shape, jnp.float32), cell_index, NG * NG)
    divisor = jnp.maximum(counts, 1.0)
    out_scale = 1.0 / math.sqrt(NG)

    def per_band(band_index):
        twiddle = twiddle_band(band_index * FB, FB)
        spectra = jnp.dot(traces, twiddle, preferred_element_type=jnp.float32).astype(jnp.bfloat16)
        cell_sums = jax.ops.segment_sum(spectra.astype(jnp.float32), cell_index, NG * NG)
        grid_field = (cell_sums / divisor[:, None]).astype(jnp.bfloat16)
        grid_field = grid_field.T.reshape(2, FB, NG, NG).transpose(1, 0, 2, 3)
        wide = grid_field.astype(jnp.float32)
        symmetric = (0.5 * (wide + jnp.swapaxes(wide, 2, 3))).astype(jnp.bfloat16)
        real_part = symmetric[:, 0].astype(jnp.float32)
        imag_part = symmetric[:, 1].astype(jnp.float32)
        product_real = jnp.einsum('fik,fkj->fij', real_part, real_part) - jnp.einsum('fik,fkj->fij', imag_part, imag_part)
        product_imag = jnp.einsum('fik,fkj->fij', real_part, imag_part) + jnp.einsum('fik,fkj->fij', imag_part, real_part)
        return jnp.stack([product_real, product_imag], axis=1) * out_scale
    stacked = lax.map(per_band, jnp.arange(N_BAND, dtype=jnp.int32))
    return stacked.reshape(NF, 2, NG, NG)
```

```python
import functools
import math

import jax
import jax.numpy as jnp
import ml_dtypes
import numpy as np
from jax import lax
from jax.experimental import pallas as pl
from jax.experimental.pallas import tpu as pltpu
from jax.sharding import PartitionSpec as P

NG = 512
NT = 2048
FB = 10
CH = 2 * FB
ROWS = 32
BLOCK = 16
BLOCKS = NG // BLOCK
WIN = 128
STEP = 4
VMEM = 56 * 1024 * 1024


def twiddle_rows(band_count):
    time_index = np.arange(NT)[None, None, :]
    freq_index = np.arange(band_count * FB).reshape(band_count, FB, 1) + 1
    angle = (time_index * freq_index % NT) * (2.0 * math.pi / NT)
    norm = 1.0 / math.sqrt(NT)
    table = np.zeros((band_count, ROWS, NT), np.float64)
    table[:, :FB] = np.cos(angle) * norm
    table[:, FB:CH] = -np.sin(angle) * norm
    return table.reshape(band_count * ROWS, NT).astype(ml_dtypes.bfloat16)


def contract_last(left, right):
    return lax.dot_general(
        left, right, (((1,), (1,)), ((), ())), preferred_element_type=jnp.float32
    )


def rank_kernel(cells_dev, owner_ref, offset_ref, rank_ref, keys_ref, starts_ref, order, column):
    length = owner_ref.shape[1]
    cell = owner_ref[...] * cells_dev + offset_ref[...]
    place = lax.broadcasted_iota(jnp.int32, (1, length), 1)
    order[...] = cell * length + place
    for first in range(0, length, 128):
        column[first : first + 128, :] = jnp.transpose(
            jnp.broadcast_to(order[:, first : first + 128], (128, 128))
        )
    bound = jnp.minimum(lax.broadcasted_iota(jnp.int32, (1, 128), 1), BLOCKS)
    limit = bound * (BLOCK * NG * length)

    def below(bound):
        hits = (column[...] < bound).astype(jnp.int32)
        return jnp.sum(hits, axis=0, keepdims=True)

    starts_ref[...] = below(limit)

    def one(block, _):
        lanes = pl.ds(pl.multiple_of(block * 128, 128), 128)
        rank_ref[:, lanes] = below(order[:, lanes])
        return 0

    lax.fori_loop(0, length // 128, one, 0)
    source = cell // NG
    receiver = cell % NG
    row = lax.broadcasted_iota(jnp.int32, (ROWS, length), 0)
    digits = jnp.where(row == CH, source // BLOCK, 0)
    digits = jnp.where(row == CH + 1, source % BLOCK, digits)
    digits = jnp.where(row == CH + 2, receiver // 256, digits)
    digits = jnp.where(row == CH + 3, receiver % 256, digits)
    keys_ref[...] = digits.astype(jnp.float32).astype(jnp.bfloat16)


def sort_kernel(values_ref, rank_ref, keys_ref, sorted_ref, held):
    parts, _, width = values_ref.shape
    length = parts * width
    for part in range(parts):
        held[:, part * width : (part + 1) * width] = (
            values_ref[part] + keys_ref[:, part * width : (part + 1) * width]
        )
    size = 256
    rank = rank_ref[...]

    def one(block, _):
        first = pl.multiple_of(block * size, size)
        target = lax.broadcasted_iota(jnp.int32, (size, length), 0) + first
        permute = (target == rank).astype(jnp.float32).astype(jnp.bfloat16)
        sorted_ref[:, pl.ds(first, size)] = contract_last(held[...], permute).astype(
            jnp.bfloat16
        )
        return 0

    lax.fori_loop(0, length // size, one, 0)


def list_kernel(windows, starts_ref, list_ref, steps_ref):
    runs = starts_ref.shape[0]

    def block(b, _):
        def run(r, filled):
            start = starts_ref[r, b]
            end = starts_ref[r, b + 1]
            first = start // WIN
            last = jnp.where(end > start, (end + WIN - 1) // WIN, first)

            def window(w, at):
                list_ref[b, at] = r * windows + w
                return at + 1

            return lax.fori_loop(first, last, window, filled)

        filled = lax.fori_loop(0, runs, run, 0)
        steps = (filled + STEP - 1) // STEP

        def pad(at, _):
            list_ref[b, at] = -1
            return 0

        lax.fori_loop(filled, steps * STEP, pad, 0)
        steps_ref[b, 0] = steps
        return 0

    lax.fori_loop(0, BLOCKS, block, 0)


def grid_kernel(
    scale, row_block, list_ref, steps_ref, tile_ref, lists_ref, out_ref, grid, left, right, total, turned
):
    windows = lists_ref.shape[2] // WIN
    lane_row = lax.broadcasted_iota(jnp.int32, (BLOCK, WIN), 0).astype(jnp.float32)
    lane_col = lax.broadcasted_iota(jnp.int32, (NG, WIN), 0).astype(jnp.float32)

    def block(b, _):
        total[...] = jnp.zeros_like(total)

        def step(i, _):
            for q in range(STEP):
                entry = list_ref[b, i * STEP + q]
                wanted = jnp.where(entry < 0, -1, b).astype(jnp.float32)
                entry = jnp.maximum(entry, 0)
                run = entry // windows
                first = pl.multiple_of((entry % windows) * WIN, WIN)
                part = lists_ref[run, :, pl.ds(first, WIN)].astype(jnp.float32)
                hit = (part[CH : CH + 1] == wanted) & (part[CH + 1 : CH + 2] == lane_row)
                cols = slice(q * WIN, (q + 1) * WIN)
                for c in range(CH):
                    left[c * BLOCK : (c + 1) * BLOCK, cols] = jnp.where(
                        hit, part[c : c + 1], 0.0
                    ).astype(jnp.bfloat16)
                left[CH * BLOCK :, cols] = jnp.where(hit, 1.0, 0.0).astype(jnp.bfloat16)
                receiver = part[CH + 2 : CH + 3] * 256.0 + part[CH + 3 : CH + 4]
                right[:, cols] = jnp.where(receiver == lane_col, 1.0, 0.0).astype(jnp.bfloat16)
            total[...] += contract_last(left[...], right[...])
            return 0

        lax.fori_loop(0, steps_ref[b, 0], step, 0)
        inverse = 1.0 / jnp.maximum(total[CH * BLOCK :, :], 1.0)
        rows = pl.ds(pl.multiple_of(b * BLOCK, BLOCK), BLOCK)
        for c in range(CH):
            grid[c, rows, :] = (total[c * BLOCK : (c + 1) * BLOCK, :] * inverse).astype(
                jnp.bfloat16
            )
        return 0

    lax.fori_loop(0, BLOCKS, block, 0)

    first_row = pl.multiple_of(tile_ref[0] * row_block, row_block)
    first_col = pl.multiple_of(first_row // 128 * 128, 128)
    within = pl.multiple_of(first_row % 128, row_block)

    def own_rows(c):
        turned[...] = jnp.transpose(grid[c, :, pl.ds(first_col, 128)].astype(jnp.float32))
        across = turned[pl.ds(within, row_block), :]
        along = grid[c, pl.ds(first_row, row_block), :].astype(jnp.float32)
        return (0.5 * (along + across)).astype(jnp.bfloat16)

    def frequency(f, _):
        own = jnp.concatenate([own_rows(f), own_rows(FB + f)], axis=0)
        real = grid[f]
        imag = grid[FB + f]
        by_real = jnp.dot(own, real, preferred_element_type=jnp.float32) + contract_last(own, real)
        by_imag = jnp.dot(own, imag, preferred_element_type=jnp.float32) + contract_last(own, imag)
        half = 0.5 * scale
        out_ref[f, 0] = (by_real[:row_block] - by_imag[row_block:]) * half
        out_ref[f, 1] = (by_imag[:row_block] + by_real[row_block:]) * half
        return 0

    lax.fori_loop(0, FB, frequency, 0)


def whole(space=pltpu.VMEM):
    return pl.BlockSpec(memory_space=space)


def per_device(raw_traces, bin_owner, bin_offset):
    band_count = lax.axis_size("band")
    tile_count = lax.axis_size("tile")
    length = bin_offset.shape[1]
    cells_dev = NG * NG // tile_count
    row_block = NG // tile_count
    windows = length // WIN
    params = pltpu.CompilerParams(vmem_limit_bytes=VMEM)

    rank, keys, starts = pl.pallas_call(
        functools.partial(rank_kernel, cells_dev),
        out_shape=[
            jax.ShapeDtypeStruct((1, length), jnp.int32),
            jax.ShapeDtypeStruct((ROWS, length), jnp.bfloat16),
            jax.ShapeDtypeStruct((1, 128), jnp.int32),
        ],
        in_specs=[whole()] * 2,
        out_specs=[whole()] * 3,
        scratch_shapes=[
            pltpu.VMEM((1, length), jnp.int32),
            pltpu.VMEM((length, 128), jnp.int32),
        ],
        compiler_params=params,
        name="rank",
    )(bin_owner.reshape(1, length), bin_offset)
    starts_all = lax.all_gather(starts, "tile", axis=0, tiled=True)

    spectra = contract_last(jnp.asarray(twiddle_rows(band_count)), raw_traces[0]).astype(
        jnp.bfloat16
    )
    spectra = spectra.reshape(band_count, ROWS, -1)
    received = lax.all_to_all(spectra, "band", split_axis=0, concat_axis=0, tiled=True)
    ordered = pl.pallas_call(
        sort_kernel,
        out_shape=jax.ShapeDtypeStruct((ROWS, length), jnp.bfloat16),
        in_specs=[whole()] * 3,
        out_specs=whole(),
        scratch_shapes=[pltpu.VMEM((ROWS, length), jnp.bfloat16)],
        compiler_params=params,
        name="sort",
    )(received, rank, keys)
    lists = lax.all_gather(ordered[None], "tile", axis=0, tiled=True)

    most = tile_count * windows + STEP
    window_list, steps = pl.pallas_call(
        functools.partial(list_kernel, windows),
        out_shape=[
            jax.ShapeDtypeStruct((BLOCKS, most), jnp.int32),
            jax.ShapeDtypeStruct((BLOCKS, 1), jnp.int32),
        ],
        in_specs=[whole(pltpu.SMEM)],
        out_specs=[whole(pltpu.SMEM)] * 2,
        compiler_params=params,
        name="windows",
    )(starts_all)

    tile = lax.axis_index("tile").astype(jnp.int32).reshape(1)
    return pl.pallas_call(
        functools.partial(grid_kernel, 1.0 / math.sqrt(NG), row_block),
        out_shape=jax.ShapeDtypeStruct((FB, 2, row_block, NG), jnp.float32),
        in_specs=[whole(pltpu.SMEM)] * 3 + [whole()],
        out_specs=whole(),
        scratch_shapes=[
            pltpu.VMEM((CH, NG, NG), jnp.bfloat16),
            pltpu.VMEM(((CH + 1) * BLOCK, STEP * WIN), jnp.bfloat16),
            pltpu.VMEM((NG, STEP * WIN), jnp.bfloat16),
            pltpu.VMEM(((CH + 1) * BLOCK, NG), jnp.float32),
            pltpu.VMEM((128, NG), jnp.float32),
        ],
        compiler_params=params,
        name="grid",
    )(window_list, steps, tile, lists)


def solution(mesh):
    return jax.shard_map(
        per_device,
        mesh=mesh,
        in_specs=(P("tile", "band", None), P("tile", None, None), P("tile", None)),
        out_specs=P("band", None, "tile", None),
        check_vma=False,
    )
```

```python
import functools
import math

import jax
import jax.numpy as jnp
import ml_dtypes
import numpy as np
from jax import lax
from jax.experimental import pallas as pl
from jax.experimental.pallas import tpu as pltpu
from jax.sharding import PartitionSpec as P

NG = 512
NT = 2048
FB = 10
CH = 2 * FB
ROWS = 24
BLOCK = 16
BLOCKS = NG // BLOCK
GROUP = 32
COPY = 32
CHUNK = 256
UNROLL = 2
VMEM = 56 * 1024 * 1024


def twiddle_rows(band_count):
    time_index = np.arange(NT)[None, None, :]
    freq_index = np.arange(band_count * FB).reshape(band_count, FB, 1) + 1
    angle = (time_index * freq_index % NT) * (2.0 * math.pi / NT)
    norm = 1.0 / math.sqrt(NT)
    table = np.zeros((band_count, ROWS, NT), np.float64)
    table[:, :FB] = np.cos(angle) * norm
    table[:, FB:CH] = -np.sin(angle) * norm
    return table.reshape(band_count * ROWS, NT).astype(ml_dtypes.bfloat16)


def contract_last(left, right):
    return lax.dot_general(
        left, right, (((1,), (1,)), ((), ())), preferred_element_type=jnp.float32
    )


def run_kernel(cells_dev, twiddle_ref, traces_ref, owner_ref, offset_ref, out_ref):
    bands, tiles, _, count = out_ref.shape
    lanes = pl.ds(pl.multiple_of(lax.axis_index("band") * count, count), count)
    cell = owner_ref[:, lanes] * cells_dev + offset_ref[:, lanes]
    order = cell * count + lax.broadcasted_iota(jnp.int32, (1, count), 1)
    rank = jnp.zeros((1, count), jnp.int32)
    for first in range(0, count, 128):
        column = jnp.transpose(jnp.broadcast_to(order[:, first : first + 128], (128, 128)))
        column = jnp.concatenate([column] * (count // 128), axis=1)
        rank += jnp.sum((column < order).astype(jnp.int32), axis=0, keepdims=True)
    target = lax.broadcasted_iota(jnp.int32, (count, count), 0)
    permute = (target == rank).astype(jnp.float32).astype(jnp.bfloat16)
    source = cell // NG
    receiver = cell % NG
    row = lax.broadcasted_iota(jnp.int32, (bands * ROWS, count), 0) % ROWS
    digits = jnp.where(row == CH, source // BLOCK, 0)
    digits = jnp.where(row == CH + 1, source % BLOCK, digits)
    digits = jnp.where(row == CH + 2, receiver // 256, digits)
    digits = jnp.where(row == CH + 3, receiver % 256, digits)
    spectra = contract_last(twiddle_ref[...], traces_ref[0])
    packed = (spectra + digits.astype(jnp.float32)).astype(jnp.bfloat16)
    ordered = contract_last(packed, permute)
    for band in range(bands):
        part = ordered[band * ROWS : (band + 1) * ROWS].astype(jnp.bfloat16)
        for tile in range(tiles):
            out_ref[band, tile] = part


def merge_group(first_run, lists_ref, flat, packed, keys, counts, counts_s, chunks_s, sem):
    length = lists_ref.shape[2]

    for r in range(GROUP):
        part = lists_ref[first_run + r].astype(jnp.float32)
        keys[r : r + 1, :] = part[CH : CH + 1]
        for first in range(0, length, 128):
            at = r * length + first
            flat[at : at + 128, :ROWS] = jnp.transpose(part[:, first : first + 128])

    block_of = keys[...]
    lane = lax.broadcasted_iota(jnp.int32, (GROUP, 128), 1)
    starts = jnp.zeros((GROUP, 128), jnp.float32)
    for b in range(1, BLOCKS + 1):
        below = jnp.sum((block_of < float(b)).astype(jnp.float32), axis=1, keepdims=True)
        starts = jnp.where(lane == b, below, starts)
    starts = starts.astype(jnp.int32)
    widest = jnp.max(pltpu.roll(starts, 127, 1) - starts, axis=0, keepdims=True)
    counts[:GROUP, :] = starts
    counts[GROUP:, :] = jnp.broadcast_to(widest, (8, 128))
    copy = pltpu.make_async_copy(counts, counts_s, sem)
    copy.start()
    copy.wait()

    def block(b, carry):
        base, filled = carry

        def plain():
            at = base
            for r in range(GROUP):
                start = counts_s[r, b]
                packed[pl.ds(at, COPY), :] = flat[pl.ds(r * length + start, COPY), :]
                at = at + (counts_s[r, b + 1] - start)
            return at

        def long():
            def run(r, at):
                start = counts_s[r, b]
                size = counts_s[r, b + 1] - start

                def piece(k, _):
                    packed[pl.ds(at + 8 * k, 8), :] = flat[pl.ds(r * length + start + 8 * k, 8), :]
                    return 0

                lax.fori_loop(0, (size + 7) // 8, piece, 0)
                return at + size

            return lax.fori_loop(0, GROUP, run, base)

        end = lax.cond(counts_s[GROUP, b] <= COPY, plain, long)
        size = end - base

        def entry(k, at):
            chunks_s[0, at] = b
            chunks_s[1, at] = base + k * CHUNK
            chunks_s[2, at] = size - k * CHUNK
            return at + 1

        filled = lax.fori_loop(0, (size + CHUNK - 1) // CHUNK, entry, filled)
        return (end + 7) // 8 * 8, filled

    _, filled = lax.fori_loop(0, BLOCKS, block, (jnp.int32(0), jnp.int32(0)))
    padded = (filled + UNROLL - 1) // UNROLL * UNROLL

    def pad(at, _):
        chunks_s[0, at] = 0
        chunks_s[1, at] = 0
        chunks_s[2, at] = 0
        return 0

    lax.fori_loop(filled, padded, pad, 0)
    return padded


def add_chunks(chunk_count, packed, chunks_s, grid):
    row = lax.broadcasted_iota(jnp.int32, (BLOCK, CHUNK), 0).astype(jnp.float32)
    place = lax.broadcasted_iota(jnp.int32, (BLOCK, CHUNK), 1)
    column = lax.broadcasted_iota(jnp.int32, (NG, CHUNK), 0).astype(jnp.float32)

    def product(i):
        first = pl.multiple_of(chunks_s[1, i], 8)
        part = jnp.concatenate(
            [
                jnp.transpose(packed[pl.ds(first + k, 128), :])[:ROWS]
                for k in range(0, CHUNK, 128)
            ],
            axis=1,
        )
        hit = (part[CH + 1 : CH + 2] == row) & (place < chunks_s[2, i])
        left = [jnp.where(hit, part[c : c + 1], 0.0).astype(jnp.bfloat16) for c in range(CH)]
        left.append(jnp.where(hit, 1.0, 0.0).astype(jnp.bfloat16))
        receiver = part[CH + 2 : CH + 3] * 256.0 + part[CH + 3 : CH + 4]
        right = jnp.where(receiver == column, 1.0, 0.0).astype(jnp.bfloat16)
        return contract_last(jnp.concatenate(left, axis=0), right)

    def body(step, _):
        products = [product(step * UNROLL + q) for q in range(UNROLL)]
        for q in range(UNROLL):
            rows = pl.ds(pl.multiple_of(chunks_s[0, step * UNROLL + q] * BLOCK, BLOCK), BLOCK)
            for c in range(CH + 1):
                grid[c, rows, :] += products[q][c * BLOCK : (c + 1) * BLOCK]
        return 0

    lax.fori_loop(0, chunk_count // UNROLL, body, 0)


def grid_kernel(
    scale, row_block, lists_ref, out_ref, grid, planes, flat, packed, keys, counts, turned,
    counts_s, chunks_s, sem
):
    runs = lists_ref.shape[0]
    grid[...] = jnp.zeros_like(grid)

    def group(g):
        chunk_count = merge_group(
            g * GROUP, lists_ref, flat, packed, keys, counts, counts_s, chunks_s, sem
        )
        add_chunks(chunk_count, packed, chunks_s, grid)

    if runs == GROUP:
        group(0)
    else:
        lax.fori_loop(0, runs // GROUP, lambda g, _: (group(g), 0)[1], 0)

    grid[CH] = 1.0 / jnp.maximum(grid[CH], 1.0)

    first_row = pl.multiple_of(lax.axis_index("tile") * row_block, row_block)
    first_col = pl.multiple_of(first_row // 128 * 128, 128)
    within = pl.multiple_of(first_row % 128, row_block)

    def own_rows(p):
        turned[...] = jnp.transpose(planes[p, :, pl.ds(first_col, 128)].astype(jnp.float32))
        across = turned[pl.ds(within, row_block), :]
        along = planes[p, pl.ds(first_row, row_block), :].astype(jnp.float32)
        return (0.5 * (along + across)).astype(jnp.bfloat16)

    def frequency(f, _):
        planes[0] = (grid[f] * grid[CH]).astype(jnp.bfloat16)
        planes[1] = (grid[FB + f] * grid[CH]).astype(jnp.bfloat16)
        own = jnp.concatenate([own_rows(0), own_rows(1)], axis=0)
        real = planes[0]
        imag = planes[1]
        by_real = jnp.dot(own, real, preferred_element_type=jnp.float32) + contract_last(own, real)
        by_imag = jnp.dot(own, imag, preferred_element_type=jnp.float32) + contract_last(own, imag)
        half = 0.5 * scale
        out_ref[f, 0] = (by_real[:row_block] - by_imag[row_block:]) * half
        out_ref[f, 1] = (by_imag[:row_block] + by_real[row_block:]) * half
        return 0

    lax.fori_loop(0, FB, frequency, 0)


def whole(space=pltpu.VMEM):
    return pl.BlockSpec(memory_space=space)


def per_device(raw_traces, bin_owner, bin_offset):
    band_count = lax.axis_size("band")
    tile_count = lax.axis_size("tile")
    length = bin_offset.shape[1]
    count = raw_traces.shape[1]
    cells_dev = NG * NG // tile_count
    row_block = NG // tile_count
    runs = band_count * tile_count
    params = pltpu.CompilerParams(vmem_limit_bytes=VMEM)

    own = pl.pallas_call(
        functools.partial(run_kernel, cells_dev),
        out_shape=jax.ShapeDtypeStruct((band_count, tile_count, ROWS, count), jnp.bfloat16),
        in_specs=[whole()] * 4,
        out_specs=whole(),
        compiler_params=params,
        name="own_run",
    )(
        jnp.asarray(twiddle_rows(band_count)),
        raw_traces,
        bin_owner.reshape(1, length),
        bin_offset,
    )
    lists = lax.all_to_all(
        own.reshape(runs, ROWS, count), ("band", "tile"), split_axis=0, concat_axis=0, tiled=True
    )

    traces = GROUP * count
    slots = traces + BLOCKS * 8 + CHUNK + COPY
    return pl.pallas_call(
        functools.partial(grid_kernel, 1.0 / math.sqrt(NG), row_block),
        out_shape=jax.ShapeDtypeStruct((FB, 2, row_block, NG), jnp.float32),
        in_specs=[whole()],
        out_specs=whole(),
        scratch_shapes=[
            pltpu.VMEM((CH + 1, NG, NG), jnp.float32),
            pltpu.VMEM((2, NG, NG), jnp.bfloat16),
            pltpu.VMEM((traces + COPY, 128), jnp.float32),
            pltpu.VMEM((slots, 128), jnp.float32),
            pltpu.VMEM((GROUP, count), jnp.float32),
            pltpu.VMEM((GROUP + 8, 128), jnp.int32),
            pltpu.VMEM((128, NG), jnp.float32),
            pltpu.SMEM((GROUP + 8, 128), jnp.int32),
            pltpu.SMEM((3, traces // CHUNK + BLOCKS + UNROLL), jnp.int32),
            pltpu.SemaphoreType.DMA,
        ],
        compiler_params=params,
        name="grid",
    )(lists)


def solution(mesh):
    return jax.shard_map(
        per_device,
        mesh=mesh,
        in_specs=(P("tile", "band", None), P("tile", None, None), P("tile", None)),
        out_specs=P("band", None, "tile", None),
        check_vma=False,
    )
```

```python
import functools
import math

import jax
import jax.numpy as jnp
import ml_dtypes
import numpy as np
from jax import lax
from jax.experimental import pallas as pl
from jax.experimental.pallas import tpu as pltpu
from jax.sharding import PartitionSpec as P

NG = 512
NT = 2048
FB = 10
CH = 2 * FB
ROWS = 24
BLOCK = 16
BLOCKS = NG // BLOCK
GROUP = 32
COPY = 32
SMALL = 256
LARGE = 512
UNROLL = 2
VMEM = 56 * 1024 * 1024


def twiddle_rows(band_count):
    time_index = np.arange(NT)[None, None, :]
    freq_index = np.arange(band_count * FB).reshape(band_count, FB, 1) + 1
    angle = (time_index * freq_index % NT) * (2.0 * math.pi / NT)
    norm = 1.0 / math.sqrt(NT)
    table = np.zeros((band_count, ROWS, NT), np.float64)
    table[:, :FB] = np.cos(angle) * norm
    table[:, FB:CH] = -np.sin(angle) * norm
    return table.reshape(band_count * ROWS, NT).astype(ml_dtypes.bfloat16)


def contract_last(left, right):
    return lax.dot_general(
        left, right, (((1,), (1,)), ((), ())), preferred_element_type=jnp.float32
    )


def run_kernel(cells_dev, twiddle_ref, traces_ref, owner_ref, offset_ref, out_ref):
    bands, tiles, _, count = out_ref.shape
    lanes = pl.ds(pl.multiple_of(lax.axis_index("band") * count, count), count)
    cell = owner_ref[:, lanes] * cells_dev + offset_ref[:, lanes]
    order = cell * count + lax.broadcasted_iota(jnp.int32, (1, count), 1)
    rank = jnp.zeros((1, count), jnp.int32)
    for first in range(0, count, 128):
        column = jnp.transpose(jnp.broadcast_to(order[:, first : first + 128], (128, 128)))
        column = jnp.concatenate([column] * (count // 128), axis=1)
        rank += jnp.sum((column < order).astype(jnp.int32), axis=0, keepdims=True)
    target = lax.broadcasted_iota(jnp.int32, (count, count), 0)
    permute = (target == rank).astype(jnp.float32).astype(jnp.bfloat16)
    source = cell // NG
    receiver = cell % NG
    row = lax.broadcasted_iota(jnp.int32, (bands * ROWS, count), 0) % ROWS
    digits = jnp.where(row == CH, source // BLOCK, 0)
    digits = jnp.where(row == CH + 1, source % BLOCK, digits)
    digits = jnp.where(row == CH + 2, receiver // 256, digits)
    digits = jnp.where(row == CH + 3, receiver % 256, digits)
    spectra = contract_last(twiddle_ref[...], traces_ref[0])
    packed = (spectra + digits.astype(jnp.float32)).astype(jnp.bfloat16)
    ordered = contract_last(packed, permute)
    for band in range(bands):
        part = ordered[band * ROWS : (band + 1) * ROWS].astype(jnp.bfloat16)
        for tile in range(tiles):
            out_ref[band, tile] = part


def merge_group(first_run, lists_ref, flat, packed, keys, counts, counts_s, lists_s, sem, alone):
    length = lists_ref.shape[2]

    for r in range(GROUP):
        keys[r : r + 1, :] = lists_ref[first_run + r].astype(jnp.float32)[CH : CH + 1]
    block_of = keys[...]
    lane = lax.broadcasted_iota(jnp.int32, (GROUP, 128), 1)
    starts = jnp.zeros((GROUP, 128), jnp.float32)
    for b in range(1, BLOCKS + 1):
        below = jnp.sum((block_of < float(b)).astype(jnp.float32), axis=1, keepdims=True)
        starts = jnp.where(lane == b, below, starts)
    starts = starts.astype(jnp.int32)
    widest = jnp.max(pltpu.roll(starts, 127, 1) - starts, axis=0, keepdims=True)
    counts[:GROUP, :] = starts
    counts[GROUP:, :] = jnp.broadcast_to(widest, (8, 128))
    copy = pltpu.make_async_copy(counts, counts_s, sem)
    copy.start()
    for r in range(GROUP):
        part = lists_ref[first_run + r].astype(jnp.float32)
        for first in range(0, length, 128):
            at = r * length + first
            flat[at : at + 128, :ROWS] = jnp.transpose(part[:, first : first + 128])
    copy.wait()

    def block(b, carry):
        base, filled = carry[0], list(carry[1:])

        def plain():
            at = base
            for r in range(GROUP):
                start = counts_s[r, b]
                packed[pl.ds(at, COPY), :] = flat[pl.ds(r * length + start, COPY), :]
                at = at + (counts_s[r, b + 1] - start)
            return at

        def long():
            def run(r, at):
                start = counts_s[r, b]
                size = counts_s[r, b + 1] - start

                def piece(k, _):
                    packed[pl.ds(at + 8 * k, 8), :] = flat[pl.ds(r * length + start + 8 * k, 8), :]
                    return 0

                lax.fori_loop(0, (size + 7) // 8, piece, 0)
                return at + size

            return lax.fori_loop(0, GROUP, run, base)

        end = lax.cond(counts_s[GROUP, b] <= COPY, plain, long)
        size = end - base
        kind = (size > SMALL).astype(jnp.int32) + (size > LARGE).astype(jnp.int32)
        at = jnp.where(kind == 0, filled[0], jnp.where(kind == 1, filled[1], filled[2]))
        lists_s[3 * kind, at] = b
        lists_s[3 * kind + 1, at] = base
        lists_s[3 * kind + 2, at] = size
        filled = [filled[k] + (kind == k).astype(jnp.int32) for k in range(3)]
        return ((end + 7) // 8 * 8, *filled)

    zero = jnp.int32(0)
    _, *filled = lax.fori_loop(0, BLOCKS, block, (zero,) * 4)
    for kind in range(2):

        def pad(at, _, kind=kind):
            last = at - 1
            lists_s[3 * kind, at] = lists_s[3 * kind, last]
            lists_s[3 * kind + 1, at] = lists_s[3 * kind + 1, last]
            lists_s[3 * kind + 2, at] = lists_s[3 * kind + 2, last] if alone else 0
            return 0

        whole_steps = (filled[kind] + UNROLL - 1) // UNROLL * UNROLL
        lax.fori_loop(filled[kind], whole_steps, pad, 0)
        filled[kind] = whole_steps
    return filled


def product(first, size, width, packed):
    part = jnp.concatenate(
        [jnp.transpose(packed[pl.ds(first + k, 128), :])[:ROWS] for k in range(0, width, 128)],
        axis=1,
    )
    step = lax.broadcasted_iota(jnp.int32, (BLOCK, width), 0).astype(jnp.float32)
    step = step.astype(jnp.bfloat16)
    place = lax.broadcasted_iota(jnp.int32, (1, width), 1)
    one = jnp.ones((), jnp.bfloat16)
    none = jnp.zeros((), jnp.bfloat16)

    def spread(row):
        return jnp.broadcast_to(row, (BLOCK, width)).astype(jnp.bfloat16)

    hit = spread(jnp.where(place < size, part[CH + 1 : CH + 2], -1.0)) == step
    left = [jnp.where(hit, spread(part[c : c + 1]), none) for c in range(CH)]
    left.append(jnp.where(hit, one, none))
    right = []
    for half in range(NG // 256):
        low = spread(jnp.where(part[CH + 2 : CH + 3] == float(half), part[CH + 3 : CH + 4], -1.0))
        for j in range(0, 256, BLOCK):
            right.append(jnp.where(low == step + jnp.bfloat16(j), one, none))
    return contract_last(jnp.concatenate(left, axis=0), jnp.concatenate(right, axis=0))


def block_rows(b):
    return pl.ds(pl.multiple_of(b * BLOCK, BLOCK), BLOCK)


def add_blocks(filled, packed, lists_s, total, emit):
    for kind, width in ((0, SMALL), (1, LARGE)):

        def body(step, _, kind=kind, width=width):
            sums = []
            for q in range(UNROLL):
                at = step * UNROLL + q
                first = pl.multiple_of(lists_s[3 * kind + 1, at], 8)
                sums.append(product(first, lists_s[3 * kind + 2, at], width, packed))
            for q in range(UNROLL):
                emit(lists_s[3 * kind, step * UNROLL + q], sums[q])
            return 0

        lax.fori_loop(0, filled[kind] // UNROLL, body, 0)

    def long(at, _):
        total[...] = jnp.zeros_like(total)
        size = lists_s[8, at]

        def piece(k, _):
            first = pl.multiple_of(lists_s[7, at] + k * LARGE, 8)
            total[...] += product(first, size - k * LARGE, LARGE, packed)
            return 0

        lax.fori_loop(0, (size + LARGE - 1) // LARGE, piece, 0)
        emit(lists_s[6, at], total[...])
        return 0

    lax.fori_loop(0, filled[2], long, 0)


def grid_kernel(
    scale, row_block, lists_ref, out_ref, planes, flat, packed, keys, counts, turned, total,
    counts_s, lists_s, sem, grid=None
):
    runs = lists_ref.shape[0]
    alone = runs == GROUP

    def finish(sums, inverse, rows):
        for c in range(CH):
            planes[c, rows, :] = (sums(c) * inverse).astype(jnp.bfloat16)

    def emit(b, sums):
        rows = block_rows(b)
        if alone:
            inverse = 1.0 / jnp.maximum(sums[CH * BLOCK :], 1.0)
            finish(lambda c: sums[c * BLOCK : (c + 1) * BLOCK], inverse, rows)
        else:
            for c in range(CH + 1):
                grid[c, rows, :] += sums[c * BLOCK : (c + 1) * BLOCK]

    def group(g, _):
        filled = merge_group(
            g * GROUP, lists_ref, flat, packed, keys, counts, counts_s, lists_s, sem, alone
        )
        add_blocks(filled, packed, lists_s, total, emit)
        return 0

    if alone:
        group(0, 0)
    else:
        grid[...] = jnp.zeros_like(grid)
        lax.fori_loop(0, runs // GROUP, group, 0)

        def divide(b, _):
            rows = block_rows(b)
            finish(lambda c: grid[c, rows, :], 1.0 / jnp.maximum(grid[CH, rows, :], 1.0), rows)
            return 0

        lax.fori_loop(0, BLOCKS, divide, 0)

    first_row = pl.multiple_of(lax.axis_index("tile") * row_block, row_block)
    first_col = pl.multiple_of(first_row // 128 * 128, 128)
    within = pl.multiple_of(first_row % 128, row_block)

    def own_rows(p, slot):
        turned[slot] = jnp.transpose(planes[p, :, pl.ds(first_col, 128)].astype(jnp.float32))
        across = turned[slot, pl.ds(within, row_block), :]
        along = planes[p, pl.ds(first_row, row_block), :].astype(jnp.float32)
        return (0.5 * (along + across)).astype(jnp.bfloat16)

    def frequency(f, slot):
        own = jnp.concatenate([own_rows(f, slot), own_rows(FB + f, slot + 1)], axis=0)
        real = planes[f]
        imag = planes[FB + f]
        by_real = jnp.dot(own, real, preferred_element_type=jnp.float32) + contract_last(own, real)
        by_imag = jnp.dot(own, imag, preferred_element_type=jnp.float32) + contract_last(own, imag)
        half = 0.5 * scale
        out_ref[f, 0] = (by_real[:row_block] - by_imag[row_block:]) * half
        out_ref[f, 1] = (by_imag[:row_block] + by_real[row_block:]) * half

    def pair(i, _):
        frequency(2 * i, 0)
        frequency(2 * i + 1, 2)
        return 0

    lax.fori_loop(0, FB // 2, pair, 0)


def whole(space=pltpu.VMEM):
    return pl.BlockSpec(memory_space=space)


def per_device(raw_traces, bin_owner, bin_offset):
    band_count = lax.axis_size("band")
    tile_count = lax.axis_size("tile")
    length = bin_offset.shape[1]
    count = raw_traces.shape[1]
    cells_dev = NG * NG // tile_count
    row_block = NG // tile_count
    runs = band_count * tile_count
    params = pltpu.CompilerParams(vmem_limit_bytes=VMEM)

    own = pl.pallas_call(
        functools.partial(run_kernel, cells_dev),
        out_shape=jax.ShapeDtypeStruct((band_count, tile_count, ROWS, count), jnp.bfloat16),
        in_specs=[whole()] * 4,
        out_specs=whole(),
        compiler_params=params,
        name="own_run",
    )(
        jnp.asarray(twiddle_rows(band_count)),
        raw_traces,
        bin_owner.reshape(1, length),
        bin_offset,
    )
    lists = lax.all_to_all(
        own.reshape(runs, ROWS, count), ("band", "tile"), split_axis=0, concat_axis=0, tiled=True
    )

    traces = GROUP * count
    slots = traces + BLOCKS * 8 + LARGE + COPY
    scratch = [
        pltpu.VMEM((CH, NG, NG), jnp.bfloat16),
        pltpu.VMEM((traces + COPY, 128), jnp.float32),
        pltpu.VMEM((slots, 128), jnp.float32),
        pltpu.VMEM((GROUP, count), jnp.float32),
        pltpu.VMEM((GROUP + 8, 128), jnp.int32),
        pltpu.VMEM((4, 128, NG), jnp.float32),
        pltpu.VMEM(((CH + 1) * BLOCK, NG), jnp.float32),
        pltpu.SMEM((GROUP + 8, 128), jnp.int32),
        pltpu.SMEM((9, BLOCKS + UNROLL), jnp.int32),
        pltpu.SemaphoreType.DMA,
    ]
    if runs != GROUP:
        scratch.append(pltpu.VMEM((CH + 1, NG, NG), jnp.float32))
    return pl.pallas_call(
        functools.partial(grid_kernel, 1.0 / math.sqrt(NG), row_block),
        out_shape=jax.ShapeDtypeStruct((FB, 2, row_block, NG), jnp.float32),
        in_specs=[whole()],
        out_specs=whole(),
        scratch_shapes=scratch,
        compiler_params=params,
        name="grid",
    )(lists)


def solution(mesh):
    return jax.shard_map(
        per_device,
        mesh=mesh,
        in_specs=(P("tile", "band", None), P("tile", None, None), P("tile", None)),
        out_specs=P("band", None, "tile", None),
        check_vma=False,
    )
```

```python
import functools
import math

import jax
import jax.numpy as jnp
import ml_dtypes
import numpy as np
from jax import lax
from jax.experimental import pallas as pl
from jax.experimental.pallas import tpu as pltpu
from jax.sharding import PartitionSpec as P

NG = 512
NT = 2048
FB = 10
CH = 2 * FB
ROWS = 24
BLOCK = 16
BLOCKS = NG // BLOCK
GROUP = 32
COPY = 32
SMALL = 256
LARGE = 512
SIDE = 4
VMEM = 56 * 1024 * 1024


def twiddle_rows(band_count):
    time_index = np.arange(NT)[None, None, :]
    freq_index = np.arange(band_count * FB).reshape(band_count, FB, 1) + 1
    angle = (time_index * freq_index % NT) * (2.0 * math.pi / NT)
    norm = 1.0 / math.sqrt(NT)
    table = np.zeros((band_count, ROWS, NT), np.float64)
    table[:, :FB] = np.cos(angle) * norm
    table[:, FB:CH] = -np.sin(angle) * norm
    return table.reshape(band_count * ROWS, NT).astype(ml_dtypes.bfloat16)


def contract_last(left, right):
    return lax.dot_general(
        left, right, (((1,), (1,)), ((), ())), preferred_element_type=jnp.float32
    )


def run_kernel(cells_dev, twiddle_ref, traces_ref, owner_ref, offset_ref, out_ref):
    bands, tiles, _, count = out_ref.shape
    lanes = pl.ds(pl.multiple_of(lax.axis_index("band") * count, count), count)
    cell = owner_ref[:, lanes] * cells_dev + offset_ref[:, lanes]
    order = cell * count + lax.broadcasted_iota(jnp.int32, (1, count), 1)
    rank = jnp.zeros((1, count), jnp.int32)
    for first in range(0, count, 128):
        column = jnp.transpose(jnp.broadcast_to(order[:, first : first + 128], (128, 128)))
        column = jnp.concatenate([column] * (count // 128), axis=1)
        rank += jnp.sum((column < order).astype(jnp.int32), axis=0, keepdims=True)
    target = lax.broadcasted_iota(jnp.int32, (count, count), 0)
    permute = (target == rank).astype(jnp.float32).astype(jnp.bfloat16)
    source = cell // NG
    receiver = cell % NG
    row = lax.broadcasted_iota(jnp.int32, (bands * ROWS, count), 0) % ROWS
    digits = jnp.where(row == CH, source // BLOCK, 0)
    digits = jnp.where(row == CH + 1, source % BLOCK, digits)
    digits = jnp.where(row == CH + 2, receiver // 256, digits)
    digits = jnp.where(row == CH + 3, receiver % 256, digits)
    spectra = contract_last(twiddle_ref[...], traces_ref[0])
    packed = (spectra + digits.astype(jnp.float32)).astype(jnp.bfloat16)
    ordered = contract_last(packed, permute)
    for band in range(bands):
        part = ordered[band * ROWS : (band + 1) * ROWS].astype(jnp.bfloat16)
        for tile in range(tiles):
            out_ref[band, tile] = part


def make_table(first_run, lists_ref, keys, table, table_s, sem):
    length = lists_ref.shape[2]
    for r in range(GROUP):
        keys[r : r + 1, :] = lists_ref[first_run + r].astype(jnp.float32)[CH : CH + 1]
    block_of = keys[...]
    lane = lax.broadcasted_iota(jnp.int32, (GROUP, 128), 1)
    starts = jnp.zeros((GROUP, 128), jnp.float32)
    for b in range(1, BLOCKS + 1):
        below = jnp.sum((block_of < float(b)).astype(jnp.float32), axis=1, keepdims=True)
        starts = jnp.where(lane == b, below, starts)
    sizes = jnp.where(lane < BLOCKS, pltpu.roll(starts, 127, 1) - starts, 0.0)
    earlier = lax.broadcasted_iota(jnp.int32, (GROUP, GROUP), 0) > lax.broadcasted_iota(
        jnp.int32, (GROUP, GROUP), 1
    )
    targets = jnp.dot(
        earlier.astype(jnp.float32).astype(jnp.bfloat16),
        sizes.astype(jnp.bfloat16),
        preferred_element_type=jnp.float32,
    )
    run = lax.broadcasted_iota(jnp.int32, (GROUP, 128), 0)
    table[:GROUP, :] = starts.astype(jnp.int32) + run * length
    table[GROUP : 2 * GROUP, :] = targets.astype(jnp.int32)
    widest = jnp.max(sizes, axis=0, keepdims=True)
    total = jnp.sum(sizes, axis=0, keepdims=True)
    last = lax.broadcasted_iota(jnp.int32, (8, 128), 0)
    table[2 * GROUP :, :] = jnp.where(last == 0, widest, total).astype(jnp.int32)
    copy = pltpu.make_async_copy(table, table_s, sem)
    copy.start()
    return copy


def turn_runs(first_run, lists_ref, flat):
    length = lists_ref.shape[2]
    for r in range(GROUP):
        part = lists_ref[first_run + r].astype(jnp.float32)
        for first in range(0, length, 128):
            at = r * length + first
            flat[at : at + 128, :ROWS] = jnp.transpose(part[:, first : first + 128])


def product(first, size, width, packed):
    part = jnp.concatenate(
        [jnp.transpose(packed[pl.ds(first + k, 128), :])[:ROWS] for k in range(0, width, 128)],
        axis=1,
    )
    step = lax.broadcasted_iota(jnp.int32, (BLOCK, width), 0).astype(jnp.float32)
    step = step.astype(jnp.bfloat16)
    place = lax.broadcasted_iota(jnp.int32, (1, width), 1)
    one = jnp.ones((), jnp.bfloat16)
    none = jnp.zeros((), jnp.bfloat16)

    def spread(row):
        return jnp.broadcast_to(row, (BLOCK, width)).astype(jnp.bfloat16)

    hit = spread(jnp.where(place < size, part[CH + 1 : CH + 2], -1.0)) == step
    left = [jnp.where(hit, spread(part[c : c + 1]), none) for c in range(CH)]
    left.append(jnp.where(hit, one, none))
    right = []
    for half in range(NG // 256):
        low = spread(jnp.where(part[CH + 2 : CH + 3] == float(half), part[CH + 3 : CH + 4], -1.0))
        for j in range(0, 256, BLOCK):
            right.append(jnp.where(low == step + jnp.bfloat16(j), one, none))
    return contract_last(jnp.concatenate(left, axis=0), jnp.concatenate(right, axis=0))


def block_rows(b):
    return pl.ds(pl.multiple_of(b * BLOCK, BLOCK), BLOCK)


def add_blocks(table_s, flat, buffers, packed, total, emit):
    def fast(b, width):
        sums = []
        for q in range(SIDE):
            buffer = buffers[q]
            for r in range(GROUP):
                buffer[pl.ds(table_s[GROUP + r, b + q], COPY), :] = flat[
                    pl.ds(table_s[r, b + q], COPY), :
                ]
            sums.append(product(0, table_s[2 * GROUP + 1, b + q], width, buffer))
        for q in range(SIDE):
            emit(b + q, sums[q])

    def slow(b):
        def run(r, _):
            source = table_s[r, b]
            target = table_s[GROUP + r, b]
            after = table_s[2 * GROUP + 1, b]
            after = jnp.where(r + 1 < GROUP, table_s[jnp.minimum(GROUP + r + 1, 2 * GROUP - 1), b], after)

            def piece(k, _):
                packed[pl.ds(target + 8 * k, 8), :] = flat[pl.ds(source + 8 * k, 8), :]
                return 0

            return lax.fori_loop(0, (after - target + 7) // 8, piece, 0)

        lax.fori_loop(0, GROUP, run, 0)
        total[...] = jnp.zeros_like(total)
        size = table_s[2 * GROUP + 1, b]

        def piece(k, _):
            first = pl.multiple_of(k * LARGE, LARGE)
            total[...] += product(first, size - first, LARGE, packed)
            return 0

        lax.fori_loop(0, (size + LARGE - 1) // LARGE, piece, 0)
        emit(b, total[...])

    def side(i, _):
        b = i * SIDE
        widest = table_s[2 * GROUP, b]
        largest = table_s[2 * GROUP + 1, b]
        for q in range(1, SIDE):
            widest = jnp.maximum(widest, table_s[2 * GROUP, b + q])
            largest = jnp.maximum(largest, table_s[2 * GROUP + 1, b + q])
        plain = widest <= COPY

        @pl.when(plain & (largest <= SMALL))
        def _():
            fast(b, SMALL)

        @pl.when(plain & (largest > SMALL) & (largest <= LARGE))
        def _():
            fast(b, LARGE)

        @pl.when(jnp.logical_not(plain) | (largest > LARGE))
        def _():
            lax.fori_loop(0, SIDE, lambda q, _: (slow(b + q), 0)[1], 0)

        return 0

    lax.fori_loop(0, BLOCKS // SIDE, side, 0)


def grid_kernel(
    scale, row_block, lists_ref, out_ref, planes, flat, packed, keys, table, turned, total, result,
    table_s, sem, out_sems, *rest
):
    runs = lists_ref.shape[0]
    alone = runs == GROUP
    buffers = rest[:SIDE]
    grid = rest[SIDE] if not alone else None

    def finish(sums, inverse, rows):
        for c in range(CH):
            planes[c, rows, :] = (sums(c) * inverse).astype(jnp.bfloat16)

    def emit(b, sums):
        rows = block_rows(b)
        if alone:
            inverse = 1.0 / jnp.maximum(sums[CH * BLOCK :], 1.0)
            finish(lambda c: sums[c * BLOCK : (c + 1) * BLOCK], inverse, rows)
        else:
            for c in range(CH + 1):
                grid[c, rows, :] += sums[c * BLOCK : (c + 1) * BLOCK]

    def group(g, _):
        copy = make_table(g * GROUP, lists_ref, keys, table, table_s, sem)
        turn_runs(g * GROUP, lists_ref, flat)
        copy.wait()
        add_blocks(table_s, flat, buffers, packed, total, emit)
        return 0

    if alone:
        group(0, 0)
    else:
        grid[...] = jnp.zeros_like(grid)
        lax.fori_loop(0, runs // GROUP, group, 0)

        def divide(b, _):
            rows = block_rows(b)
            finish(lambda c: grid[c, rows, :], 1.0 / jnp.maximum(grid[CH, rows, :], 1.0), rows)
            return 0

        lax.fori_loop(0, BLOCKS, divide, 0)

    first_row = pl.multiple_of(lax.axis_index("tile") * row_block, row_block)
    first_col = pl.multiple_of(first_row // 128 * 128, 128)
    within = pl.multiple_of(first_row % 128, row_block)

    def own_rows(p, slot):
        turned[slot] = jnp.transpose(planes[p, :, pl.ds(first_col, 128)].astype(jnp.float32))
        across = turned[slot, pl.ds(within, row_block), :]
        along = planes[p, pl.ds(first_row, row_block), :].astype(jnp.float32)
        return (0.5 * (along + across)).astype(jnp.bfloat16)

    def sent(f):
        return pltpu.make_async_copy(result.at[f], out_ref.at[f], out_sems.at[f])

    def frequency(f, slot):
        own = jnp.concatenate([own_rows(f, slot), own_rows(FB + f, slot + 1)], axis=0)
        real = planes[f]
        imag = planes[FB + f]
        by_real = jnp.dot(own, real, preferred_element_type=jnp.float32) + contract_last(own, real)
        by_imag = jnp.dot(own, imag, preferred_element_type=jnp.float32) + contract_last(own, imag)
        half = 0.5 * scale
        result[f, 0] = (by_real[:row_block] - by_imag[row_block:]) * half
        result[f, 1] = (by_imag[:row_block] + by_real[row_block:]) * half
        sent(f).start()

    def pair(i, _):
        frequency(2 * i, 0)
        frequency(2 * i + 1, 2)
        return 0

    lax.fori_loop(0, FB // 2, pair, 0)
    for f in range(FB):
        sent(f).wait()


def whole(space=pltpu.VMEM):
    return pl.BlockSpec(memory_space=space)


def per_device(raw_traces, bin_owner, bin_offset):
    band_count = lax.axis_size("band")
    tile_count = lax.axis_size("tile")
    length = bin_offset.shape[1]
    count = raw_traces.shape[1]
    cells_dev = NG * NG // tile_count
    row_block = NG // tile_count
    runs = band_count * tile_count
    params = pltpu.CompilerParams(vmem_limit_bytes=VMEM)

    own = pl.pallas_call(
        functools.partial(run_kernel, cells_dev),
        out_shape=jax.ShapeDtypeStruct((band_count, tile_count, ROWS, count), jnp.bfloat16),
        in_specs=[whole()] * 4,
        out_specs=whole(),
        compiler_params=params,
        name="own_run",
    )(
        jnp.asarray(twiddle_rows(band_count)),
        raw_traces,
        bin_owner.reshape(1, length),
        bin_offset,
    )
    lists = lax.all_to_all(
        own.reshape(runs, ROWS, count), ("band", "tile"), split_axis=0, concat_axis=0, tiled=True
    )

    traces = GROUP * count
    scratch = [
        pltpu.VMEM((CH, NG, NG), jnp.bfloat16),
        pltpu.VMEM((traces + COPY, 128), jnp.float32),
        pltpu.VMEM((traces + LARGE, 128), jnp.float32),
        pltpu.VMEM((GROUP, count), jnp.float32),
        pltpu.VMEM((2 * GROUP + 8, 128), jnp.int32),
        pltpu.VMEM((4, 128, NG), jnp.float32),
        pltpu.VMEM(((CH + 1) * BLOCK, NG), jnp.float32),
        pltpu.VMEM((FB, 2, row_block, NG), jnp.float32),
        pltpu.SMEM((2 * GROUP + 8, 128), jnp.int32),
        pltpu.SemaphoreType.DMA,
        pltpu.SemaphoreType.DMA((FB,)),
    ]
    scratch += [pltpu.VMEM((LARGE + COPY, 128), jnp.float32)] * SIDE
    if runs != GROUP:
        scratch.append(pltpu.VMEM((CH + 1, NG, NG), jnp.float32))
    return pl.pallas_call(
        functools.partial(grid_kernel, 1.0 / math.sqrt(NG), row_block),
        out_shape=jax.ShapeDtypeStruct((FB, 2, row_block, NG), jnp.float32),
        in_specs=[whole()],
        out_specs=whole(pl.ANY),
        scratch_shapes=scratch,
        compiler_params=params,
        name="grid",
    )(lists)


def solution(mesh):
    return jax.shard_map(
        per_device,
        mesh=mesh,
        in_specs=(P("tile", "band", None), P("tile", None, None), P("tile", None)),
        out_specs=P("band", None, "tile", None),
        check_vma=False,
    )
```

```python
import functools
import math

import jax
import jax.numpy as jnp
import ml_dtypes
import numpy as np
from jax import lax
from jax.experimental import pallas as pl
from jax.experimental.pallas import tpu as pltpu
from jax.sharding import PartitionSpec as P

NG = 512
NT = 2048
FB = 10
CH = 2 * FB
ROWS = 24
BLOCK = 16
BLOCKS = NG // BLOCK
GROUP = 32
COPY = 32
WIDTHS = (256, 512, 640)
LARGE = WIDTHS[-1]
SIDE = 4
VMEM = 56 * 1024 * 1024


def twiddle_rows(band_count):
    time_index = np.arange(NT)[None, None, :]
    freq_index = np.arange(band_count * FB).reshape(band_count, FB, 1) + 1
    angle = (time_index * freq_index % NT) * (2.0 * math.pi / NT)
    norm = 1.0 / math.sqrt(NT)
    table = np.zeros((band_count, ROWS, NT), np.float64)
    table[:, :FB] = np.cos(angle) * norm
    table[:, FB:CH] = -np.sin(angle) * norm
    return table.reshape(band_count * ROWS, NT).astype(ml_dtypes.bfloat16)


def contract_last(left, right):
    return lax.dot_general(
        left, right, (((1,), (1,)), ((), ())), preferred_element_type=jnp.float32
    )


def run_kernel(cells_dev, twiddle_ref, traces_ref, owner_ref, offset_ref, out_ref):
    bands, tiles, _, count = out_ref.shape
    lanes = pl.ds(pl.multiple_of(lax.axis_index("band") * count, count), count)
    cell = owner_ref[:, lanes] * cells_dev + offset_ref[:, lanes]
    order = cell * count + lax.broadcasted_iota(jnp.int32, (1, count), 1)
    rank = jnp.zeros((1, count), jnp.int32)
    for first in range(0, count, 128):
        column = jnp.transpose(jnp.broadcast_to(order[:, first : first + 128], (128, 128)))
        column = jnp.concatenate([column] * (count // 128), axis=1)
        rank += jnp.sum((column < order).astype(jnp.int32), axis=0, keepdims=True)
    target = lax.broadcasted_iota(jnp.int32, (count, count), 0)
    permute = (target == rank).astype(jnp.float32).astype(jnp.bfloat16)
    source = cell // NG
    receiver = cell % NG
    row = lax.broadcasted_iota(jnp.int32, (bands * ROWS, count), 0) % ROWS
    digits = jnp.where(row == CH, source // BLOCK, 0)
    digits = jnp.where(row == CH + 1, source % BLOCK, digits)
    digits = jnp.where(row == CH + 2, receiver // 256, digits)
    digits = jnp.where(row == CH + 3, receiver % 256, digits)
    spectra = contract_last(twiddle_ref[...], traces_ref[0])
    packed = (spectra + digits.astype(jnp.float32)).astype(jnp.bfloat16)
    ordered = contract_last(packed, permute)
    for band in range(bands):
        part = ordered[band * ROWS : (band + 1) * ROWS].astype(jnp.bfloat16)
        for tile in range(tiles):
            out_ref[band, tile] = part


def make_table(first_run, lists_ref, keys, table, table_s, sem):
    length = lists_ref.shape[2]
    for r in range(GROUP):
        keys[r : r + 1, :] = lists_ref[first_run + r].astype(jnp.float32)[CH : CH + 1]
    block_of = keys[...]
    lane = lax.broadcasted_iota(jnp.int32, (GROUP, 128), 1)
    starts = jnp.zeros((GROUP, 128), jnp.float32)
    for b in range(1, BLOCKS + 1):
        below = jnp.sum((block_of < float(b)).astype(jnp.float32), axis=1, keepdims=True)
        starts = jnp.where(lane == b, below, starts)
    sizes = jnp.where(lane < BLOCKS, pltpu.roll(starts, 127, 1) - starts, 0.0)
    earlier = lax.broadcasted_iota(jnp.int32, (GROUP, GROUP), 0) > lax.broadcasted_iota(
        jnp.int32, (GROUP, GROUP), 1
    )
    targets = jnp.dot(
        earlier.astype(jnp.float32).astype(jnp.bfloat16),
        sizes.astype(jnp.bfloat16),
        preferred_element_type=jnp.float32,
    )
    run = lax.broadcasted_iota(jnp.int32, (GROUP, 128), 0)
    table[:GROUP, :] = starts.astype(jnp.int32) + run * length
    table[GROUP : 2 * GROUP, :] = targets.astype(jnp.int32)
    widest = jnp.max(sizes, axis=0, keepdims=True)
    total = jnp.sum(sizes, axis=0, keepdims=True)
    last = lax.broadcasted_iota(jnp.int32, (8, 128), 0)
    table[2 * GROUP :, :] = jnp.where(last == 0, widest, total).astype(jnp.int32)
    copy = pltpu.make_async_copy(table, table_s, sem)
    copy.start()
    return copy


def turn_runs(first_run, lists_ref, flat):
    length = lists_ref.shape[2]
    for r in range(GROUP):
        part = lists_ref[first_run + r].astype(jnp.float32)
        for first in range(0, length, 128):
            at = r * length + first
            flat[at : at + 128, :ROWS] = jnp.transpose(part[:, first : first + 128])


def product(first, size, width, packed):
    part = jnp.concatenate(
        [jnp.transpose(packed[pl.ds(first + k, 128), :])[:ROWS] for k in range(0, width, 128)],
        axis=1,
    )
    step = lax.broadcasted_iota(jnp.int32, (BLOCK, width), 0).astype(jnp.float32)
    step = step.astype(jnp.bfloat16)
    place = lax.broadcasted_iota(jnp.int32, (1, width), 1)
    one = jnp.ones((), jnp.bfloat16)
    none = jnp.zeros((), jnp.bfloat16)

    def spread(row):
        return jnp.broadcast_to(row, (BLOCK, width)).astype(jnp.bfloat16)

    hit = spread(jnp.where(place < size, part[CH + 1 : CH + 2], -1.0)) == step
    left = [jnp.where(hit, spread(part[c : c + 1]), none) for c in range(CH)]
    left.append(jnp.where(hit, one, none))
    right = []
    for half in range(NG // 256):
        low = spread(jnp.where(part[CH + 2 : CH + 3] == float(half), part[CH + 3 : CH + 4], -1.0))
        for j in range(0, 256, BLOCK):
            right.append(jnp.where(low == step + jnp.bfloat16(j), one, none))
    return contract_last(jnp.concatenate(left, axis=0), jnp.concatenate(right, axis=0))


def block_rows(b):
    return pl.ds(pl.multiple_of(b * BLOCK, BLOCK), BLOCK)


def add_blocks(table_s, flat, buffers, packed, total, emit):
    def fast(b, width):
        sums = []
        for q in range(SIDE):
            buffer = buffers[q]
            for r in range(GROUP):
                buffer[pl.ds(table_s[GROUP + r, b + q], COPY), :] = flat[
                    pl.ds(table_s[r, b + q], COPY), :
                ]
            sums.append(product(0, table_s[2 * GROUP + 1, b + q], width, buffer))
        for q in range(SIDE):
            emit(b + q, sums[q])

    def slow(b):
        def run(r, _):
            source = table_s[r, b]
            target = table_s[GROUP + r, b]
            after = table_s[2 * GROUP + 1, b]
            after = jnp.where(r + 1 < GROUP, table_s[jnp.minimum(GROUP + r + 1, 2 * GROUP - 1), b], after)

            def piece(k, _):
                packed[pl.ds(target + 8 * k, 8), :] = flat[pl.ds(source + 8 * k, 8), :]
                return 0

            return lax.fori_loop(0, (after - target + 7) // 8, piece, 0)

        lax.fori_loop(0, GROUP, run, 0)
        total[...] = jnp.zeros_like(total)
        size = table_s[2 * GROUP + 1, b]

        def piece(k, _):
            first = pl.multiple_of(k * LARGE, LARGE)
            total[...] += product(first, size - first, LARGE, packed)
            return 0

        lax.fori_loop(0, (size + LARGE - 1) // LARGE, piece, 0)
        emit(b, total[...])

    def side(i, _):
        b = i * SIDE
        widest = table_s[2 * GROUP, b]
        largest = table_s[2 * GROUP + 1, b]
        for q in range(1, SIDE):
            widest = jnp.maximum(widest, table_s[2 * GROUP, b + q])
            largest = jnp.maximum(largest, table_s[2 * GROUP + 1, b + q])
        plain = widest <= COPY

        least = -1
        for width in WIDTHS:

            @pl.when(plain & (largest > least) & (largest <= width))
            def _(width=width):
                fast(b, width)

            least = width

        @pl.when(jnp.logical_not(plain) | (largest > LARGE))
        def _():
            lax.fori_loop(0, SIDE, lambda q, _: (slow(b + q), 0)[1], 0)

        return 0

    lax.fori_loop(0, BLOCKS // SIDE, side, 0)


def grid_kernel(
    scale, row_block, lists_ref, out_ref, planes, flat, packed, keys, table, turned, total, result,
    table_s, sem, out_sems, *rest
):
    runs = lists_ref.shape[0]
    alone = runs == GROUP
    buffers = rest[:SIDE]
    grid = rest[SIDE] if not alone else None

    def finish(sums, inverse, rows):
        for c in range(CH):
            planes[c, rows, :] = (sums(c) * inverse).astype(jnp.bfloat16)

    def emit(b, sums):
        rows = block_rows(b)
        if alone:
            inverse = 1.0 / jnp.maximum(sums[CH * BLOCK :], 1.0)
            finish(lambda c: sums[c * BLOCK : (c + 1) * BLOCK], inverse, rows)
        else:
            for c in range(CH + 1):
                grid[c, rows, :] += sums[c * BLOCK : (c + 1) * BLOCK]

    def group(g, _):
        copy = make_table(g * GROUP, lists_ref, keys, table, table_s, sem)
        turn_runs(g * GROUP, lists_ref, flat)
        copy.wait()
        add_blocks(table_s, flat, buffers, packed, total, emit)
        return 0

    if alone:
        group(0, 0)
    else:
        grid[...] = jnp.zeros_like(grid)
        lax.fori_loop(0, runs // GROUP, group, 0)

        def divide(b, _):
            rows = block_rows(b)
            finish(lambda c: grid[c, rows, :], 1.0 / jnp.maximum(grid[CH, rows, :], 1.0), rows)
            return 0

        lax.fori_loop(0, BLOCKS, divide, 0)

    first_row = pl.multiple_of(lax.axis_index("tile") * row_block, row_block)
    first_col = pl.multiple_of(first_row // 128 * 128, 128)
    within = pl.multiple_of(first_row % 128, row_block)

    def own_rows(p, slot):
        turned[slot] = jnp.transpose(planes[p, :, pl.ds(first_col, 128)].astype(jnp.float32))
        across = turned[slot, pl.ds(within, row_block), :]
        along = planes[p, pl.ds(first_row, row_block), :].astype(jnp.float32)
        return (0.5 * (along + across)).astype(jnp.bfloat16)

    def sent(f):
        return pltpu.make_async_copy(result.at[f], out_ref.at[f], out_sems.at[f])

    def frequency(f, slot):
        own = jnp.concatenate([own_rows(f, slot), own_rows(FB + f, slot + 1)], axis=0)
        real = planes[f]
        imag = planes[FB + f]
        by_real = jnp.dot(own, real, preferred_element_type=jnp.float32) + contract_last(own, real)
        by_imag = jnp.dot(own, imag, preferred_element_type=jnp.float32) + contract_last(own, imag)
        half = 0.5 * scale
        result[f, 0] = (by_real[:row_block] - by_imag[row_block:]) * half
        result[f, 1] = (by_imag[:row_block] + by_real[row_block:]) * half
        sent(f).start()

    def pair(i, _):
        frequency(2 * i, 0)
        frequency(2 * i + 1, 2)
        return 0

    lax.fori_loop(0, FB // 2, pair, 0)
    for f in range(FB):
        sent(f).wait()


def whole(space=pltpu.VMEM):
    return pl.BlockSpec(memory_space=space)


def per_device(raw_traces, bin_owner, bin_offset):
    band_count = lax.axis_size("band")
    tile_count = lax.axis_size("tile")
    length = bin_offset.shape[1]
    count = raw_traces.shape[1]
    cells_dev = NG * NG // tile_count
    row_block = NG // tile_count
    runs = band_count * tile_count
    params = pltpu.CompilerParams(vmem_limit_bytes=VMEM)

    own = pl.pallas_call(
        functools.partial(run_kernel, cells_dev),
        out_shape=jax.ShapeDtypeStruct((band_count, tile_count, ROWS, count), jnp.bfloat16),
        in_specs=[whole()] * 4,
        out_specs=whole(),
        compiler_params=params,
        name="own_run",
    )(
        jnp.asarray(twiddle_rows(band_count)),
        raw_traces,
        bin_owner.reshape(1, length),
        bin_offset,
    )
    lists = lax.all_to_all(
        own.reshape(runs, ROWS, count), ("band", "tile"), split_axis=0, concat_axis=0, tiled=True
    )

    traces = GROUP * count
    scratch = [
        pltpu.VMEM((CH, NG, NG), jnp.bfloat16),
        pltpu.VMEM((traces + COPY, 128), jnp.float32),
        pltpu.VMEM((traces + LARGE, 128), jnp.float32),
        pltpu.VMEM((GROUP, count), jnp.float32),
        pltpu.VMEM((2 * GROUP + 8, 128), jnp.int32),
        pltpu.VMEM((4, 128, NG), jnp.float32),
        pltpu.VMEM(((CH + 1) * BLOCK, NG), jnp.float32),
        pltpu.VMEM((FB, 2, row_block, NG), jnp.float32),
        pltpu.SMEM((2 * GROUP + 8, 128), jnp.int32),
        pltpu.SemaphoreType.DMA,
        pltpu.SemaphoreType.DMA((FB,)),
    ]
    scratch += [pltpu.VMEM((LARGE + COPY, 128), jnp.float32)] * SIDE
    if runs != GROUP:
        scratch.append(pltpu.VMEM((CH + 1, NG, NG), jnp.float32))
    return pl.pallas_call(
        functools.partial(grid_kernel, 1.0 / math.sqrt(NG), row_block),
        out_shape=jax.ShapeDtypeStruct((FB, 2, row_block, NG), jnp.float32),
        in_specs=[whole()],
        out_specs=whole(pl.ANY),
        scratch_shapes=scratch,
        compiler_params=params,
        name="grid",
    )(lists)


def solution(mesh):
    return jax.shard_map(
        per_device,
        mesh=mesh,
        in_specs=(P("tile", "band", None), P("tile", None, None), P("tile", None)),
        out_specs=P("band", None, "tile", None),
        check_vma=False,
    )
```

```python
import functools
import math

import jax
import jax.numpy as jnp
import ml_dtypes
import numpy as np
from jax import lax
from jax.experimental import pallas as pl
from jax.experimental.pallas import tpu as pltpu
from jax.sharding import PartitionSpec as P

NG = 512
NT = 2048
FB = 10
CH = 2 * FB
ROWS = 24
BLOCK = 16
BLOCKS = NG // BLOCK
GROUP = 32
FORMS = ((16, 256), (32, 512), (32, 640))
COPY, LARGE = FORMS[-1]
SIDE = 4
HALF = 256
VMEM = 56 * 1024 * 1024


def twiddle_rows(band_count):
    time_index = np.arange(NT)[None, None, :]
    freq_index = np.arange(band_count * FB).reshape(band_count, FB, 1) + 1
    angle = (time_index * freq_index % NT) * (2.0 * math.pi / NT)
    norm = 1.0 / math.sqrt(NT)
    table = np.zeros((band_count, ROWS, NT), np.float64)
    table[:, :FB] = np.cos(angle) * norm
    table[:, FB:CH] = -np.sin(angle) * norm
    return table.reshape(band_count * ROWS, NT).astype(ml_dtypes.bfloat16)


def contract_last(left, right):
    return lax.dot_general(
        left, right, (((1,), (1,)), ((), ())), preferred_element_type=jnp.float32
    )


def run_kernel(cells_dev, twiddle_ref, traces_ref, owner_ref, offset_ref, out_ref):
    bands, tiles, _, count = out_ref.shape
    lanes = pl.ds(pl.multiple_of(lax.axis_index("band") * count, count), count)
    cell = owner_ref[:, lanes] * cells_dev + offset_ref[:, lanes]
    order = cell * count + lax.broadcasted_iota(jnp.int32, (1, count), 1)
    rank = jnp.zeros((1, count), jnp.int32)
    starts = jnp.zeros((1, count), jnp.int32)
    limit = lax.broadcasted_iota(jnp.int32, (1, count), 1) * (BLOCK * NG * count)
    limit = jnp.minimum(limit, NG * NG * count)
    for first in range(0, count, 128):
        column = jnp.transpose(jnp.broadcast_to(order[:, first : first + 128], (128, 128)))
        column = jnp.concatenate([column] * (count // 128), axis=1)
        rank += jnp.sum((column < order).astype(jnp.int32), axis=0, keepdims=True)
        starts += jnp.sum((column < limit).astype(jnp.int32), axis=0, keepdims=True)
    target = lax.broadcasted_iota(jnp.int32, (count, count), 0)
    permute = (target == rank).astype(jnp.float32).astype(jnp.bfloat16)
    source = cell // NG
    receiver = cell % NG
    row = lax.broadcasted_iota(jnp.int32, (bands * ROWS, count), 0) % ROWS
    digits = jnp.where(row == CH + 1, source % BLOCK, 0)
    digits = jnp.where(row == CH + 2, receiver // HALF, digits)
    digits = jnp.where(row == CH + 3, receiver % HALF, digits)
    spectra = contract_last(twiddle_ref[...], traces_ref[0])
    packed = (spectra + digits.astype(jnp.float32)).astype(jnp.bfloat16)
    ordered = contract_last(packed, permute) + jnp.where(row == CH, starts, 0).astype(jnp.float32)
    for band in range(bands):
        part = ordered[band * ROWS : (band + 1) * ROWS].astype(jnp.bfloat16)
        for tile in range(tiles):
            out_ref[band, tile] = part


def make_table(first_run, lists_ref, keys, table, table_s, sem):
    length = lists_ref.shape[2]
    for r in range(GROUP):
        part = lists_ref[first_run + r].astype(jnp.float32)
        keys[r : r + 1, :] = part[CH : CH + 1, :128]
    starts = keys[...]
    lane = lax.broadcasted_iota(jnp.int32, (GROUP, 128), 1)
    sizes = jnp.where(lane < BLOCKS, pltpu.roll(starts, 127, 1) - starts, 0.0)
    earlier = lax.broadcasted_iota(jnp.int32, (GROUP, GROUP), 0) > lax.broadcasted_iota(
        jnp.int32, (GROUP, GROUP), 1
    )
    targets = jnp.dot(
        earlier.astype(jnp.float32).astype(jnp.bfloat16),
        sizes.astype(jnp.bfloat16),
        preferred_element_type=jnp.float32,
    )
    run = lax.broadcasted_iota(jnp.int32, (GROUP, 128), 0)
    table[:GROUP, :] = starts.astype(jnp.int32) + run * length
    table[GROUP : 2 * GROUP, :] = targets.astype(jnp.int32)
    widest = jnp.max(sizes, axis=0, keepdims=True)
    total = jnp.sum(sizes, axis=0, keepdims=True)
    last = lax.broadcasted_iota(jnp.int32, (8, 128), 0)
    table[2 * GROUP :, :] = jnp.where(last == 0, widest, total).astype(jnp.int32)
    copy = pltpu.make_async_copy(table, table_s, sem)
    copy.start()
    return copy


def turn_runs(first_run, lists_ref, flat):
    length = lists_ref.shape[2]
    for r in range(GROUP):
        part = lists_ref[first_run + r].astype(jnp.float32)
        for first in range(0, length, 128):
            at = r * length + first
            flat[at : at + 128, :ROWS] = jnp.transpose(part[:, first : first + 128])


def products(first, size, width, packed):
    part = jnp.concatenate(
        [jnp.transpose(packed[pl.ds(first + k, 128), :])[:ROWS] for k in range(0, width, 128)],
        axis=1,
    )
    step = lax.broadcasted_iota(jnp.int32, (BLOCK, width), 0).astype(jnp.float32)
    step = step.astype(jnp.bfloat16)
    place = lax.broadcasted_iota(jnp.int32, (1, width), 1)
    one = jnp.ones((), jnp.bfloat16)
    none = jnp.zeros((), jnp.bfloat16)

    def spread(row):
        return jnp.broadcast_to(row, (BLOCK, width)).astype(jnp.bfloat16)

    hit = spread(jnp.where(place < size, part[CH + 1 : CH + 2], -1.0)) == step
    left = [jnp.where(hit, one, none)]
    left += [jnp.where(hit, spread(part[c : c + 1]), none) for c in range(CH)]
    left = jnp.concatenate(left, axis=0)
    for half in range(NG // HALF):
        low = spread(jnp.where(part[CH + 2 : CH + 3] == float(half), part[CH + 3 : CH + 4], -1.0))
        right = [
            jnp.where(low == step + jnp.bfloat16(j), one, none) for j in range(0, HALF, BLOCK)
        ]
        yield pl.ds(half * HALF, HALF), contract_last(left, jnp.concatenate(right, axis=0))


def block_rows(b):
    return pl.ds(pl.multiple_of(b * BLOCK, BLOCK), BLOCK)


def add_blocks(table_s, flat, buffers, packed, total, emit):
    def fast(b, rows, width):
        def copies(q):
            for r in range(GROUP):
                buffers[q][pl.ds(table_s[GROUP + r, b + q], rows), :] = flat[
                    pl.ds(table_s[r, b + q], rows), :
                ]

        copies(0)
        for q in range(SIDE):
            if q + 1 < SIDE:
                copies(q + 1)
            for lanes, sums in products(0, table_s[2 * GROUP + 1, b + q], width, buffers[q]):
                emit(b + q, lanes, sums)

    def slow(b):
        def run(r, _):
            source = table_s[r, b]
            target = table_s[GROUP + r, b]
            after = table_s[2 * GROUP + 1, b]
            after = jnp.where(r + 1 < GROUP, table_s[jnp.minimum(GROUP + r + 1, 2 * GROUP - 1), b], after)

            def piece(k, _):
                packed[pl.ds(target + 8 * k, 8), :] = flat[pl.ds(source + 8 * k, 8), :]
                return 0

            return lax.fori_loop(0, (after - target + 7) // 8, piece, 0)

        lax.fori_loop(0, GROUP, run, 0)
        total[...] = jnp.zeros_like(total)
        size = table_s[2 * GROUP + 1, b]

        def piece(k, _):
            first = pl.multiple_of(k * LARGE, LARGE)
            for lanes, sums in products(first, size - first, LARGE, packed):
                total[:, lanes] += sums
            return 0

        lax.fori_loop(0, (size + LARGE - 1) // LARGE, piece, 0)
        for half in range(NG // HALF):
            lanes = pl.ds(half * HALF, HALF)
            emit(b, lanes, total[:, lanes])

    def side(i, _):
        b = i * SIDE
        widest = table_s[2 * GROUP, b]
        largest = table_s[2 * GROUP + 1, b]
        for q in range(1, SIDE):
            widest = jnp.maximum(widest, table_s[2 * GROUP, b + q])
            largest = jnp.maximum(largest, table_s[2 * GROUP + 1, b + q])
        left_over = jnp.bool_(True)
        for rows, width in FORMS:
            fits = (widest <= rows) & (largest <= width)

            @pl.when(left_over & fits)
            def _(rows=rows, width=width):
                fast(b, rows, width)

            left_over = left_over & jnp.logical_not(fits)

        @pl.when(left_over)
        def _():
            lax.fori_loop(0, SIDE, lambda q, _: (slow(b + q), 0)[1], 0)

        return 0

    lax.fori_loop(0, BLOCKS // SIDE, side, 0)


def grid_kernel(
    scale, row_block, lists_ref, out_ref, planes, flat, packed, keys, table, turned, total, result,
    table_s, sem, out_sems, *rest
):
    runs = lists_ref.shape[0]
    alone = runs == GROUP
    buffers = rest[:SIDE]
    grid = rest[SIDE] if not alone else None

    def finish(sums, rows, lanes):
        inverse = 1.0 / jnp.maximum(sums(0), 1.0)
        for c in range(CH):
            planes[c, rows, lanes] = (sums(c + 1) * inverse).astype(jnp.bfloat16)

    def emit(b, lanes, sums):
        rows = block_rows(b)
        if alone:
            finish(lambda c: sums[c * BLOCK : (c + 1) * BLOCK], rows, lanes)
        else:
            for c in range(CH + 1):
                grid[c, rows, lanes] += sums[c * BLOCK : (c + 1) * BLOCK]

    def group(g, _):
        copy = make_table(g * GROUP, lists_ref, keys, table, table_s, sem)
        turn_runs(g * GROUP, lists_ref, flat)
        copy.wait()
        add_blocks(table_s, flat, buffers, packed, total, emit)
        return 0

    if alone:
        group(0, 0)
    else:
        grid[...] = jnp.zeros_like(grid)
        lax.fori_loop(0, runs // GROUP, group, 0)

        def divide(b, _):
            rows = block_rows(b)
            finish(lambda c: grid[c, rows, :], rows, pl.ds(0, NG))
            return 0

        lax.fori_loop(0, BLOCKS, divide, 0)

    first_row = pl.multiple_of(lax.axis_index("tile") * row_block, row_block)
    first_col = pl.multiple_of(first_row // 128 * 128, 128)
    within = pl.multiple_of(first_row % 128, row_block)

    def own_rows(p, slot):
        turned[slot] = jnp.transpose(planes[p, :, pl.ds(first_col, 128)].astype(jnp.float32))
        across = turned[slot, pl.ds(within, row_block), :]
        along = planes[p, pl.ds(first_row, row_block), :].astype(jnp.float32)
        return (0.5 * (along + across)).astype(jnp.bfloat16)

    def sent(f):
        return pltpu.make_async_copy(result.at[f], out_ref.at[f], out_sems.at[f])

    def frequency(f, slot):
        own = jnp.concatenate([own_rows(f, slot), own_rows(FB + f, slot + 1)], axis=0)
        real = planes[f]
        imag = planes[FB + f]
        by_real = jnp.dot(own, real, preferred_element_type=jnp.float32) + contract_last(own, real)
        by_imag = jnp.dot(own, imag, preferred_element_type=jnp.float32) + contract_last(own, imag)
        half = 0.5 * scale
        result[f, 0] = (by_real[:row_block] - by_imag[row_block:]) * half
        result[f, 1] = (by_imag[:row_block] + by_real[row_block:]) * half
        sent(f).start()

    def pair(i, _):
        frequency(2 * i, 0)
        frequency(2 * i + 1, 2)
        return 0

    lax.fori_loop(0, FB // 2, pair, 0)
    for f in range(FB):
        sent(f).wait()


def whole(space=pltpu.VMEM):
    return pl.BlockSpec(memory_space=space)


def per_device(raw_traces, bin_owner, bin_offset):
    band_count = lax.axis_size("band")
    tile_count = lax.axis_size("tile")
    length = bin_offset.shape[1]
    count = raw_traces.shape[1]
    cells_dev = NG * NG // tile_count
    row_block = NG // tile_count
    runs = band_count * tile_count
    params = pltpu.CompilerParams(vmem_limit_bytes=VMEM)

    own = pl.pallas_call(
        functools.partial(run_kernel, cells_dev),
        out_shape=jax.ShapeDtypeStruct((band_count, tile_count, ROWS, count), jnp.bfloat16),
        in_specs=[whole()] * 4,
        out_specs=whole(),
        compiler_params=params,
        name="own_run",
    )(
        jnp.asarray(twiddle_rows(band_count)),
        raw_traces,
        bin_owner.reshape(1, length),
        bin_offset,
    )
    lists = lax.all_to_all(
        own.reshape(runs, ROWS, count), ("band", "tile"), split_axis=0, concat_axis=0, tiled=True
    )

    traces = GROUP * count
    scratch = [
        pltpu.VMEM((CH, NG, NG), jnp.bfloat16),
        pltpu.VMEM((traces + COPY, 128), jnp.float32),
        pltpu.VMEM((traces + LARGE, 128), jnp.float32),
        pltpu.VMEM((GROUP, 128), jnp.float32),
        pltpu.VMEM((2 * GROUP + 8, 128), jnp.int32),
        pltpu.VMEM((4, 128, NG), jnp.float32),
        pltpu.VMEM(((CH + 1) * BLOCK, NG), jnp.float32),
        pltpu.VMEM((FB, 2, row_block, NG), jnp.float32),
        pltpu.SMEM((2 * GROUP + 8, 128), jnp.int32),
        pltpu.SemaphoreType.DMA,
        pltpu.SemaphoreType.DMA((FB,)),
    ]
    scratch += [pltpu.VMEM((LARGE + COPY, 128), jnp.float32)] * SIDE
    if runs != GROUP:
        scratch.append(pltpu.VMEM((CH + 1, NG, NG), jnp.float32))
    return pl.pallas_call(
        functools.partial(grid_kernel, 1.0 / math.sqrt(NG), row_block),
        out_shape=jax.ShapeDtypeStruct((FB, 2, row_block, NG), jnp.float32),
        in_specs=[whole()],
        out_specs=whole(pl.ANY),
        scratch_shapes=scratch,
        compiler_params=params,
        name="grid",
    )(lists)


def solution(mesh):
    return jax.shard_map(
        per_device,
        mesh=mesh,
        in_specs=(P("tile", "band", None), P("tile", None, None), P("tile", None)),
        out_specs=P("band", None, "tile", None),
        check_vma=False,
    )
```

```python
import functools
import math

import jax
import jax.numpy as jnp
import ml_dtypes
import numpy as np
from jax import lax
from jax.experimental import pallas as pl
from jax.experimental.pallas import tpu as pltpu
from jax.sharding import PartitionSpec as P

NG = 512
NT = 2048
FB = 10
CH = 2 * FB
ROWS = 24
BLOCK = 16
BLOCKS = NG // BLOCK
GROUP = 32
FORMS = ((16, 256), (32, 512), (32, 640))
COPY, LARGE = FORMS[-1]
SIDE = 2
HALF = 256
VMEM = 56 * 1024 * 1024


def twiddle_rows(band_count):
    time_index = np.arange(NT)[None, None, :]
    freq_index = np.arange(band_count * FB).reshape(band_count, FB, 1) + 1
    angle = (time_index * freq_index % NT) * (2.0 * math.pi / NT)
    norm = 1.0 / math.sqrt(NT)
    table = np.zeros((band_count, ROWS, NT), np.float64)
    table[:, :FB] = np.cos(angle) * norm
    table[:, FB:CH] = -np.sin(angle) * norm
    return table.reshape(band_count * ROWS, NT).astype(ml_dtypes.bfloat16)


def contract_last(left, right):
    return lax.dot_general(
        left, right, (((1,), (1,)), ((), ())), preferred_element_type=jnp.float32
    )


def run_kernel(cells_dev, twiddle_ref, traces_ref, owner_ref, offset_ref, out_ref):
    bands, tiles, _, count = out_ref.shape
    lanes = pl.ds(pl.multiple_of(lax.axis_index("band") * count, count), count)
    cell = owner_ref[:, lanes] * cells_dev + offset_ref[:, lanes]
    order = cell * count + lax.broadcasted_iota(jnp.int32, (1, count), 1)
    rank = jnp.zeros((1, count), jnp.int32)
    starts = jnp.zeros((1, count), jnp.int32)
    limit = lax.broadcasted_iota(jnp.int32, (1, count), 1) * (BLOCK * NG * count)
    limit = jnp.minimum(limit, NG * NG * count)
    for first in range(0, count, 128):
        column = jnp.transpose(jnp.broadcast_to(order[:, first : first + 128], (128, 128)))
        column = jnp.concatenate([column] * (count // 128), axis=1)
        rank += jnp.sum((column < order).astype(jnp.int32), axis=0, keepdims=True)
        starts += jnp.sum((column < limit).astype(jnp.int32), axis=0, keepdims=True)
    target = lax.broadcasted_iota(jnp.int32, (count, count), 0)
    permute = (target == rank).astype(jnp.float32).astype(jnp.bfloat16)
    source = cell // NG
    receiver = cell % NG
    row = lax.broadcasted_iota(jnp.int32, (bands * ROWS, count), 0) % ROWS
    digits = jnp.where(row == CH + 1, source % BLOCK, 0)
    digits = jnp.where(row == CH + 2, receiver // HALF, digits)
    digits = jnp.where(row == CH + 3, receiver % HALF, digits)
    spectra = contract_last(twiddle_ref[...], traces_ref[0])
    packed = (spectra + digits.astype(jnp.float32)).astype(jnp.bfloat16)
    ordered = contract_last(packed, permute) + jnp.where(row == CH, starts, 0).astype(jnp.float32)
    for band in range(bands):
        part = ordered[band * ROWS : (band + 1) * ROWS].astype(jnp.bfloat16)
        for tile in range(tiles):
            out_ref[band, tile] = part


def make_table(first_run, lists_ref, keys, table, table_s, sem):
    length = lists_ref.shape[2]
    for r in range(GROUP):
        part = lists_ref[first_run + r].astype(jnp.float32)
        keys[r : r + 1, :] = part[CH : CH + 1, :128]
    starts = keys[...]
    lane = lax.broadcasted_iota(jnp.int32, (GROUP, 128), 1)
    sizes = jnp.where(lane < BLOCKS, pltpu.roll(starts, 127, 1) - starts, 0.0)
    earlier = lax.broadcasted_iota(jnp.int32, (GROUP, GROUP), 0) > lax.broadcasted_iota(
        jnp.int32, (GROUP, GROUP), 1
    )
    targets = jnp.dot(
        earlier.astype(jnp.float32).astype(jnp.bfloat16),
        sizes.astype(jnp.bfloat16),
        preferred_element_type=jnp.float32,
    )
    run = lax.broadcasted_iota(jnp.int32, (GROUP, 128), 0)
    table[:GROUP, :] = starts.astype(jnp.int32) + run * length
    table[GROUP : 2 * GROUP, :] = targets.astype(jnp.int32)
    widest = jnp.max(sizes, axis=0, keepdims=True)
    total = jnp.sum(sizes, axis=0, keepdims=True)
    last = lax.broadcasted_iota(jnp.int32, (8, 128), 0)
    table[2 * GROUP :, :] = jnp.where(last == 0, widest, total).astype(jnp.int32)
    copy = pltpu.make_async_copy(table, table_s, sem)
    copy.start()
    return copy


def turn_runs(first_run, lists_ref, flat):
    length = lists_ref.shape[2]
    for r in range(GROUP):
        part = lists_ref[first_run + r].astype(jnp.float32)
        for first in range(0, length, 128):
            at = r * length + first
            flat[at : at + 128, :ROWS] = jnp.transpose(part[:, first : first + 128])


def products(first, size, width, packed):
    part = jnp.concatenate(
        [jnp.transpose(packed[pl.ds(first + k, 128), :])[:ROWS] for k in range(0, width, 128)],
        axis=1,
    )
    step = lax.broadcasted_iota(jnp.int32, (BLOCK, width), 0).astype(jnp.float32)
    step = step.astype(jnp.bfloat16)
    place = lax.broadcasted_iota(jnp.int32, (1, width), 1)
    one = jnp.ones((), jnp.bfloat16)
    none = jnp.zeros((), jnp.bfloat16)

    def spread(row):
        return jnp.broadcast_to(row, (BLOCK, width)).astype(jnp.bfloat16)

    hit = spread(jnp.where(place < size, part[CH + 1 : CH + 2], -1.0)) == step
    left = [jnp.where(hit, one, none)]
    left += [jnp.where(hit, spread(part[c : c + 1]), none) for c in range(CH)]
    left = jnp.concatenate(left, axis=0)
    for half in range(NG // HALF):
        low = spread(jnp.where(part[CH + 2 : CH + 3] == float(half), part[CH + 3 : CH + 4], -1.0))
        right = [
            jnp.where(low == step + jnp.bfloat16(j), one, none) for j in range(0, HALF, BLOCK)
        ]
        yield pl.ds(half * HALF, HALF), contract_last(left, jnp.concatenate(right, axis=0))


def block_rows(b):
    return pl.ds(pl.multiple_of(b * BLOCK, BLOCK), BLOCK)


def add_blocks(table_s, flat, buffers, packed, total, emit):
    def fast(b, rows, width):
        def copies(q):
            for r in range(GROUP):
                buffers[q][pl.ds(table_s[GROUP + r, b + q], rows), :] = flat[
                    pl.ds(table_s[r, b + q], rows), :
                ]

        copies(0)
        for q in range(SIDE):
            if q + 1 < SIDE:
                copies(q + 1)
            for lanes, sums in products(0, table_s[2 * GROUP + 1, b + q], width, buffers[q]):
                emit(b + q, lanes, sums)

    def slow(b):
        def run(r, _):
            source = table_s[r, b]
            target = table_s[GROUP + r, b]
            after = table_s[2 * GROUP + 1, b]
            after = jnp.where(r + 1 < GROUP, table_s[jnp.minimum(GROUP + r + 1, 2 * GROUP - 1), b], after)

            def piece(k, _):
                packed[pl.ds(target + 8 * k, 8), :] = flat[pl.ds(source + 8 * k, 8), :]
                return 0

            return lax.fori_loop(0, (after - target + 7) // 8, piece, 0)

        lax.fori_loop(0, GROUP, run, 0)
        total[...] = jnp.zeros_like(total)
        size = table_s[2 * GROUP + 1, b]

        def piece(k, _):
            first = pl.multiple_of(k * LARGE, LARGE)
            for lanes, sums in products(first, size - first, LARGE, packed):
                total[:, lanes] += sums
            return 0

        lax.fori_loop(0, (size + LARGE - 1) // LARGE, piece, 0)
        for half in range(NG // HALF):
            lanes = pl.ds(half * HALF, HALF)
            emit(b, lanes, total[:, lanes])

    def side(i, _):
        b = i * SIDE
        widest = table_s[2 * GROUP, b]
        largest = table_s[2 * GROUP + 1, b]
        for q in range(1, SIDE):
            widest = jnp.maximum(widest, table_s[2 * GROUP, b + q])
            largest = jnp.maximum(largest, table_s[2 * GROUP + 1, b + q])
        left_over = jnp.bool_(True)
        for rows, width in FORMS:
            fits = (widest <= rows) & (largest <= width)

            @pl.when(left_over & fits)
            def _(rows=rows, width=width):
                fast(b, rows, width)

            left_over = left_over & jnp.logical_not(fits)

        @pl.when(left_over)
        def _():
            lax.fori_loop(0, SIDE, lambda q, _: (slow(b + q), 0)[1], 0)

        return 0

    lax.fori_loop(0, BLOCKS // SIDE, side, 0)


def grid_kernel(
    scale, row_block, lists_ref, out_ref, planes, flat, packed, keys, table, turned, total, result,
    table_s, sem, out_sems, *rest
):
    runs = lists_ref.shape[0]
    alone = runs == GROUP
    buffers = rest[:SIDE]
    grid = rest[SIDE] if not alone else None

    def finish(sums, rows, lanes):
        inverse = 1.0 / jnp.maximum(sums(0), 1.0)
        for c in range(CH):
            planes[c, rows, lanes] = (sums(c + 1) * inverse).astype(jnp.bfloat16)

    def emit(b, lanes, sums):
        rows = block_rows(b)
        if alone:
            finish(lambda c: sums[c * BLOCK : (c + 1) * BLOCK], rows, lanes)
        else:
            for c in range(CH + 1):
                grid[c, rows, lanes] += sums[c * BLOCK : (c + 1) * BLOCK]

    def group(g, _):
        copy = make_table(g * GROUP, lists_ref, keys, table, table_s, sem)
        turn_runs(g * GROUP, lists_ref, flat)
        copy.wait()
        add_blocks(table_s, flat, buffers, packed, total, emit)
        return 0

    if alone:
        group(0, 0)
    else:
        grid[...] = jnp.zeros_like(grid)
        lax.fori_loop(0, runs // GROUP, group, 0)

        def divide(b, _):
            rows = block_rows(b)
            finish(lambda c: grid[c, rows, :], rows, pl.ds(0, NG))
            return 0

        lax.fori_loop(0, BLOCKS, divide, 0)

    first_row = pl.multiple_of(lax.axis_index("tile") * row_block, row_block)
    first_col = pl.multiple_of(first_row // 128 * 128, 128)
    within = pl.multiple_of(first_row % 128, row_block)

    def own_rows(p, slot):
        turned[slot] = jnp.transpose(planes[p, :, pl.ds(first_col, 128)].astype(jnp.float32))
        across = turned[slot, pl.ds(within, row_block), :]
        along = planes[p, pl.ds(first_row, row_block), :].astype(jnp.float32)
        return (0.5 * (along + across)).astype(jnp.bfloat16)

    def sent(f):
        return pltpu.make_async_copy(result.at[f], out_ref.at[f], out_sems.at[f])

    def frequency(f, slot):
        own = jnp.concatenate([own_rows(f, slot), own_rows(FB + f, slot + 1)], axis=0)
        real = planes[f]
        imag = planes[FB + f]
        by_real = jnp.dot(own, real, preferred_element_type=jnp.float32) + contract_last(own, real)
        by_imag = jnp.dot(own, imag, preferred_element_type=jnp.float32) + contract_last(own, imag)
        half = 0.5 * scale
        result[f, 0] = (by_real[:row_block] - by_imag[row_block:]) * half
        result[f, 1] = (by_imag[:row_block] + by_real[row_block:]) * half
        sent(f).start()

    def pair(i, _):
        frequency(2 * i, 0)
        frequency(2 * i + 1, 2)
        return 0

    lax.fori_loop(0, FB // 2, pair, 0)
    for f in range(FB):
        sent(f).wait()


def whole(space=pltpu.VMEM):
    return pl.BlockSpec(memory_space=space)


def per_device(raw_traces, bin_owner, bin_offset):
    band_count = lax.axis_size("band")
    tile_count = lax.axis_size("tile")
    length = bin_offset.shape[1]
    count = raw_traces.shape[1]
    cells_dev = NG * NG // tile_count
    row_block = NG // tile_count
    runs = band_count * tile_count
    params = pltpu.CompilerParams(vmem_limit_bytes=VMEM)

    own = pl.pallas_call(
        functools.partial(run_kernel, cells_dev),
        out_shape=jax.ShapeDtypeStruct((band_count, tile_count, ROWS, count), jnp.bfloat16),
        in_specs=[whole()] * 4,
        out_specs=whole(),
        compiler_params=params,
        name="own_run",
    )(
        jnp.asarray(twiddle_rows(band_count)),
        raw_traces,
        bin_owner.reshape(1, length),
        bin_offset,
    )
    lists = lax.all_to_all(
        own.reshape(runs, ROWS, count), ("band", "tile"), split_axis=0, concat_axis=0, tiled=True
    )

    traces = GROUP * count
    scratch = [
        pltpu.VMEM((CH, NG, NG), jnp.bfloat16),
        pltpu.VMEM((traces + COPY, 128), jnp.float32),
        pltpu.VMEM((traces + LARGE, 128), jnp.float32),
        pltpu.VMEM((GROUP, 128), jnp.float32),
        pltpu.VMEM((2 * GROUP + 8, 128), jnp.int32),
        pltpu.VMEM((4, 128, NG), jnp.float32),
        pltpu.VMEM(((CH + 1) * BLOCK, NG), jnp.float32),
        pltpu.VMEM((FB, 2, row_block, NG), jnp.float32),
        pltpu.SMEM((2 * GROUP + 8, 128), jnp.int32),
        pltpu.SemaphoreType.DMA,
        pltpu.SemaphoreType.DMA((FB,)),
    ]
    scratch += [pltpu.VMEM((LARGE + COPY, 128), jnp.float32)] * SIDE
    if runs != GROUP:
        scratch.append(pltpu.VMEM((CH + 1, NG, NG), jnp.float32))
    return pl.pallas_call(
        functools.partial(grid_kernel, 1.0 / math.sqrt(NG), row_block),
        out_shape=jax.ShapeDtypeStruct((FB, 2, row_block, NG), jnp.float32),
        in_specs=[whole()],
        out_specs=whole(pl.ANY),
        scratch_shapes=scratch,
        compiler_params=params,
        name="grid",
    )(lists)


def solution(mesh):
    return jax.shard_map(
        per_device,
        mesh=mesh,
        in_specs=(P("tile", "band", None), P("tile", None, None), P("tile", None)),
        out_specs=P("band", None, "tile", None),
        check_vma=False,
    )
```

```python
import functools
import math

import jax
import jax.numpy as jnp
import ml_dtypes
import numpy as np
from jax import lax
from jax.experimental import pallas as pl
from jax.experimental.pallas import tpu as pltpu
from jax.sharding import PartitionSpec as P

NG = 512
NT = 2048
FB = 10
CH = 2 * FB
ROWS = 24
BLOCK = 16
BLOCKS = NG // BLOCK
GROUP = 32
FORMS = ((16, 256), (32, 512), (32, 640))
COPY, LARGE = FORMS[-1]
BESIDE = 5
SIDE = 4
HALF = 256
VMEM = 56 * 1024 * 1024


def twiddle_rows(band_count):
    time_index = np.arange(NT)[None, None, :]
    freq_index = np.arange(band_count * FB).reshape(band_count, FB, 1) + 1
    angle = (time_index * freq_index % NT) * (2.0 * math.pi / NT)
    norm = 1.0 / math.sqrt(NT)
    table = np.zeros((band_count, ROWS, NT), np.float64)
    table[:, :FB] = np.cos(angle) * norm
    table[:, FB:CH] = -np.sin(angle) * norm
    return table.reshape(band_count * ROWS, NT).astype(ml_dtypes.bfloat16)


def contract_last(left, right):
    return lax.dot_general(
        left, right, (((1,), (1,)), ((), ())), preferred_element_type=jnp.float32
    )


def run_kernel(cells_dev, twiddle_ref, traces_ref, owner_ref, offset_ref, out_ref):
    bands, tiles, _, count = out_ref.shape
    lanes = pl.ds(pl.multiple_of(lax.axis_index("band") * count, count), count)
    cell = owner_ref[:, lanes] * cells_dev + offset_ref[:, lanes]
    order = cell * count + lax.broadcasted_iota(jnp.int32, (1, count), 1)
    rank = jnp.zeros((1, count), jnp.int32)
    starts = jnp.zeros((1, count), jnp.int32)
    limit = lax.broadcasted_iota(jnp.int32, (1, count), 1) * (BLOCK * NG * count)
    limit = jnp.minimum(limit, NG * NG * count)
    for first in range(0, count, 128):
        column = jnp.transpose(jnp.broadcast_to(order[:, first : first + 128], (128, 128)))
        column = jnp.concatenate([column] * (count // 128), axis=1)
        rank += jnp.sum((column < order).astype(jnp.int32), axis=0, keepdims=True)
        starts += jnp.sum((column < limit).astype(jnp.int32), axis=0, keepdims=True)
    target = lax.broadcasted_iota(jnp.int32, (count, count), 0)
    permute = (target == rank).astype(jnp.float32).astype(jnp.bfloat16)
    source = cell // NG
    receiver = cell % NG
    row = lax.broadcasted_iota(jnp.int32, (bands * ROWS, count), 0) % ROWS
    digits = jnp.where(row == CH + 1, source % BLOCK, 0)
    digits = jnp.where(row == CH + 2, receiver // HALF, digits)
    digits = jnp.where(row == CH + 3, receiver % HALF, digits)
    spectra = contract_last(twiddle_ref[...], traces_ref[0])
    packed = (spectra + digits.astype(jnp.float32)).astype(jnp.bfloat16)
    ordered = contract_last(packed, permute) + jnp.where(row == CH, starts, 0).astype(jnp.float32)
    for band in range(bands):
        part = ordered[band * ROWS : (band + 1) * ROWS].astype(jnp.bfloat16)
        for tile in range(tiles):
            out_ref[band, tile] = part


def make_table(first_run, lists_ref, keys, table, table_s, sem):
    length = lists_ref.shape[2]
    for r in range(GROUP):
        part = lists_ref[first_run + r].astype(jnp.float32)
        keys[r : r + 1, :] = part[CH : CH + 1, :128]
    starts = keys[...]
    lane = lax.broadcasted_iota(jnp.int32, (GROUP, 128), 1)
    sizes = jnp.where(lane < BLOCKS, pltpu.roll(starts, 127, 1) - starts, 0.0)
    earlier = lax.broadcasted_iota(jnp.int32, (GROUP, GROUP), 0) > lax.broadcasted_iota(
        jnp.int32, (GROUP, GROUP), 1
    )
    targets = jnp.dot(
        earlier.astype(jnp.float32).astype(jnp.bfloat16),
        sizes.astype(jnp.bfloat16),
        preferred_element_type=jnp.float32,
    )
    run = lax.broadcasted_iota(jnp.int32, (GROUP, 128), 0)
    table[:GROUP, :] = starts.astype(jnp.int32) + run * length
    table[GROUP : 2 * GROUP, :] = targets.astype(jnp.int32)
    widest = jnp.max(sizes, axis=0, keepdims=True)
    total = jnp.sum(sizes, axis=0, keepdims=True)
    last = lax.broadcasted_iota(jnp.int32, (8, 128), 0)
    table[2 * GROUP :, :] = jnp.where(last == 0, widest, total).astype(jnp.int32)
    copy = pltpu.make_async_copy(table, table_s, sem)
    copy.start()
    return copy


def turn_runs(first_run, lists_ref, flat):
    length = lists_ref.shape[2]
    for r in range(GROUP):
        part = lists_ref[first_run + r].astype(jnp.float32)
        for first in range(0, length, 128):
            at = r * length + first
            flat[at : at + 128, :ROWS] = jnp.transpose(part[:, first : first + 128])


def products(first, size, width, packed):
    part = jnp.concatenate(
        [jnp.transpose(packed[pl.ds(first + k, 128), :])[:ROWS] for k in range(0, width, 128)],
        axis=1,
    )
    step = lax.broadcasted_iota(jnp.int32, (BLOCK, width), 0).astype(jnp.float32)
    step = step.astype(jnp.bfloat16)
    place = lax.broadcasted_iota(jnp.int32, (1, width), 1)
    one = jnp.ones((), jnp.bfloat16)
    none = jnp.zeros((), jnp.bfloat16)

    def spread(row):
        return jnp.broadcast_to(row, (BLOCK, width)).astype(jnp.bfloat16)

    hit = spread(jnp.where(place < size, part[CH + 1 : CH + 2], -1.0)) == step
    left = [jnp.where(hit, one, none)]
    left += [jnp.where(hit, spread(part[c : c + 1]), none) for c in range(CH)]
    left = jnp.concatenate(left, axis=0)
    for half in range(NG // HALF):
        low = spread(jnp.where(part[CH + 2 : CH + 3] == float(half), part[CH + 3 : CH + 4], -1.0))
        right = [
            jnp.where(low == step + jnp.bfloat16(j), one, none) for j in range(0, HALF, BLOCK)
        ]
        yield pl.ds(half * HALF, HALF), contract_last(left, jnp.concatenate(right, axis=0))


def block_rows(b):
    return pl.ds(pl.multiple_of(b * BLOCK, BLOCK), BLOCK)


def add_blocks(table_s, flat, buffers, packed, total, emit):
    def fast(b, rows, width):
        def copies(q):
            for r in range(GROUP):
                buffers[q][pl.ds(table_s[GROUP + r, b + q], rows), :] = flat[
                    pl.ds(table_s[r, b + q], rows), :
                ]

        copies(0)
        for q in range(SIDE):
            if q + 1 < SIDE:
                copies(q + 1)
            for lanes, sums in products(0, table_s[2 * GROUP + 1, b + q], width, buffers[q]):
                emit(b + q, lanes, sums)

    def slow(b):
        def run(r, _):
            source = table_s[r, b]
            target = table_s[GROUP + r, b]
            after = table_s[2 * GROUP + 1, b]
            after = jnp.where(r + 1 < GROUP, table_s[jnp.minimum(GROUP + r + 1, 2 * GROUP - 1), b], after)

            def piece(k, _):
                packed[pl.ds(target + 8 * k, 8), :] = flat[pl.ds(source + 8 * k, 8), :]
                return 0

            return lax.fori_loop(0, (after - target + 7) // 8, piece, 0)

        lax.fori_loop(0, GROUP, run, 0)
        total[...] = jnp.zeros_like(total)
        size = table_s[2 * GROUP + 1, b]

        def piece(k, _):
            first = pl.multiple_of(k * LARGE, LARGE)
            for lanes, sums in products(first, size - first, LARGE, packed):
                total[:, lanes] += sums
            return 0

        lax.fori_loop(0, (size + LARGE - 1) // LARGE, piece, 0)
        for half in range(NG // HALF):
            lanes = pl.ds(half * HALF, HALF)
            emit(b, lanes, total[:, lanes])

    def side(i, _):
        b = i * SIDE
        widest = table_s[2 * GROUP, b]
        largest = table_s[2 * GROUP + 1, b]
        for q in range(1, SIDE):
            widest = jnp.maximum(widest, table_s[2 * GROUP, b + q])
            largest = jnp.maximum(largest, table_s[2 * GROUP + 1, b + q])
        left_over = jnp.bool_(True)
        for rows, width in FORMS:
            fits = (widest <= rows) & (largest <= width)

            @pl.when(left_over & fits)
            def _(rows=rows, width=width):
                fast(b, rows, width)

            left_over = left_over & jnp.logical_not(fits)

        @pl.when(left_over)
        def _():
            lax.fori_loop(0, SIDE, lambda q, _: (slow(b + q), 0)[1], 0)

        return 0

    lax.fori_loop(0, BLOCKS // SIDE, side, 0)


def grid_kernel(
    scale, row_block, lists_ref, out_ref, planes, flat, packed, keys, table, turned, total, result,
    table_s, sem, out_sems, *rest
):
    runs = lists_ref.shape[0]
    alone = runs == GROUP
    buffers = rest[:SIDE]
    grid = rest[SIDE] if not alone else None

    def finish(sums, rows, lanes):
        inverse = 1.0 / jnp.maximum(sums(0), 1.0)
        for c in range(CH):
            planes[c, rows, lanes] = (sums(c + 1) * inverse).astype(jnp.bfloat16)

    def emit(b, lanes, sums):
        rows = block_rows(b)
        if alone:
            finish(lambda c: sums[c * BLOCK : (c + 1) * BLOCK], rows, lanes)
        else:
            for c in range(CH + 1):
                grid[c, rows, lanes] += sums[c * BLOCK : (c + 1) * BLOCK]

    def group(g, _):
        copy = make_table(g * GROUP, lists_ref, keys, table, table_s, sem)
        turn_runs(g * GROUP, lists_ref, flat)
        copy.wait()
        add_blocks(table_s, flat, buffers, packed, total, emit)
        return 0

    if alone:
        group(0, 0)
    else:
        grid[...] = jnp.zeros_like(grid)
        lax.fori_loop(0, runs // GROUP, group, 0)

        def divide(b, _):
            rows = block_rows(b)
            finish(lambda c: grid[c, rows, :], rows, pl.ds(0, NG))
            return 0

        lax.fori_loop(0, BLOCKS, divide, 0)

    first_row = pl.multiple_of(lax.axis_index("tile") * row_block, row_block)
    first_col = pl.multiple_of(first_row // 128 * 128, 128)
    within = pl.multiple_of(first_row % 128, row_block)

    def own_rows(p, slot):
        turned[slot] = jnp.transpose(planes[p, :, pl.ds(first_col, 128)].astype(jnp.float32))
        across = turned[slot, pl.ds(within, row_block), :]
        along = planes[p, pl.ds(first_row, row_block), :].astype(jnp.float32)
        return (0.5 * (along + across)).astype(jnp.bfloat16)

    def sent(f):
        return pltpu.make_async_copy(result.at[f], out_ref.at[f], out_sems.at[f])

    def frequency(f, slot):
        own = jnp.concatenate([own_rows(f, slot), own_rows(FB + f, slot + 1)], axis=0)
        real = planes[f]
        imag = planes[FB + f]
        by_real = jnp.dot(own, real, preferred_element_type=jnp.float32) + contract_last(own, real)
        by_imag = jnp.dot(own, imag, preferred_element_type=jnp.float32) + contract_last(own, imag)
        half = 0.5 * scale
        result[f, 0] = (by_real[:row_block] - by_imag[row_block:]) * half
        result[f, 1] = (by_imag[:row_block] + by_real[row_block:]) * half
        sent(f).start()

    def some(i, _):
        for q in range(BESIDE):
            frequency(i * BESIDE + q, 2 * q)
        return 0

    lax.fori_loop(0, FB // BESIDE, some, 0)
    for f in range(FB):
        sent(f).wait()


def whole(space=pltpu.VMEM):
    return pl.BlockSpec(memory_space=space)


def per_device(raw_traces, bin_owner, bin_offset):
    band_count = lax.axis_size("band")
    tile_count = lax.axis_size("tile")
    length = bin_offset.shape[1]
    count = raw_traces.shape[1]
    cells_dev = NG * NG // tile_count
    row_block = NG // tile_count
    runs = band_count * tile_count
    params = pltpu.CompilerParams(vmem_limit_bytes=VMEM)

    own = pl.pallas_call(
        functools.partial(run_kernel, cells_dev),
        out_shape=jax.ShapeDtypeStruct((band_count, tile_count, ROWS, count), jnp.bfloat16),
        in_specs=[whole()] * 4,
        out_specs=whole(),
        compiler_params=params,
        name="own_run",
    )(
        jnp.asarray(twiddle_rows(band_count)),
        raw_traces,
        bin_owner.reshape(1, length),
        bin_offset,
    )
    lists = lax.all_to_all(
        own.reshape(runs, ROWS, count), ("band", "tile"), split_axis=0, concat_axis=0, tiled=True
    )

    traces = GROUP * count
    scratch = [
        pltpu.VMEM((CH, NG, NG), jnp.bfloat16),
        pltpu.VMEM((traces + COPY, 128), jnp.float32),
        pltpu.VMEM((traces + LARGE, 128), jnp.float32),
        pltpu.VMEM((GROUP, 128), jnp.float32),
        pltpu.VMEM((2 * GROUP + 8, 128), jnp.int32),
        pltpu.VMEM((2 * BESIDE, 128, NG), jnp.float32),
        pltpu.VMEM(((CH + 1) * BLOCK, NG), jnp.float32),
        pltpu.VMEM((FB, 2, row_block, NG), jnp.float32),
        pltpu.SMEM((2 * GROUP + 8, 128), jnp.int32),
        pltpu.SemaphoreType.DMA,
        pltpu.SemaphoreType.DMA((FB,)),
    ]
    scratch += [pltpu.VMEM((LARGE + COPY, 128), jnp.float32)] * SIDE
    if runs != GROUP:
        scratch.append(pltpu.VMEM((CH + 1, NG, NG), jnp.float32))
    return pl.pallas_call(
        functools.partial(grid_kernel, 1.0 / math.sqrt(NG), row_block),
        out_shape=jax.ShapeDtypeStruct((FB, 2, row_block, NG), jnp.float32),
        in_specs=[whole()],
        out_specs=whole(pl.ANY),
        scratch_shapes=scratch,
        compiler_params=params,
        name="grid",
    )(lists)


def solution(mesh):
    return jax.shard_map(
        per_device,
        mesh=mesh,
        in_specs=(P("tile", "band", None), P("tile", None, None), P("tile", None)),
        out_specs=P("band", None, "tile", None),
        check_vma=False,
    )
```

```python
import functools
import math

import jax
import jax.numpy as jnp
import ml_dtypes
import numpy as np
from jax import lax
from jax.experimental import pallas as pl
from jax.experimental.pallas import tpu as pltpu
from jax.sharding import PartitionSpec as P

NG = 512
NT = 2048
FB = 10
CH = 2 * FB
ROWS = 24
BLOCK = 16
BLOCKS = NG // BLOCK
GROUP = 32
FORMS = ((16, 256), (32, 512), (32, 640))
COPY, LARGE = FORMS[-1]
BESIDE = 2
SIDE = 4
HALF = 256
VMEM = 56 * 1024 * 1024


def twiddle_rows(band_count):
    time_index = np.arange(NT)[None, None, :]
    freq_index = np.arange(band_count * FB).reshape(band_count, FB, 1) + 1
    angle = (time_index * freq_index % NT) * (2.0 * math.pi / NT)
    norm = 1.0 / math.sqrt(NT)
    table = np.zeros((band_count, ROWS, NT), np.float64)
    table[:, :FB] = np.cos(angle) * norm
    table[:, FB:CH] = -np.sin(angle) * norm
    return table.reshape(band_count * ROWS, NT).astype(ml_dtypes.bfloat16)


def contract_last(left, right):
    return lax.dot_general(
        left, right, (((1,), (1,)), ((), ())), preferred_element_type=jnp.float32
    )


def run_kernel(cells_dev, twiddle_ref, traces_ref, owner_ref, offset_ref, out_ref):
    bands, tiles, _, count = out_ref.shape
    lanes = pl.ds(pl.multiple_of(lax.axis_index("band") * count, count), count)
    cell = owner_ref[:, lanes] * cells_dev + offset_ref[:, lanes]
    order = cell * count + lax.broadcasted_iota(jnp.int32, (1, count), 1)
    rank = jnp.zeros((1, count), jnp.int32)
    starts = jnp.zeros((1, count), jnp.int32)
    limit = lax.broadcasted_iota(jnp.int32, (1, count), 1) * (BLOCK * NG * count)
    limit = jnp.minimum(limit, NG * NG * count)
    for first in range(0, count, 128):
        column = jnp.transpose(jnp.broadcast_to(order[:, first : first + 128], (128, 128)))
        column = jnp.concatenate([column] * (count // 128), axis=1)
        rank += jnp.sum((column < order).astype(jnp.int32), axis=0, keepdims=True)
        starts += jnp.sum((column < limit).astype(jnp.int32), axis=0, keepdims=True)
    target = lax.broadcasted_iota(jnp.int32, (count, count), 0)
    permute = (target == rank).astype(jnp.float32).astype(jnp.bfloat16)
    source = cell // NG
    receiver = cell % NG
    row = lax.broadcasted_iota(jnp.int32, (bands * ROWS, count), 0) % ROWS
    digits = jnp.where(row == CH + 1, source % BLOCK, 0)
    digits = jnp.where(row == CH + 2, receiver // HALF, digits)
    digits = jnp.where(row == CH + 3, receiver % HALF, digits)
    spectra = contract_last(twiddle_ref[...], traces_ref[0])
    packed = (spectra + digits.astype(jnp.float32)).astype(jnp.bfloat16)
    ordered = contract_last(packed, permute) + jnp.where(row == CH, starts, 0).astype(jnp.float32)
    for band in range(bands):
        part = ordered[band * ROWS : (band + 1) * ROWS].astype(jnp.bfloat16)
        for tile in range(tiles):
            out_ref[band, tile] = part


def make_table(first_run, lists_ref, keys, table, table_s, sem):
    length = lists_ref.shape[2]
    for r in range(GROUP):
        part = lists_ref[first_run + r].astype(jnp.float32)
        keys[r : r + 1, :] = part[CH : CH + 1, :128]
    starts = keys[...]
    lane = lax.broadcasted_iota(jnp.int32, (GROUP, 128), 1)
    sizes = jnp.where(lane < BLOCKS, pltpu.roll(starts, 127, 1) - starts, 0.0)
    earlier = lax.broadcasted_iota(jnp.int32, (GROUP, GROUP), 0) > lax.broadcasted_iota(
        jnp.int32, (GROUP, GROUP), 1
    )
    targets = jnp.dot(
        earlier.astype(jnp.float32).astype(jnp.bfloat16),
        sizes.astype(jnp.bfloat16),
        preferred_element_type=jnp.float32,
    )
    run = lax.broadcasted_iota(jnp.int32, (GROUP, 128), 0)
    table[:GROUP, :] = starts.astype(jnp.int32) + run * length
    table[GROUP : 2 * GROUP, :] = targets.astype(jnp.int32)
    widest = jnp.max(sizes, axis=0, keepdims=True)
    total = jnp.sum(sizes, axis=0, keepdims=True)
    last = lax.broadcasted_iota(jnp.int32, (8, 128), 0)
    table[2 * GROUP :, :] = jnp.where(last == 0, widest, total).astype(jnp.int32)
    copy = pltpu.make_async_copy(table, table_s, sem)
    copy.start()
    return copy


def turn_runs(first_run, lists_ref, flat):
    length = lists_ref.shape[2]
    for r in range(GROUP):
        part = lists_ref[first_run + r].astype(jnp.float32)
        for first in range(0, length, 128):
            at = r * length + first
            flat[at : at + 128, :ROWS] = jnp.transpose(part[:, first : first + 128])


def products(first, size, width, packed):
    part = jnp.concatenate(
        [jnp.transpose(packed[pl.ds(first + k, 128), :])[:ROWS] for k in range(0, width, 128)],
        axis=1,
    )
    step = lax.broadcasted_iota(jnp.int32, (BLOCK, width), 0).astype(jnp.float32)
    step = step.astype(jnp.bfloat16)
    place = lax.broadcasted_iota(jnp.int32, (1, width), 1)
    one = jnp.ones((), jnp.bfloat16)
    none = jnp.zeros((), jnp.bfloat16)

    def spread(row):
        return jnp.broadcast_to(row, (BLOCK, width)).astype(jnp.bfloat16)

    hit = spread(jnp.where(place < size, part[CH + 1 : CH + 2], -1.0)) == step
    left = [jnp.where(hit, one, none)]
    left += [jnp.where(hit, spread(part[c : c + 1]), none) for c in range(CH)]
    left = jnp.concatenate(left, axis=0)
    for half in range(NG // HALF):
        low = spread(jnp.where(part[CH + 2 : CH + 3] == float(half), part[CH + 3 : CH + 4], -1.0))
        right = [
            jnp.where(low == step + jnp.bfloat16(j), one, none) for j in range(0, HALF, BLOCK)
        ]
        yield pl.ds(half * HALF, HALF), contract_last(left, jnp.concatenate(right, axis=0))


def block_rows(b):
    return pl.ds(pl.multiple_of(b * BLOCK, BLOCK), BLOCK)


def add_blocks(table_s, flat, buffers, packed, total, emit):
    def fast(b, rows, width):
        def copies(q):
            for r in range(GROUP):
                buffers[q][pl.ds(table_s[GROUP + r, b + q], rows), :] = flat[
                    pl.ds(table_s[r, b + q], rows), :
                ]

        copies(0)
        for q in range(SIDE):
            if q + 1 < SIDE:
                copies(q + 1)
            for lanes, sums in products(0, table_s[2 * GROUP + 1, b + q], width, buffers[q]):
                emit(b + q, lanes, sums)

    def slow(b):
        def run(r, _):
            source = table_s[r, b]
            target = table_s[GROUP + r, b]
            after = table_s[2 * GROUP + 1, b]
            after = jnp.where(r + 1 < GROUP, table_s[jnp.minimum(GROUP + r + 1, 2 * GROUP - 1), b], after)

            def piece(k, _):
                packed[pl.ds(target + 8 * k, 8), :] = flat[pl.ds(source + 8 * k, 8), :]
                return 0

            return lax.fori_loop(0, (after - target + 7) // 8, piece, 0)

        lax.fori_loop(0, GROUP, run, 0)
        total[...] = jnp.zeros_like(total)
        size = table_s[2 * GROUP + 1, b]

        def piece(k, _):
            first = pl.multiple_of(k * LARGE, LARGE)
            for lanes, sums in products(first, size - first, LARGE, packed):
                total[:, lanes] += sums
            return 0

        lax.fori_loop(0, (size + LARGE - 1) // LARGE, piece, 0)
        for half in range(NG // HALF):
            lanes = pl.ds(half * HALF, HALF)
            emit(b, lanes, total[:, lanes])

    def side(i, _):
        b = i * SIDE
        widest = table_s[2 * GROUP, b]
        largest = table_s[2 * GROUP + 1, b]
        for q in range(1, SIDE):
            widest = jnp.maximum(widest, table_s[2 * GROUP, b + q])
            largest = jnp.maximum(largest, table_s[2 * GROUP + 1, b + q])
        left_over = jnp.bool_(True)
        for rows, width in FORMS:
            fits = (widest <= rows) & (largest <= width)

            @pl.when(left_over & fits)
            def _(rows=rows, width=width):
                fast(b, rows, width)

            left_over = left_over & jnp.logical_not(fits)

        @pl.when(left_over)
        def _():
            lax.fori_loop(0, SIDE, lambda q, _: (slow(b + q), 0)[1], 0)

        return 0

    lax.fori_loop(0, BLOCKS // SIDE, side, 0)


def grid_kernel(
    scale, row_block, lists_ref, out_ref, planes, flat, packed, keys, table, twice, total, result,
    table_s, sem, out_sems, *rest
):
    runs = lists_ref.shape[0]
    alone = runs == GROUP
    buffers = rest[:SIDE]
    grid = rest[SIDE] if not alone else None

    def finish(sums, rows, lanes):
        inverse = 1.0 / jnp.maximum(sums(0), 1.0)
        for c in range(CH):
            planes[c, rows, lanes] = (sums(c + 1) * inverse).astype(jnp.bfloat16)

    def emit(b, lanes, sums):
        rows = block_rows(b)
        if alone:
            finish(lambda c: sums[c * BLOCK : (c + 1) * BLOCK], rows, lanes)
        else:
            for c in range(CH + 1):
                grid[c, rows, lanes] += sums[c * BLOCK : (c + 1) * BLOCK]

    def group(g, _):
        copy = make_table(g * GROUP, lists_ref, keys, table, table_s, sem)
        turn_runs(g * GROUP, lists_ref, flat)
        copy.wait()
        add_blocks(table_s, flat, buffers, packed, total, emit)
        return 0

    if alone:
        group(0, 0)
    else:
        grid[...] = jnp.zeros_like(grid)
        lax.fori_loop(0, runs // GROUP, group, 0)

        def divide(b, _):
            rows = block_rows(b)
            finish(lambda c: grid[c, rows, :], rows, pl.ds(0, NG))
            return 0

        lax.fori_loop(0, BLOCKS, divide, 0)

    own_rows = pl.ds(pl.multiple_of(lax.axis_index("tile") * row_block, row_block), row_block)

    def sent(f):
        return pltpu.make_async_copy(result.at[f], out_ref.at[f], out_sems.at[f])

    def frequency(f, slot):
        for part, p in enumerate((f, FB + f)):
            plane = planes[p]
            twice[slot + part] = plane + jnp.transpose(plane)
        own = jnp.concatenate([twice[slot, own_rows, :], twice[slot + 1, own_rows, :]], axis=0)
        by_real = jnp.dot(own, twice[slot], preferred_element_type=jnp.float32)
        by_imag = jnp.dot(own, twice[slot + 1], preferred_element_type=jnp.float32)
        quarter = 0.25 * scale
        result[f, 0] = (by_real[:row_block] - by_imag[row_block:]) * quarter
        result[f, 1] = (by_imag[:row_block] + by_real[row_block:]) * quarter
        sent(f).start()

    def some(i, _):
        for q in range(BESIDE):
            frequency(i * BESIDE + q, 2 * q)
        return 0

    lax.fori_loop(0, FB // BESIDE, some, 0)
    for f in range(FB):
        sent(f).wait()


def whole(space=pltpu.VMEM):
    return pl.BlockSpec(memory_space=space)


def per_device(raw_traces, bin_owner, bin_offset):
    band_count = lax.axis_size("band")
    tile_count = lax.axis_size("tile")
    length = bin_offset.shape[1]
    count = raw_traces.shape[1]
    cells_dev = NG * NG // tile_count
    row_block = NG // tile_count
    runs = band_count * tile_count
    params = pltpu.CompilerParams(vmem_limit_bytes=VMEM)

    own = pl.pallas_call(
        functools.partial(run_kernel, cells_dev),
        out_shape=jax.ShapeDtypeStruct((band_count, tile_count, ROWS, count), jnp.bfloat16),
        in_specs=[whole()] * 4,
        out_specs=whole(),
        compiler_params=params,
        name="own_run",
    )(
        jnp.asarray(twiddle_rows(band_count)),
        raw_traces,
        bin_owner.reshape(1, length),
        bin_offset,
    )
    lists = lax.all_to_all(
        own.reshape(runs, ROWS, count), ("band", "tile"), split_axis=0, concat_axis=0, tiled=True
    )

    traces = GROUP * count
    scratch = [
        pltpu.VMEM((CH, NG, NG), jnp.bfloat16),
        pltpu.VMEM((traces + COPY, 128), jnp.float32),
        pltpu.VMEM((traces + LARGE, 128), jnp.float32),
        pltpu.VMEM((GROUP, 128), jnp.float32),
        pltpu.VMEM((2 * GROUP + 8, 128), jnp.int32),
        pltpu.VMEM((2 * BESIDE, NG, NG), jnp.bfloat16),
        pltpu.VMEM(((CH + 1) * BLOCK, NG), jnp.float32),
        pltpu.VMEM((FB, 2, row_block, NG), jnp.float32),
        pltpu.SMEM((2 * GROUP + 8, 128), jnp.int32),
        pltpu.SemaphoreType.DMA,
        pltpu.SemaphoreType.DMA((FB,)),
    ]
    scratch += [pltpu.VMEM((LARGE + COPY, 128), jnp.float32)] * SIDE
    if runs != GROUP:
        scratch.append(pltpu.VMEM((CH + 1, NG, NG), jnp.float32))
    return pl.pallas_call(
        functools.partial(grid_kernel, 1.0 / math.sqrt(NG), row_block),
        out_shape=jax.ShapeDtypeStruct((FB, 2, row_block, NG), jnp.float32),
        in_specs=[whole()],
        out_specs=whole(pl.ANY),
        scratch_shapes=scratch,
        compiler_params=params,
        name="grid",
    )(lists)


def solution(mesh):
    return jax.shard_map(
        per_device,
        mesh=mesh,
        in_specs=(P("tile", "band", None), P("tile", None, None), P("tile", None)),
        out_specs=P("band", None, "tile", None),
        check_vma=False,
    )
```

```python
import functools
import math

import jax
import jax.numpy as jnp
import ml_dtypes
import numpy as np
from jax import lax
from jax.experimental import pallas as pl
from jax.experimental.pallas import tpu as pltpu
from jax.sharding import PartitionSpec as P

NG = 512
NT = 2048
FB = 10
CH = 2 * FB
ROWS = 24
BLOCK = 16
BLOCKS = NG // BLOCK
GROUP = 32
COPY = 32
WIDTHS = (256, 512, 640)
LARGE = WIDTHS[-1]
BESIDE = 2
SIDE = 4
HALF = 256
VMEM = 56 * 1024 * 1024


def twiddle_rows(band_count):
    time_index = np.arange(NT)[None, None, :]
    freq_index = np.arange(band_count * FB).reshape(band_count, FB, 1) + 1
    angle = (time_index * freq_index % NT) * (2.0 * math.pi / NT)
    norm = 1.0 / math.sqrt(NT)
    table = np.zeros((band_count, ROWS, NT), np.float64)
    table[:, :FB] = np.cos(angle) * norm
    table[:, FB:CH] = -np.sin(angle) * norm
    return table.reshape(band_count * ROWS, NT).astype(ml_dtypes.bfloat16)


def contract_last(left, right):
    return lax.dot_general(
        left, right, (((1,), (1,)), ((), ())), preferred_element_type=jnp.float32
    )


def run_kernel(cells_dev, twiddle_ref, traces_ref, owner_ref, offset_ref, out_ref):
    bands, tiles, _, count = out_ref.shape
    lanes = pl.ds(pl.multiple_of(lax.axis_index("band") * count, count), count)
    cell = owner_ref[:, lanes] * cells_dev + offset_ref[:, lanes]
    order = cell * count + lax.broadcasted_iota(jnp.int32, (1, count), 1)
    rank = jnp.zeros((1, count), jnp.int32)
    starts = jnp.zeros((1, count), jnp.int32)
    limit = lax.broadcasted_iota(jnp.int32, (1, count), 1) * (BLOCK * NG * count)
    limit = jnp.minimum(limit, NG * NG * count)
    for first in range(0, count, 128):
        column = jnp.transpose(jnp.broadcast_to(order[:, first : first + 128], (128, 128)))
        column = jnp.concatenate([column] * (count // 128), axis=1)
        rank += jnp.sum((column < order).astype(jnp.int32), axis=0, keepdims=True)
        starts += jnp.sum((column < limit).astype(jnp.int32), axis=0, keepdims=True)
    target = lax.broadcasted_iota(jnp.int32, (count, count), 0)
    permute = (target == rank).astype(jnp.float32).astype(jnp.bfloat16)
    source = cell // NG
    receiver = cell % NG
    row = lax.broadcasted_iota(jnp.int32, (bands * ROWS, count), 0) % ROWS
    digits = jnp.where(row == CH + 1, source % BLOCK, 0)
    digits = jnp.where(row == CH + 2, receiver // HALF, digits)
    digits = jnp.where(row == CH + 3, receiver % HALF, digits)
    spectra = contract_last(twiddle_ref[...], traces_ref[0])
    packed = (spectra + digits.astype(jnp.float32)).astype(jnp.bfloat16)
    ordered = contract_last(packed, permute) + jnp.where(row == CH, starts, 0).astype(jnp.float32)
    for band in range(bands):
        part = ordered[band * ROWS : (band + 1) * ROWS].astype(jnp.bfloat16)
        for tile in range(tiles):
            out_ref[band, tile] = part


def make_table(first_run, lists_ref, keys, table, table_s, sem):
    length = lists_ref.shape[2]
    for r in range(GROUP):
        part = lists_ref[first_run + r].astype(jnp.float32)
        keys[r : r + 1, :] = part[CH : CH + 1, :128]
    starts = keys[...]
    lane = lax.broadcasted_iota(jnp.int32, (GROUP, 128), 1)
    sizes = jnp.where(lane < BLOCKS, pltpu.roll(starts, 127, 1) - starts, 0.0)
    earlier = lax.broadcasted_iota(jnp.int32, (GROUP, GROUP), 0) > lax.broadcasted_iota(
        jnp.int32, (GROUP, GROUP), 1
    )
    targets = jnp.dot(
        earlier.astype(jnp.float32).astype(jnp.bfloat16),
        sizes.astype(jnp.bfloat16),
        preferred_element_type=jnp.float32,
    )
    run = lax.broadcasted_iota(jnp.int32, (GROUP, 128), 0)
    table[:GROUP, :] = starts.astype(jnp.int32) + run * length
    table[GROUP : 2 * GROUP, :] = jnp.minimum(targets, float(LARGE)).astype(jnp.int32)
    widest = jnp.max(sizes, axis=0, keepdims=True)
    total = jnp.sum(sizes, axis=0, keepdims=True)
    last = lax.broadcasted_iota(jnp.int32, (8, 128), 0)
    table[2 * GROUP :, :] = jnp.where(last == 0, widest, total).astype(jnp.int32)
    copy = pltpu.make_async_copy(table, table_s, sem)
    copy.start()
    return copy


def turn_runs(first_run, lists_ref, flat):
    length = lists_ref.shape[2]
    for r in range(GROUP):
        part = lists_ref[first_run + r].astype(jnp.float32)
        for first in range(0, length, 128):
            at = r * length + first
            flat[at : at + 128, :ROWS] = jnp.transpose(part[:, first : first + 128])


def turned(first, width, packed):
    return jnp.concatenate(
        [jnp.transpose(packed[pl.ds(first + k, 128), :])[:ROWS] for k in range(0, width, 128)],
        axis=1,
    )


def products(part, size):
    width = part.shape[1]
    step = lax.broadcasted_iota(jnp.int32, (BLOCK, width), 0).astype(jnp.float32)
    step = step.astype(jnp.bfloat16)
    place = lax.broadcasted_iota(jnp.int32, (1, width), 1)
    one = jnp.ones((), jnp.bfloat16)
    none = jnp.zeros((), jnp.bfloat16)

    def spread(row):
        return jnp.broadcast_to(row, (BLOCK, width)).astype(jnp.bfloat16)

    hit = spread(jnp.where(place < size, part[CH + 1 : CH + 2], -1.0)) == step
    left = [jnp.where(hit, one, none)]
    left += [jnp.where(hit, spread(part[c : c + 1]), none) for c in range(CH)]
    left = jnp.concatenate(left, axis=0)
    for half in range(NG // HALF):
        low = spread(jnp.where(part[CH + 2 : CH + 3] == float(half), part[CH + 3 : CH + 4], -1.0))
        right = [
            jnp.where(low == step + jnp.bfloat16(j), one, none) for j in range(0, HALF, BLOCK)
        ]
        yield pl.ds(half * HALF, HALF), contract_last(left, jnp.concatenate(right, axis=0))


def block_rows(b):
    return pl.ds(pl.multiple_of(b * BLOCK, BLOCK), BLOCK)


def add_blocks(table_s, flat, buffers, now, later, packed, total, emit):
    sides = BLOCKS // SIDE

    def merge(i, q):
        b = jnp.minimum(i, sides - 1) * SIDE + q
        for r in range(GROUP):
            buffers[q][pl.ds(table_s[GROUP + r, b], COPY), :] = flat[pl.ds(table_s[r, b], COPY), :]
        later[q] = turned(0, LARGE, buffers[q])

    def fast(i, width):
        for q in range(SIDE):
            merge(i + 1, q)
            b = i * SIDE + q
            for lanes, sums in products(now[q, :, :width], table_s[2 * GROUP + 1, b]):
                emit(b, lanes, sums)

    def slow(b):
        def run(r, target):
            source = table_s[r, b]
            count = table_s[r, b + 1] - source

            def piece(k, _):
                packed[pl.ds(target + 8 * k, 8), :] = flat[pl.ds(source + 8 * k, 8), :]
                return 0

            lax.fori_loop(0, (count + 7) // 8, piece, 0)
            return target + count

        lax.fori_loop(0, GROUP, run, 0)
        total[...] = jnp.zeros_like(total)
        size = table_s[2 * GROUP + 1, b]

        def piece(k, _):
            first = pl.multiple_of(k * LARGE, LARGE)
            for lanes, sums in products(turned(first, LARGE, packed), size - first):
                total[:, lanes] += sums
            return 0

        lax.fori_loop(0, (size + LARGE - 1) // LARGE, piece, 0)
        for half in range(NG // HALF):
            lanes = pl.ds(half * HALF, HALF)
            emit(b, lanes, total[:, lanes])

    def side(i, _):
        b = i * SIDE
        widest = table_s[2 * GROUP, b]
        largest = table_s[2 * GROUP + 1, b]
        for q in range(1, SIDE):
            widest = jnp.maximum(widest, table_s[2 * GROUP, b + q])
            largest = jnp.maximum(largest, table_s[2 * GROUP + 1, b + q])
        now[...] = later[...]
        plain = widest <= COPY
        least = -1
        for width in WIDTHS:

            @pl.when(plain & (largest > least) & (largest <= width))
            def _(width=width):
                fast(i, width)

            least = width

        @pl.when(jnp.logical_not(plain) | (largest > LARGE))
        def _():
            for q in range(SIDE):
                merge(i + 1, q)
            lax.fori_loop(0, SIDE, lambda q, _: (slow(b + q), 0)[1], 0)

        return 0

    for q in range(SIDE):
        merge(jnp.int32(0), q)
    lax.fori_loop(0, sides, side, 0)


def grid_kernel(
    scale, row_block, lists_ref, out_ref, planes, flat, packed, keys, table, twice, total, result,
    table_s, sem, out_sems, *rest
):
    runs = lists_ref.shape[0]
    alone = runs == GROUP
    now, later, *buffers = rest[: SIDE + 2]
    grid = rest[SIDE + 2] if not alone else None

    def finish(sums, rows, lanes):
        inverse = 1.0 / jnp.maximum(sums(0), 1.0)
        for c in range(CH):
            planes[c, rows, lanes] = (sums(c + 1) * inverse).astype(jnp.bfloat16)

    def emit(b, lanes, sums):
        rows = block_rows(b)
        if alone:
            finish(lambda c: sums[c * BLOCK : (c + 1) * BLOCK], rows, lanes)
        else:
            for c in range(CH + 1):
                grid[c, rows, lanes] += sums[c * BLOCK : (c + 1) * BLOCK]

    def group(g, _):
        copy = make_table(g * GROUP, lists_ref, keys, table, table_s, sem)
        turn_runs(g * GROUP, lists_ref, flat)
        copy.wait()
        add_blocks(table_s, flat, buffers, now, later, packed, total, emit)
        return 0

    if alone:
        group(0, 0)
    else:
        grid[...] = jnp.zeros_like(grid)
        lax.fori_loop(0, runs // GROUP, group, 0)

        def divide(b, _):
            rows = block_rows(b)
            finish(lambda c: grid[c, rows, :], rows, pl.ds(0, NG))
            return 0

        lax.fori_loop(0, BLOCKS, divide, 0)

    own_rows = pl.ds(pl.multiple_of(lax.axis_index("tile") * row_block, row_block), row_block)

    def sent(f):
        return pltpu.make_async_copy(result.at[f], out_ref.at[f], out_sems.at[f])

    def frequency(f, slot):
        for part, p in enumerate((f, FB + f)):
            plane = planes[p]
            twice[slot + part] = plane + jnp.transpose(plane)
        own = jnp.concatenate([twice[slot, own_rows, :], twice[slot + 1, own_rows, :]], axis=0)
        by_real = jnp.dot(own, twice[slot], preferred_element_type=jnp.float32)
        by_imag = jnp.dot(own, twice[slot + 1], preferred_element_type=jnp.float32)
        quarter = 0.25 * scale
        result[f, 0] = (by_real[:row_block] - by_imag[row_block:]) * quarter
        result[f, 1] = (by_imag[:row_block] + by_real[row_block:]) * quarter
        sent(f).start()

    def some(i, _):
        for q in range(BESIDE):
            frequency(i * BESIDE + q, 2 * q)
        return 0

    lax.fori_loop(0, FB // BESIDE, some, 0)
    for f in range(FB):
        sent(f).wait()


def whole(space=pltpu.VMEM):
    return pl.BlockSpec(memory_space=space)


def per_device(raw_traces, bin_owner, bin_offset):
    band_count = lax.axis_size("band")
    tile_count = lax.axis_size("tile")
    length = bin_offset.shape[1]
    count = raw_traces.shape[1]
    cells_dev = NG * NG // tile_count
    row_block = NG // tile_count
    runs = band_count * tile_count
    params = pltpu.CompilerParams(vmem_limit_bytes=VMEM)

    own = pl.pallas_call(
        functools.partial(run_kernel, cells_dev),
        out_shape=jax.ShapeDtypeStruct((band_count, tile_count, ROWS, count), jnp.bfloat16),
        in_specs=[whole()] * 4,
        out_specs=whole(),
        compiler_params=params,
        name="own_run",
    )(
        jnp.asarray(twiddle_rows(band_count)),
        raw_traces,
        bin_owner.reshape(1, length),
        bin_offset,
    )
    lists = lax.all_to_all(
        own.reshape(runs, ROWS, count), ("band", "tile"), split_axis=0, concat_axis=0, tiled=True
    )

    traces = GROUP * count
    scratch = [
        pltpu.VMEM((CH, NG, NG), jnp.bfloat16),
        pltpu.VMEM((traces + COPY, 128), jnp.float32),
        pltpu.VMEM((traces + LARGE, 128), jnp.float32),
        pltpu.VMEM((GROUP, 128), jnp.float32),
        pltpu.VMEM((2 * GROUP + 8, 128), jnp.int32),
        pltpu.VMEM((2 * BESIDE, NG, NG), jnp.bfloat16),
        pltpu.VMEM(((CH + 1) * BLOCK, NG), jnp.float32),
        pltpu.VMEM((FB, 2, row_block, NG), jnp.float32),
        pltpu.SMEM((2 * GROUP + 8, 128), jnp.int32),
        pltpu.SemaphoreType.DMA,
        pltpu.SemaphoreType.DMA((FB,)),
    ]
    scratch += [pltpu.VMEM((SIDE, ROWS, LARGE), jnp.float32)] * 2
    scratch += [pltpu.VMEM((LARGE + COPY, 128), jnp.float32)] * SIDE
    if runs != GROUP:
        scratch.append(pltpu.VMEM((CH + 1, NG, NG), jnp.float32))
    return pl.pallas_call(
        functools.partial(grid_kernel, 1.0 / math.sqrt(NG), row_block),
        out_shape=jax.ShapeDtypeStruct((FB, 2, row_block, NG), jnp.float32),
        in_specs=[whole()],
        out_specs=whole(pl.ANY),
        scratch_shapes=scratch,
        compiler_params=params,
        name="grid",
    )(lists)


def solution(mesh):
    return jax.shard_map(
        per_device,
        mesh=mesh,
        in_specs=(P("tile", "band", None), P("tile", None, None), P("tile", None)),
        out_specs=P("band", None, "tile", None),
        check_vma=False,
    )
```

```python
import functools
import math

import jax
import jax.numpy as jnp
import ml_dtypes
import numpy as np
from jax import lax
from jax.experimental import pallas as pl
from jax.experimental.pallas import tpu as pltpu
from jax.sharding import PartitionSpec as P

NG = 512
NT = 2048
FB = 10
CH = 2 * FB
ROWS = 24
BLOCK = 16
BLOCKS = NG // BLOCK
GROUP = 32
COPY = 32
WIDTHS = (256, 512, 640)
LARGE = WIDTHS[-1]
BESIDE = 5
SIDE = 4
PIECES = 4
HALF = 256
VMEM = 56 * 1024 * 1024


def twiddle_rows(band_count):
    time_index = np.arange(NT)[None, None, :]
    freq_index = np.arange(band_count * FB).reshape(band_count, FB, 1) + 1
    angle = (time_index * freq_index % NT) * (2.0 * math.pi / NT)
    norm = 1.0 / math.sqrt(NT)
    table = np.zeros((band_count, ROWS, NT), np.float64)
    table[:, :FB] = np.cos(angle) * norm
    table[:, FB:CH] = -np.sin(angle) * norm
    return table.reshape(band_count * ROWS, NT).astype(ml_dtypes.bfloat16)


def contract_last(left, right):
    return lax.dot_general(
        left, right, (((1,), (1,)), ((), ())), preferred_element_type=jnp.float32
    )


def run_kernel(
    cells_dev, twiddle_ref, traces_ref, owner_ref, offset_ref, out_ref, twiddle, traces, sems
):
    width = traces.shape[1] // PIECES
    pieces = []
    for k in range(PIECES):
        columns = pl.ds(k * width, width)
        pair = (
            pltpu.make_async_copy(
                twiddle_ref.at[:, columns], twiddle.at[:, columns], sems.at[0, k]
            ),
            pltpu.make_async_copy(
                traces_ref.at[0, :, columns], traces.at[:, columns], sems.at[1, k]
            ),
        )
        for copy in pair:
            copy.start()
        pieces.append(pair)
    bands, tiles, _, count = out_ref.shape
    lanes = pl.ds(pl.multiple_of(lax.axis_index("band") * count, count), count)
    cell = owner_ref[:, lanes] * cells_dev + offset_ref[:, lanes]
    order = cell * count + lax.broadcasted_iota(jnp.int32, (1, count), 1)
    rank = jnp.zeros((1, count), jnp.int32)
    starts = jnp.zeros((1, count), jnp.int32)
    limit = lax.broadcasted_iota(jnp.int32, (1, count), 1) * (BLOCK * NG * count)
    limit = jnp.minimum(limit, NG * NG * count)
    for first in range(0, count, 128):
        column = jnp.transpose(jnp.broadcast_to(order[:, first : first + 128], (128, 128)))
        column = jnp.concatenate([column] * (count // 128), axis=1)
        rank += jnp.sum((column < order).astype(jnp.int32), axis=0, keepdims=True)
        starts += jnp.sum((column < limit).astype(jnp.int32), axis=0, keepdims=True)
    target = lax.broadcasted_iota(jnp.int32, (count, count), 0)
    permute = (target == rank).astype(jnp.float32).astype(jnp.bfloat16)
    source = cell // NG
    receiver = cell % NG
    row = lax.broadcasted_iota(jnp.int32, (bands * ROWS, count), 0) % ROWS
    digits = jnp.where(row == CH + 1, source % BLOCK, 0)
    digits = jnp.where(row == CH + 2, receiver // HALF, digits)
    digits = jnp.where(row == CH + 3, receiver % HALF, digits)
    spectra = jnp.zeros((bands * ROWS, count), jnp.float32)
    for k in range(PIECES):
        for copy in pieces[k]:
            copy.wait()
        columns = pl.ds(k * width, width)
        spectra += contract_last(twiddle[:, columns], traces[:, columns])
    packed = (spectra + digits.astype(jnp.float32)).astype(jnp.bfloat16)
    ordered = contract_last(packed, permute) + jnp.where(row == CH, starts, 0).astype(jnp.float32)
    for band in range(bands):
        part = ordered[band * ROWS : (band + 1) * ROWS].astype(jnp.bfloat16)
        for tile in range(tiles):
            out_ref[band, tile] = part


def make_table(first_run, lists_ref, keys, table, table_s, sem):
    length = lists_ref.shape[2]
    for r in range(GROUP):
        part = lists_ref[first_run + r].astype(jnp.float32)
        keys[r : r + 1, :] = part[CH : CH + 1, :128]
    starts = keys[...]
    lane = lax.broadcasted_iota(jnp.int32, (GROUP, 128), 1)
    sizes = jnp.where(lane < BLOCKS, pltpu.roll(starts, 127, 1) - starts, 0.0)
    earlier = lax.broadcasted_iota(jnp.int32, (GROUP, GROUP), 0) > lax.broadcasted_iota(
        jnp.int32, (GROUP, GROUP), 1
    )
    targets = jnp.dot(
        earlier.astype(jnp.float32).astype(jnp.bfloat16),
        sizes.astype(jnp.bfloat16),
        preferred_element_type=jnp.float32,
    )
    run = lax.broadcasted_iota(jnp.int32, (GROUP, 128), 0)
    table[:GROUP, :] = starts.astype(jnp.int32) + run * length
    table[GROUP : 2 * GROUP, :] = jnp.minimum(targets, float(LARGE)).astype(jnp.int32)
    widest = jnp.max(sizes, axis=0, keepdims=True)
    total = jnp.sum(sizes, axis=0, keepdims=True)
    last = lax.broadcasted_iota(jnp.int32, (8, 128), 0)
    table[2 * GROUP :, :] = jnp.where(last == 0, widest, total).astype(jnp.int32)
    copy = pltpu.make_async_copy(table, table_s, sem)
    copy.start()
    return copy


def turn_runs(first_run, lists_ref, flat):
    length = lists_ref.shape[2]
    for r in range(GROUP):
        part = lists_ref[first_run + r].astype(jnp.float32)
        for first in range(0, length, 128):
            at = r * length + first
            flat[at : at + 128, :ROWS] = jnp.transpose(part[:, first : first + 128])


def turned(first, width, packed):
    return jnp.concatenate(
        [jnp.transpose(packed[pl.ds(first + k, 128), :])[:ROWS] for k in range(0, width, 128)],
        axis=1,
    )


def products(part, size):
    width = part.shape[1]
    step = lax.broadcasted_iota(jnp.int32, (BLOCK, width), 0).astype(jnp.float32)
    step = step.astype(jnp.bfloat16)
    place = lax.broadcasted_iota(jnp.int32, (1, width), 1)
    one = jnp.ones((), jnp.bfloat16)
    none = jnp.zeros((), jnp.bfloat16)

    def spread(row):
        return jnp.broadcast_to(row, (BLOCK, width)).astype(jnp.bfloat16)

    hit = spread(jnp.where(place < size, part[CH + 1 : CH + 2], -1.0)) == step
    left = [jnp.where(hit, one, none)]
    left += [jnp.where(hit, spread(part[c : c + 1]), none) for c in range(CH)]
    left = jnp.concatenate(left, axis=0)
    for half in range(NG // HALF):
        low = spread(jnp.where(part[CH + 2 : CH + 3] == float(half), part[CH + 3 : CH + 4], -1.0))
        right = [
            jnp.where(low == step + jnp.bfloat16(j), one, none) for j in range(0, HALF, BLOCK)
        ]
        yield pl.ds(half * HALF, HALF), contract_last(left, jnp.concatenate(right, axis=0))


def block_rows(b):
    return pl.ds(pl.multiple_of(b * BLOCK, BLOCK), BLOCK)


def add_blocks(table_s, flat, buffers, later, packed, total, emit):
    sides = BLOCKS // SIDE

    def merge(i, q):
        b = jnp.minimum(i, sides - 1) * SIDE + q
        for r in range(GROUP):
            buffers[q][pl.ds(table_s[GROUP + r, b], COPY), :] = flat[pl.ds(table_s[r, b], COPY), :]
        later[q] = turned(0, LARGE, buffers[q])

    def fast(i, width):
        parts = [later[q, :, :width] for q in range(SIDE)]
        for q in range(SIDE):
            merge(i + 1, q)
            b = i * SIDE + q
            for lanes, sums in products(parts[q], table_s[2 * GROUP + 1, b]):
                emit(b, lanes, sums)

    def slow(b):
        def run(r, target):
            source = table_s[r, b]
            count = table_s[r, b + 1] - source

            def piece(k, _):
                packed[pl.ds(target + 8 * k, 8), :] = flat[pl.ds(source + 8 * k, 8), :]
                return 0

            lax.fori_loop(0, (count + 7) // 8, piece, 0)
            return target + count

        lax.fori_loop(0, GROUP, run, 0)
        total[...] = jnp.zeros_like(total)
        size = table_s[2 * GROUP + 1, b]

        def piece(k, _):
            first = pl.multiple_of(k * LARGE, LARGE)
            for lanes, sums in products(turned(first, LARGE, packed), size - first):
                total[:, lanes] += sums
            return 0

        lax.fori_loop(0, (size + LARGE - 1) // LARGE, piece, 0)
        for half in range(NG // HALF):
            lanes = pl.ds(half * HALF, HALF)
            emit(b, lanes, total[:, lanes])

    def side(i, _):
        b = i * SIDE
        widest = table_s[2 * GROUP, b]
        largest = table_s[2 * GROUP + 1, b]
        for q in range(1, SIDE):
            widest = jnp.maximum(widest, table_s[2 * GROUP, b + q])
            largest = jnp.maximum(largest, table_s[2 * GROUP + 1, b + q])
        plain = widest <= COPY
        least = -1
        for width in WIDTHS:

            @pl.when(plain & (largest > least) & (largest <= width))
            def _(width=width):
                fast(i, width)

            least = width

        @pl.when(jnp.logical_not(plain) | (largest > LARGE))
        def _():
            for q in range(SIDE):
                merge(i + 1, q)
            lax.fori_loop(0, SIDE, lambda q, _: (slow(b + q), 0)[1], 0)

        return 0

    for q in range(SIDE):
        merge(jnp.int32(0), q)
    lax.fori_loop(0, sides, side, 0)


def grid_kernel(
    scale, row_block, lists_ref, out_ref, planes, flat, packed, keys, table, twice, total, result,
    table_s, sem, out_sems, *rest
):
    runs = lists_ref.shape[0]
    alone = runs == GROUP
    later, *buffers = rest[: SIDE + 1]
    grid = rest[SIDE + 1] if not alone else None

    def finish(sums, rows, lanes):
        inverse = 1.0 / jnp.maximum(sums(0), 1.0)
        for c in range(CH):
            planes[c, rows, lanes] = (sums(c + 1) * inverse).astype(jnp.bfloat16)

    def emit(b, lanes, sums):
        rows = block_rows(b)
        if alone:
            finish(lambda c: sums[c * BLOCK : (c + 1) * BLOCK], rows, lanes)
        else:
            for c in range(CH + 1):
                grid[c, rows, lanes] += sums[c * BLOCK : (c + 1) * BLOCK]

    def group(g, _):
        copy = make_table(g * GROUP, lists_ref, keys, table, table_s, sem)
        turn_runs(g * GROUP, lists_ref, flat)
        copy.wait()
        add_blocks(table_s, flat, buffers, later, packed, total, emit)
        return 0

    if alone:
        group(0, 0)
    else:
        grid[...] = jnp.zeros_like(grid)
        lax.fori_loop(0, runs // GROUP, group, 0)

        def divide(b, _):
            rows = block_rows(b)
            finish(lambda c: grid[c, rows, :], rows, pl.ds(0, NG))
            return 0

        lax.fori_loop(0, BLOCKS, divide, 0)

    own_rows = pl.ds(pl.multiple_of(lax.axis_index("tile") * row_block, row_block), row_block)

    def sent(f):
        return pltpu.make_async_copy(result.at[f], out_ref.at[f], out_sems.at[f])

    def frequency(f, slot):
        for part, p in enumerate((f, FB + f)):
            plane = planes[p]
            twice[slot + part] = plane + jnp.transpose(plane)
        own = jnp.concatenate([twice[slot, own_rows, :], twice[slot + 1, own_rows, :]], axis=0)
        by_real = jnp.dot(own, twice[slot], preferred_element_type=jnp.float32)
        by_imag = jnp.dot(own, twice[slot + 1], preferred_element_type=jnp.float32)
        quarter = 0.25 * scale
        result[f, 0] = (by_real[:row_block] - by_imag[row_block:]) * quarter
        result[f, 1] = (by_imag[:row_block] + by_real[row_block:]) * quarter
        sent(f).start()

    def some(i, _):
        for q in range(BESIDE):
            frequency(i * BESIDE + q, 2 * q)
        return 0

    lax.fori_loop(0, FB // BESIDE, some, 0)
    for f in range(FB):
        sent(f).wait()


def whole(space=pltpu.VMEM):
    return pl.BlockSpec(memory_space=space)


def per_device(raw_traces, bin_owner, bin_offset):
    band_count = lax.axis_size("band")
    tile_count = lax.axis_size("tile")
    length = bin_offset.shape[1]
    count = raw_traces.shape[1]
    cells_dev = NG * NG // tile_count
    row_block = NG // tile_count
    runs = band_count * tile_count
    params = pltpu.CompilerParams(vmem_limit_bytes=VMEM)

    own = pl.pallas_call(
        functools.partial(run_kernel, cells_dev),
        out_shape=jax.ShapeDtypeStruct((band_count, tile_count, ROWS, count), jnp.bfloat16),
        in_specs=[whole(pl.ANY)] * 2 + [whole()] * 2,
        out_specs=whole(),
        scratch_shapes=[
            pltpu.VMEM((runs * ROWS // tile_count, NT), jnp.bfloat16),
            pltpu.VMEM((count, NT), jnp.bfloat16),
            pltpu.SemaphoreType.DMA((2, PIECES)),
        ],
        compiler_params=params,
        name="own_run",
    )(
        jnp.asarray(twiddle_rows(band_count)),
        raw_traces,
        bin_owner.reshape(1, length),
        bin_offset,
    )
    lists = lax.all_to_all(
        own.reshape(runs, ROWS, count), ("band", "tile"), split_axis=0, concat_axis=0, tiled=True
    )

    traces = GROUP * count
    scratch = [
        pltpu.VMEM((CH, NG, NG), jnp.bfloat16),
        pltpu.VMEM((traces + COPY, 128), jnp.float32),
        pltpu.VMEM((traces + LARGE, 128), jnp.float32),
        pltpu.VMEM((GROUP, 128), jnp.float32),
        pltpu.VMEM((2 * GROUP + 8, 128), jnp.int32),
        pltpu.VMEM((2 * BESIDE, NG, NG), jnp.bfloat16),
        pltpu.VMEM(((CH + 1) * BLOCK, NG), jnp.float32),
        pltpu.VMEM((FB, 2, row_block, NG), jnp.float32),
        pltpu.SMEM((2 * GROUP + 8, 128), jnp.int32),
        pltpu.SemaphoreType.DMA,
        pltpu.SemaphoreType.DMA((FB,)),
    ]
    scratch.append(pltpu.VMEM((SIDE, ROWS, LARGE), jnp.float32))
    scratch += [pltpu.VMEM((LARGE + COPY, 128), jnp.float32)] * SIDE
    if runs != GROUP:
        scratch.append(pltpu.VMEM((CH + 1, NG, NG), jnp.float32))
    return pl.pallas_call(
        functools.partial(grid_kernel, 1.0 / math.sqrt(NG), row_block),
        out_shape=jax.ShapeDtypeStruct((FB, 2, row_block, NG), jnp.float32),
        in_specs=[whole()],
        out_specs=whole(pl.ANY),
        scratch_shapes=scratch,
        compiler_params=params,
        name="grid",
    )(lists)


def solution(mesh):
    return jax.shard_map(
        per_device,
        mesh=mesh,
        in_specs=(P("tile", "band", None), P("tile", None, None), P("tile", None)),
        out_specs=P("band", None, "tile", None),
        check_vma=False,
    )
```

```python
import functools
import math

import jax
import jax.numpy as jnp
import ml_dtypes
import numpy as np
from jax import lax
from jax.experimental import pallas as pl
from jax.experimental.pallas import tpu as pltpu
from jax.sharding import PartitionSpec as P

NG = 512
NT = 2048
FB = 10
CH = 2 * FB
ROWS = 24
BLOCK = 16
BLOCKS = NG // BLOCK
GROUP = 32
COPY = 32
WIDTHS = (256, 512, 640)
LARGE = WIDTHS[-1]
BESIDE = 5
SIDE = 4
TURN = 128
HALF = 256
VMEM = 56 * 1024 * 1024


def twiddle_rows(band_count):
    time_index = np.arange(NT)[None, None, :]
    freq_index = np.arange(band_count * FB).reshape(band_count, FB, 1) + 1
    angle = (time_index * freq_index % NT) * (2.0 * math.pi / NT)
    norm = 1.0 / math.sqrt(NT)
    table = np.zeros((band_count, ROWS, NT), np.float64)
    table[:, :FB] = np.cos(angle) * norm
    table[:, FB:CH] = -np.sin(angle) * norm
    return table.reshape(band_count * ROWS, NT).astype(ml_dtypes.bfloat16)


def contract_last(left, right):
    return lax.dot_general(
        left, right, (((1,), (1,)), ((), ())), preferred_element_type=jnp.float32
    )


def run_kernel(cells_dev, twiddle_ref, traces_ref, owner_ref, offset_ref, out_ref):
    bands, tiles, _, count = out_ref.shape
    lanes = pl.ds(pl.multiple_of(lax.axis_index("band") * count, count), count)
    cell = owner_ref[:, lanes] * cells_dev + offset_ref[:, lanes]
    order = cell * count + lax.broadcasted_iota(jnp.int32, (1, count), 1)
    rank = jnp.zeros((1, count), jnp.int32)
    starts = jnp.zeros((1, count), jnp.int32)
    limit = lax.broadcasted_iota(jnp.int32, (1, count), 1) * (BLOCK * NG * count)
    limit = jnp.minimum(limit, NG * NG * count)
    for first in range(0, count, 128):
        column = jnp.transpose(jnp.broadcast_to(order[:, first : first + 128], (128, 128)))
        column = jnp.concatenate([column] * (count // 128), axis=1)
        rank += jnp.sum((column < order).astype(jnp.int32), axis=0, keepdims=True)
        starts += jnp.sum((column < limit).astype(jnp.int32), axis=0, keepdims=True)
    target = lax.broadcasted_iota(jnp.int32, (count, count), 0)
    permute = (target == rank).astype(jnp.float32).astype(jnp.bfloat16)
    source = cell // NG
    receiver = cell % NG
    row = lax.broadcasted_iota(jnp.int32, (bands * ROWS, count), 0) % ROWS
    digits = jnp.where(row == CH + 1, source % BLOCK, 0)
    digits = jnp.where(row == CH + 2, receiver // HALF, digits)
    digits = jnp.where(row == CH + 3, receiver % HALF, digits)
    spectra = contract_last(twiddle_ref[...], traces_ref[0])
    packed = (spectra + digits.astype(jnp.float32)).astype(jnp.bfloat16)
    ordered = contract_last(packed, permute) + jnp.where(row == CH, starts, 0).astype(jnp.float32)
    for band in range(bands):
        part = ordered[band * ROWS : (band + 1) * ROWS].astype(jnp.bfloat16)
        for tile in range(tiles):
            out_ref[band, tile] = part


def make_table(first_run, lists_ref, keys, table, table_s, sem):
    length = lists_ref.shape[2]
    for r in range(GROUP):
        part = lists_ref[first_run + r].astype(jnp.float32)
        keys[r : r + 1, :] = part[CH : CH + 1, :128]
    starts = keys[...]
    lane = lax.broadcasted_iota(jnp.int32, (GROUP, 128), 1)
    sizes = jnp.where(lane < BLOCKS, pltpu.roll(starts, 127, 1) - starts, 0.0)
    earlier = lax.broadcasted_iota(jnp.int32, (GROUP, GROUP), 0) > lax.broadcasted_iota(
        jnp.int32, (GROUP, GROUP), 1
    )
    targets = jnp.dot(
        earlier.astype(jnp.float32).astype(jnp.bfloat16),
        sizes.astype(jnp.bfloat16),
        preferred_element_type=jnp.float32,
    )
    run = lax.broadcasted_iota(jnp.int32, (GROUP, 128), 0)
    table[:GROUP, :] = starts.astype(jnp.int32) + run * length
    table[GROUP : 2 * GROUP, :] = jnp.minimum(targets, float(LARGE)).astype(jnp.int32)
    widest = jnp.max(sizes, axis=0, keepdims=True)
    total = jnp.sum(sizes, axis=0, keepdims=True)
    last = lax.broadcasted_iota(jnp.int32, (8, 128), 0)
    table[2 * GROUP :, :] = jnp.where(last == 0, widest, total).astype(jnp.int32)
    copy = pltpu.make_async_copy(table, table_s, sem)
    copy.start()
    return copy


def turn_runs(first_run, lists_ref, flat):
    length = lists_ref.shape[2]
    for r in range(GROUP):
        part = lists_ref[first_run + r].astype(jnp.float32)
        for first in range(0, length, 128):
            at = r * length + first
            flat[at : at + 128, :ROWS] = jnp.transpose(part[:, first : first + 128])


def turned(first, width, packed):
    return jnp.concatenate(
        [jnp.transpose(packed[pl.ds(first + k, 128), :])[:ROWS] for k in range(0, width, 128)],
        axis=1,
    )


def products(part, size):
    width = part.shape[1]
    step = lax.broadcasted_iota(jnp.int32, (BLOCK, width), 0).astype(jnp.float32)
    step = step.astype(jnp.bfloat16)
    place = lax.broadcasted_iota(jnp.int32, (1, width), 1)
    one = jnp.ones((), jnp.bfloat16)
    none = jnp.zeros((), jnp.bfloat16)

    def spread(row):
        return jnp.broadcast_to(row, (BLOCK, width)).astype(jnp.bfloat16)

    hit = spread(jnp.where(place < size, part[CH + 1 : CH + 2], -1.0)) == step
    left = [jnp.where(hit, one, none)]
    left += [jnp.where(hit, spread(part[c : c + 1]), none) for c in range(CH)]
    left = jnp.concatenate(left, axis=0)
    for half in range(NG // HALF):
        low = spread(jnp.where(part[CH + 2 : CH + 3] == float(half), part[CH + 3 : CH + 4], -1.0))
        right = [
            jnp.where(low == step + jnp.bfloat16(j), one, none) for j in range(0, HALF, BLOCK)
        ]
        yield pl.ds(half * HALF, HALF), contract_last(left, jnp.concatenate(right, axis=0))


def block_rows(b):
    return pl.ds(pl.multiple_of(b * BLOCK, BLOCK), BLOCK)


def add_blocks(table_s, flat, buffers, later, packed, total, emit):
    sides = BLOCKS // SIDE

    def merge(i, q):
        b = jnp.minimum(i, sides - 1) * SIDE + q
        for r in range(GROUP):
            buffers[q][pl.ds(table_s[GROUP + r, b], COPY), :] = flat[pl.ds(table_s[r, b], COPY), :]
        later[q] = turned(0, LARGE, buffers[q])

    def fast(i, width):
        parts = [later[q, :, :width] for q in range(SIDE)]
        for q in range(SIDE):
            merge(i + 1, q)
            b = i * SIDE + q
            for lanes, sums in products(parts[q], table_s[2 * GROUP + 1, b]):
                emit(b, lanes, sums)

    def slow(b):
        def run(r, target):
            source = table_s[r, b]
            count = table_s[r, b + 1] - source

            def piece(k, _):
                packed[pl.ds(target + 8 * k, 8), :] = flat[pl.ds(source + 8 * k, 8), :]
                return 0

            lax.fori_loop(0, (count + 7) // 8, piece, 0)
            return target + count

        lax.fori_loop(0, GROUP, run, 0)
        total[...] = jnp.zeros_like(total)
        size = table_s[2 * GROUP + 1, b]

        def piece(k, _):
            first = pl.multiple_of(k * LARGE, LARGE)
            for lanes, sums in products(turned(first, LARGE, packed), size - first):
                total[:, lanes] += sums
            return 0

        lax.fori_loop(0, (size + LARGE - 1) // LARGE, piece, 0)
        for half in range(NG // HALF):
            lanes = pl.ds(half * HALF, HALF)
            emit(b, lanes, total[:, lanes])

    def side(i, _):
        b = i * SIDE
        widest = table_s[2 * GROUP, b]
        largest = table_s[2 * GROUP + 1, b]
        for q in range(1, SIDE):
            widest = jnp.maximum(widest, table_s[2 * GROUP, b + q])
            largest = jnp.maximum(largest, table_s[2 * GROUP + 1, b + q])
        plain = widest <= COPY
        least = -1
        for width in WIDTHS:

            @pl.when(plain & (largest > least) & (largest <= width))
            def _(width=width):
                fast(i, width)

            least = width

        @pl.when(jnp.logical_not(plain) | (largest > LARGE))
        def _():
            for q in range(SIDE):
                merge(i + 1, q)
            lax.fori_loop(0, SIDE, lambda q, _: (slow(b + q), 0)[1], 0)

        return 0

    for q in range(SIDE):
        merge(jnp.int32(0), q)
    lax.fori_loop(0, sides, side, 0)


def grid_kernel(
    scale, row_block, lists_ref, out_ref, planes, flat, packed, keys, table, twice, total, result,
    table_s, sem, out_sems, *rest
):
    runs = lists_ref.shape[0]
    alone = runs == GROUP
    later, *buffers = rest[: SIDE + 1]
    grid = rest[SIDE + 1] if not alone else None

    def finish(sums, rows, lanes):
        inverse = 1.0 / jnp.maximum(sums(0), 1.0)
        for c in range(CH):
            planes[c, rows, lanes] = (sums(c + 1) * inverse).astype(jnp.bfloat16)

    def emit(b, lanes, sums):
        rows = block_rows(b)
        if alone:
            finish(lambda c: sums[c * BLOCK : (c + 1) * BLOCK], rows, lanes)
        else:
            for c in range(CH + 1):
                grid[c, rows, lanes] += sums[c * BLOCK : (c + 1) * BLOCK]

    def group(g, _):
        copy = make_table(g * GROUP, lists_ref, keys, table, table_s, sem)
        turn_runs(g * GROUP, lists_ref, flat)
        copy.wait()
        add_blocks(table_s, flat, buffers, later, packed, total, emit)
        return 0

    if alone:
        group(0, 0)
    else:
        grid[...] = jnp.zeros_like(grid)
        lax.fori_loop(0, runs // GROUP, group, 0)

        def divide(b, _):
            rows = block_rows(b)
            finish(lambda c: grid[c, rows, :], rows, pl.ds(0, NG))
            return 0

        lax.fori_loop(0, BLOCKS, divide, 0)

    first_row = pl.multiple_of(lax.axis_index("tile") * row_block, row_block)

    def sent(f):
        return pltpu.make_async_copy(result.at[f], out_ref.at[f], out_sems.at[f])

    def frequency(f, slot):
        for part, p in enumerate((f, FB + f)):
            for i in range(0, NG, TURN):
                for j in range(0, NG, TURN):
                    across = jnp.transpose(planes[p, j : j + TURN, i : i + TURN])
                    twice[slot, part * NG + i : part * NG + i + TURN, j : j + TURN] = (
                        planes[p, i : i + TURN, j : j + TURN] + across
                    )
        real = twice[slot, pl.ds(first_row, row_block), :]
        imag = twice[slot, pl.ds(NG + first_row, row_block), :]
        own = jnp.concatenate(
            [jnp.concatenate([real, -imag], axis=1), jnp.concatenate([imag, real], axis=1)], axis=0
        )
        for half in range(NG // HALF):
            lanes = slice(half * HALF, (half + 1) * HALF)
            both = jnp.dot(own, twice[slot, :, lanes], preferred_element_type=jnp.float32)
            both = both * (0.25 * scale)
            result[f, 0, :, lanes] = both[:row_block]
            result[f, 1, :, lanes] = both[row_block:]
        sent(f).start()

    def some(i, _):
        for q in range(BESIDE):
            frequency(i * BESIDE + q, q)
        return 0

    lax.fori_loop(0, FB // BESIDE, some, 0)
    for f in range(FB):
        sent(f).wait()


def whole(space=pltpu.VMEM):
    return pl.BlockSpec(memory_space=space)


def per_device(raw_traces, bin_owner, bin_offset):
    band_count = lax.axis_size("band")
    tile_count = lax.axis_size("tile")
    length = bin_offset.shape[1]
    count = raw_traces.shape[1]
    cells_dev = NG * NG // tile_count
    row_block = NG // tile_count
    runs = band_count * tile_count
    params = pltpu.CompilerParams(vmem_limit_bytes=VMEM)

    own = pl.pallas_call(
        functools.partial(run_kernel, cells_dev),
        out_shape=jax.ShapeDtypeStruct((band_count, tile_count, ROWS, count), jnp.bfloat16),
        in_specs=[whole()] * 4,
        out_specs=whole(),
        compiler_params=params,
        name="own_run",
    )(
        jnp.asarray(twiddle_rows(band_count)),
        raw_traces,
        bin_owner.reshape(1, length),
        bin_offset,
    )
    lists = lax.all_to_all(
        own.reshape(runs, ROWS, count), ("band", "tile"), split_axis=0, concat_axis=0, tiled=True
    )

    traces = GROUP * count
    scratch = [
        pltpu.VMEM((CH, NG, NG), jnp.bfloat16),
        pltpu.VMEM((traces + COPY, 128), jnp.float32),
        pltpu.VMEM((traces + LARGE, 128), jnp.float32),
        pltpu.VMEM((GROUP, 128), jnp.float32),
        pltpu.VMEM((2 * GROUP + 8, 128), jnp.int32),
        pltpu.VMEM((BESIDE, 2 * NG, NG), jnp.bfloat16),
        pltpu.VMEM(((CH + 1) * BLOCK, NG), jnp.float32),
        pltpu.VMEM((FB, 2, row_block, NG), jnp.float32),
        pltpu.SMEM((2 * GROUP + 8, 128), jnp.int32),
        pltpu.SemaphoreType.DMA,
        pltpu.SemaphoreType.DMA((FB,)),
    ]
    scratch.append(pltpu.VMEM((SIDE, ROWS, LARGE), jnp.float32))
    scratch += [pltpu.VMEM((LARGE + COPY, 128), jnp.float32)] * SIDE
    if runs != GROUP:
        scratch.append(pltpu.VMEM((CH + 1, NG, NG), jnp.float32))
    return pl.pallas_call(
        functools.partial(grid_kernel, 1.0 / math.sqrt(NG), row_block),
        out_shape=jax.ShapeDtypeStruct((FB, 2, row_block, NG), jnp.float32),
        in_specs=[whole()],
        out_specs=whole(pl.ANY),
        scratch_shapes=scratch,
        compiler_params=params,
        name="grid",
    )(lists)


def solution(mesh):
    return jax.shard_map(
        per_device,
        mesh=mesh,
        in_specs=(P("tile", "band", None), P("tile", None, None), P("tile", None)),
        out_specs=P("band", None, "tile", None),
        check_vma=False,
    )
```

```python
import functools
import math

import jax
import jax.numpy as jnp
import ml_dtypes
import numpy as np
from jax import lax
from jax.experimental import pallas as pl
from jax.experimental.pallas import tpu as pltpu
from jax.sharding import PartitionSpec as P

NG = 512
NT = 2048
FB = 10
CH = 2 * FB
ROWS = 24
LANES = 32
BLOCK = 16
BLOCKS = NG // BLOCK
GROUP = 32
COPY = 32
WIDTHS = (256, 512, 640)
LARGE = WIDTHS[-1]
BESIDE = 5
SIDE = 128 // LANES
TURN = 128
HALF = 256
VMEM = 56 * 1024 * 1024


def twiddle_rows(band_count):
    time_index = np.arange(NT)[None, None, :]
    freq_index = np.arange(band_count * FB).reshape(band_count, FB, 1) + 1
    angle = (time_index * freq_index % NT) * (2.0 * math.pi / NT)
    norm = 1.0 / math.sqrt(NT)
    table = np.zeros((band_count, ROWS, NT), np.float64)
    table[:, :FB] = np.cos(angle) * norm
    table[:, FB:CH] = -np.sin(angle) * norm
    return table.reshape(band_count * ROWS, NT).astype(ml_dtypes.bfloat16)


def contract_last(left, right):
    return lax.dot_general(
        left, right, (((1,), (1,)), ((), ())), preferred_element_type=jnp.float32
    )


def run_kernel(cells_dev, twiddle_ref, traces_ref, owner_ref, offset_ref, out_ref):
    bands, tiles, _, count = out_ref.shape
    lanes = pl.ds(pl.multiple_of(lax.axis_index("band") * count, count), count)
    cell = owner_ref[:, lanes] * cells_dev + offset_ref[:, lanes]
    order = cell * count + lax.broadcasted_iota(jnp.int32, (1, count), 1)
    rank = jnp.zeros((1, count), jnp.int32)
    starts = jnp.zeros((1, count), jnp.int32)
    limit = lax.broadcasted_iota(jnp.int32, (1, count), 1) * (BLOCK * NG * count)
    limit = jnp.minimum(limit, NG * NG * count)
    for first in range(0, count, 128):
        column = jnp.transpose(jnp.broadcast_to(order[:, first : first + 128], (128, 128)))
        column = jnp.concatenate([column] * (count // 128), axis=1)
        rank += jnp.sum((column < order).astype(jnp.int32), axis=0, keepdims=True)
        starts += jnp.sum((column < limit).astype(jnp.int32), axis=0, keepdims=True)
    target = lax.broadcasted_iota(jnp.int32, (count, count), 0)
    permute = (target == rank).astype(jnp.float32).astype(jnp.bfloat16)
    source = cell // NG
    receiver = cell % NG
    row = lax.broadcasted_iota(jnp.int32, (bands * ROWS, count), 0) % ROWS
    digits = jnp.where(row == CH + 1, source % BLOCK, 0)
    digits = jnp.where(row == CH + 2, receiver // HALF, digits)
    digits = jnp.where(row == CH + 3, receiver % HALF, digits)
    spectra = contract_last(twiddle_ref[...], traces_ref[0])
    packed = (spectra + digits.astype(jnp.float32)).astype(jnp.bfloat16)
    ordered = contract_last(packed, permute) + jnp.where(row == CH, starts, 0).astype(jnp.float32)
    for band in range(bands):
        part = ordered[band * ROWS : (band + 1) * ROWS].astype(jnp.bfloat16)
        for tile in range(tiles):
            out_ref[band, tile] = part


def make_table(first_run, lists_ref, keys, table, table_s, sem):
    length = lists_ref.shape[2]
    for r in range(GROUP):
        part = lists_ref[first_run + r].astype(jnp.float32)
        keys[r : r + 1, :] = part[CH : CH + 1, :128]
    starts = keys[...]
    lane = lax.broadcasted_iota(jnp.int32, (GROUP, 128), 1)
    sizes = jnp.where(lane < BLOCKS, pltpu.roll(starts, 127, 1) - starts, 0.0)
    earlier = lax.broadcasted_iota(jnp.int32, (GROUP, GROUP), 0) > lax.broadcasted_iota(
        jnp.int32, (GROUP, GROUP), 1
    )
    targets = jnp.dot(
        earlier.astype(jnp.float32).astype(jnp.bfloat16),
        sizes.astype(jnp.bfloat16),
        preferred_element_type=jnp.float32,
    )
    run = lax.broadcasted_iota(jnp.int32, (GROUP, 128), 0)
    table[:GROUP, :] = starts.astype(jnp.int32) + run * length
    table[GROUP : 2 * GROUP, :] = jnp.minimum(targets, float(LARGE)).astype(jnp.int32)
    widest = jnp.max(sizes, axis=0, keepdims=True)
    total = jnp.sum(sizes, axis=0, keepdims=True)
    last = lax.broadcasted_iota(jnp.int32, (8, 128), 0)
    table[2 * GROUP :, :] = jnp.where(last == 0, widest, total).astype(jnp.int32)
    copy = pltpu.make_async_copy(table, table_s, sem)
    copy.start()
    return copy


def turn_runs(first_run, lists_ref, flat):
    length = lists_ref.shape[2]
    rest = jnp.zeros((LANES - ROWS, length), jnp.float32)
    for r in range(GROUP):
        part = lists_ref[first_run + r].astype(jnp.float32)
        part = jnp.concatenate([part, rest] * SIDE, axis=0)
        for first in range(0, length, 128):
            at = r * length + first
            flat[at : at + 128, :] = jnp.transpose(part[:, first : first + 128])


def turned(first, packed):
    return jnp.concatenate(
        [jnp.transpose(packed[pl.ds(first + k, 128), :]) for k in range(0, LARGE, 128)], axis=1
    )


def products(part, size):
    width = part.shape[1]
    step = lax.broadcasted_iota(jnp.int32, (BLOCK, width), 0).astype(jnp.float32)
    step = step.astype(jnp.bfloat16)
    place = lax.broadcasted_iota(jnp.int32, (1, width), 1)
    one = jnp.ones((), jnp.bfloat16)
    none = jnp.zeros((), jnp.bfloat16)

    def spread(row):
        return jnp.broadcast_to(row, (BLOCK, width)).astype(jnp.bfloat16)

    hit = spread(jnp.where(place < size, part[CH + 1 : CH + 2], -1.0)) == step
    left = [jnp.where(hit, one, none)]
    left += [jnp.where(hit, spread(part[c : c + 1]), none) for c in range(CH)]
    left = jnp.concatenate(left, axis=0)
    for half in range(NG // HALF):
        low = spread(jnp.where(part[CH + 2 : CH + 3] == float(half), part[CH + 3 : CH + 4], -1.0))
        right = [
            jnp.where(low == step + jnp.bfloat16(j), one, none) for j in range(0, HALF, BLOCK)
        ]
        yield pl.ds(half * HALF, HALF), contract_last(left, jnp.concatenate(right, axis=0))


def block_rows(b):
    return pl.ds(pl.multiple_of(b * BLOCK, BLOCK), BLOCK)


def add_blocks(table_s, flat, buffer, later, packed, total, emit):
    sides = BLOCKS // SIDE

    lane = lax.broadcasted_iota(jnp.int32, (COPY, 128), 1)

    def merge(i, q):
        b = jnp.minimum(i, sides - 1) * SIDE + q
        mine = (lane >= q * LANES) & (lane < (q + 1) * LANES)
        for r in range(GROUP):
            pltpu.store(
                buffer.at[pl.ds(table_s[GROUP + r, b], COPY), :],
                flat[pl.ds(table_s[r, b], COPY), :],
                mask=mine,
            )

    def fast(i, width):
        parts = [later[q * LANES : q * LANES + ROWS, :width] for q in range(SIDE)]
        for q in range(SIDE):
            merge(i + 1, q)
            b = i * SIDE + q
            for lanes, sums in products(parts[q], table_s[2 * GROUP + 1, b]):
                emit(b, lanes, sums)
        later[...] = turned(0, buffer)

    def slow(b):
        def run(r, target):
            source = table_s[r, b]
            count = table_s[r, b + 1] - source

            def piece(k, _):
                packed[pl.ds(target + 8 * k, 8), :] = flat[pl.ds(source + 8 * k, 8), :]
                return 0

            lax.fori_loop(0, (count + 7) // 8, piece, 0)
            return target + count

        lax.fori_loop(0, GROUP, run, 0)
        total[...] = jnp.zeros_like(total)
        size = table_s[2 * GROUP + 1, b]

        def piece(k, _):
            first = pl.multiple_of(k * LARGE, LARGE)
            for lanes, sums in products(turned(first, packed)[:ROWS], size - first):
                total[:, lanes] += sums
            return 0

        lax.fori_loop(0, (size + LARGE - 1) // LARGE, piece, 0)
        for half in range(NG // HALF):
            lanes = pl.ds(half * HALF, HALF)
            emit(b, lanes, total[:, lanes])

    def side(i, _):
        b = i * SIDE
        widest = table_s[2 * GROUP, b]
        largest = table_s[2 * GROUP + 1, b]
        for q in range(1, SIDE):
            widest = jnp.maximum(widest, table_s[2 * GROUP, b + q])
            largest = jnp.maximum(largest, table_s[2 * GROUP + 1, b + q])
        plain = widest <= COPY
        least = -1
        for width in WIDTHS:

            @pl.when(plain & (largest > least) & (largest <= width))
            def _(width=width):
                fast(i, width)

            least = width

        @pl.when(jnp.logical_not(plain) | (largest > LARGE))
        def _():
            for q in range(SIDE):
                merge(i + 1, q)
            later[...] = turned(0, buffer)
            lax.fori_loop(0, SIDE, lambda q, _: (slow(b + q), 0)[1], 0)

        return 0

    for q in range(SIDE):
        merge(jnp.int32(0), q)
    later[...] = turned(0, buffer)
    lax.fori_loop(0, sides, side, 0)


def grid_kernel(
    scale, row_block, lists_ref, out_ref, planes, flat, packed, keys, table, twice, total, result,
    table_s, sem, out_sems, *rest
):
    runs = lists_ref.shape[0]
    alone = runs == GROUP
    later, buffer = rest[:2]
    grid = rest[2] if not alone else None

    def finish(sums, rows, lanes):
        inverse = 1.0 / jnp.maximum(sums(0), 1.0)
        for c in range(CH):
            planes[c, rows, lanes] = (sums(c + 1) * inverse).astype(jnp.bfloat16)

    def emit(b, lanes, sums):
        rows = block_rows(b)
        if alone:
            finish(lambda c: sums[c * BLOCK : (c + 1) * BLOCK], rows, lanes)
        else:
            for c in range(CH + 1):
                grid[c, rows, lanes] += sums[c * BLOCK : (c + 1) * BLOCK]

    def group(g, _):
        copy = make_table(g * GROUP, lists_ref, keys, table, table_s, sem)
        turn_runs(g * GROUP, lists_ref, flat)
        copy.wait()
        add_blocks(table_s, flat, buffer, later, packed, total, emit)
        return 0

    if alone:
        group(0, 0)
    else:
        grid[...] = jnp.zeros_like(grid)
        lax.fori_loop(0, runs // GROUP, group, 0)

        def divide(b, _):
            rows = block_rows(b)
            finish(lambda c: grid[c, rows, :], rows, pl.ds(0, NG))
            return 0

        lax.fori_loop(0, BLOCKS, divide, 0)

    first_row = pl.multiple_of(lax.axis_index("tile") * row_block, row_block)

    def sent(f):
        return pltpu.make_async_copy(result.at[f], out_ref.at[f], out_sems.at[f])

    def frequency(f, slot):
        for part, p in enumerate((f, FB + f)):
            for i in range(0, NG, TURN):
                for j in range(0, NG, TURN):
                    across = jnp.transpose(planes[p, j : j + TURN, i : i + TURN])
                    twice[slot, part * NG + i : part * NG + i + TURN, j : j + TURN] = (
                        planes[p, i : i + TURN, j : j + TURN] + across
                    )
        real = twice[slot, pl.ds(first_row, row_block), :]
        imag = twice[slot, pl.ds(NG + first_row, row_block), :]
        own = jnp.concatenate(
            [jnp.concatenate([real, -imag], axis=1), jnp.concatenate([imag, real], axis=1)], axis=0
        )
        for half in range(NG // HALF):
            lanes = slice(half * HALF, (half + 1) * HALF)
            both = jnp.dot(own, twice[slot, :, lanes], preferred_element_type=jnp.float32)
            both = both * (0.25 * scale)
            result[f, 0, :, lanes] = both[:row_block]
            result[f, 1, :, lanes] = both[row_block:]
        sent(f).start()

    def some(i, _):
        for q in range(BESIDE):
            frequency(i * BESIDE + q, q)
        return 0

    lax.fori_loop(0, FB // BESIDE, some, 0)
    for f in range(FB):
        sent(f).wait()


def whole(space=pltpu.VMEM):
    return pl.BlockSpec(memory_space=space)


def per_device(raw_traces, bin_owner, bin_offset):
    band_count = lax.axis_size("band")
    tile_count = lax.axis_size("tile")
    length = bin_offset.shape[1]
    count = raw_traces.shape[1]
    cells_dev = NG * NG // tile_count
    row_block = NG // tile_count
    runs = band_count * tile_count
    params = pltpu.CompilerParams(vmem_limit_bytes=VMEM)

    own = pl.pallas_call(
        functools.partial(run_kernel, cells_dev),
        out_shape=jax.ShapeDtypeStruct((band_count, tile_count, ROWS, count), jnp.bfloat16),
        in_specs=[whole()] * 4,
        out_specs=whole(),
        compiler_params=params,
        name="own_run",
    )(
        jnp.asarray(twiddle_rows(band_count)),
        raw_traces,
        bin_owner.reshape(1, length),
        bin_offset,
    )
    lists = lax.all_to_all(
        own.reshape(runs, ROWS, count), ("band", "tile"), split_axis=0, concat_axis=0, tiled=True
    )

    traces = GROUP * count
    scratch = [
        pltpu.VMEM((CH, NG, NG), jnp.bfloat16),
        pltpu.VMEM((traces + COPY, 128), jnp.float32),
        pltpu.VMEM((traces + LARGE, 128), jnp.float32),
        pltpu.VMEM((GROUP, 128), jnp.float32),
        pltpu.VMEM((2 * GROUP + 8, 128), jnp.int32),
        pltpu.VMEM((BESIDE, 2 * NG, NG), jnp.bfloat16),
        pltpu.VMEM(((CH + 1) * BLOCK, NG), jnp.float32),
        pltpu.VMEM((FB, 2, row_block, NG), jnp.float32),
        pltpu.SMEM((2 * GROUP + 8, 128), jnp.int32),
        pltpu.SemaphoreType.DMA,
        pltpu.SemaphoreType.DMA((FB,)),
    ]
    scratch.append(pltpu.VMEM((128, LARGE), jnp.float32))
    scratch.append(pltpu.VMEM((LARGE + COPY, 128), jnp.float32))
    if runs != GROUP:
        scratch.append(pltpu.VMEM((CH + 1, NG, NG), jnp.float32))
    return pl.pallas_call(
        functools.partial(grid_kernel, 1.0 / math.sqrt(NG), row_block),
        out_shape=jax.ShapeDtypeStruct((FB, 2, row_block, NG), jnp.float32),
        in_specs=[whole()],
        out_specs=whole(pl.ANY),
        scratch_shapes=scratch,
        compiler_params=params,
        name="grid",
    )(lists)


def solution(mesh):
    return jax.shard_map(
        per_device,
        mesh=mesh,
        in_specs=(P("tile", "band", None), P("tile", None, None), P("tile", None)),
        out_specs=P("band", None, "tile", None),
        check_vma=False,
    )
```

```python
import functools
import math

import jax
import jax.numpy as jnp
import ml_dtypes
import numpy as np
from jax import lax
from jax.experimental import pallas as pl
from jax.experimental.pallas import tpu as pltpu
from jax.sharding import PartitionSpec as P

NG = 512
NT = 2048
FB = 10
CH = 2 * FB
ROWS = 24
BLOCK = 32
HALF = 256
HALVES = NG // HALF
BLOCKS = NG // BLOCK * HALVES
GROUP = 32
COPY = 32
WIDTHS = (256, 512, 640)
LARGE = WIDTHS[-1]
BESIDE = 5
SIDE = 4
TURN = 128
VMEM = 56 * 1024 * 1024


def twiddle_rows(band_count):
    time_index = np.arange(NT)[None, None, :]
    freq_index = np.arange(band_count * FB).reshape(band_count, FB, 1) + 1
    angle = (time_index * freq_index % NT) * (2.0 * math.pi / NT)
    norm = 1.0 / math.sqrt(NT)
    table = np.zeros((band_count, ROWS, NT), np.float64)
    table[:, :FB] = np.cos(angle) * norm
    table[:, FB:CH] = -np.sin(angle) * norm
    return table.reshape(band_count * ROWS, NT).astype(ml_dtypes.bfloat16)


def contract_last(left, right):
    return lax.dot_general(
        left, right, (((1,), (1,)), ((), ())), preferred_element_type=jnp.float32
    )


def run_kernel(cells_dev, twiddle_ref, traces_ref, owner_ref, offset_ref, out_ref):
    bands, tiles, _, count = out_ref.shape
    lanes = pl.ds(pl.multiple_of(lax.axis_index("band") * count, count), count)
    cell = owner_ref[:, lanes] * cells_dev + offset_ref[:, lanes]
    source = cell // NG
    receiver = cell % NG
    block = source // BLOCK * HALVES + receiver // HALF
    order = block * count + lax.broadcasted_iota(jnp.int32, (1, count), 1)
    rank = jnp.zeros((1, count), jnp.int32)
    starts = jnp.zeros((1, count), jnp.int32)
    limit = lax.broadcasted_iota(jnp.int32, (1, count), 1) * count
    for first in range(0, count, 128):
        column = jnp.transpose(jnp.broadcast_to(order[:, first : first + 128], (128, 128)))
        column = jnp.concatenate([column] * (count // 128), axis=1)
        rank += jnp.sum((column < order).astype(jnp.int32), axis=0, keepdims=True)
        starts += jnp.sum((column < limit).astype(jnp.int32), axis=0, keepdims=True)
    target = lax.broadcasted_iota(jnp.int32, (count, count), 0)
    permute = (target == rank).astype(jnp.float32).astype(jnp.bfloat16)
    row = lax.broadcasted_iota(jnp.int32, (bands * ROWS, count), 0) % ROWS
    digits = jnp.where(row == CH + 1, source % BLOCK, 0)
    digits = jnp.where(row == CH + 2, receiver % HALF, digits)
    spectra = contract_last(twiddle_ref[...], traces_ref[0])
    packed = (spectra + digits.astype(jnp.float32)).astype(jnp.bfloat16)
    ordered = contract_last(packed, permute) + jnp.where(row == CH, starts, 0).astype(jnp.float32)
    for band in range(bands):
        part = ordered[band * ROWS : (band + 1) * ROWS].astype(jnp.bfloat16)
        for tile in range(tiles):
            out_ref[band, tile] = part


def make_table(first_run, lists_ref, keys, table, table_s, sem):
    length = lists_ref.shape[2]
    for r in range(GROUP):
        part = lists_ref[first_run + r].astype(jnp.float32)
        keys[r : r + 1, :] = part[CH : CH + 1, :128]
    starts = keys[...]
    lane = lax.broadcasted_iota(jnp.int32, (GROUP, 128), 1)
    sizes = jnp.where(lane < BLOCKS, pltpu.roll(starts, 127, 1) - starts, 0.0)
    earlier = lax.broadcasted_iota(jnp.int32, (GROUP, GROUP), 0) > lax.broadcasted_iota(
        jnp.int32, (GROUP, GROUP), 1
    )
    targets = jnp.dot(
        earlier.astype(jnp.float32).astype(jnp.bfloat16),
        sizes.astype(jnp.bfloat16),
        preferred_element_type=jnp.float32,
    )
    run = lax.broadcasted_iota(jnp.int32, (GROUP, 128), 0)
    table[:GROUP, :] = starts.astype(jnp.int32) + run * length
    table[GROUP : 2 * GROUP, :] = jnp.minimum(targets, float(LARGE)).astype(jnp.int32)
    widest = jnp.max(sizes, axis=0, keepdims=True)
    total = jnp.sum(sizes, axis=0, keepdims=True)
    last = lax.broadcasted_iota(jnp.int32, (8, 128), 0)
    table[2 * GROUP :, :] = jnp.where(last == 0, widest, total).astype(jnp.int32)
    copy = pltpu.make_async_copy(table, table_s, sem)
    copy.start()
    return copy


def turn_runs(first_run, lists_ref, flat):
    length = lists_ref.shape[2]
    for r in range(GROUP):
        part = lists_ref[first_run + r].astype(jnp.float32)
        for first in range(0, length, 128):
            at = r * length + first
            flat[at : at + 128, :ROWS] = jnp.transpose(part[:, first : first + 128])


def turned(first, width, packed):
    return jnp.concatenate(
        [jnp.transpose(packed[pl.ds(first + k, 128), :])[:ROWS] for k in range(0, width, 128)],
        axis=1,
    )


def products(part, size):
    width = part.shape[1]
    step = lax.broadcasted_iota(jnp.int32, (BLOCK, width), 0).astype(jnp.float32)
    step = step.astype(jnp.bfloat16)
    place = lax.broadcasted_iota(jnp.int32, (1, width), 1)
    one = jnp.ones((), jnp.bfloat16)
    none = jnp.zeros((), jnp.bfloat16)

    def spread(row):
        return jnp.broadcast_to(row, (BLOCK, width)).astype(jnp.bfloat16)

    hit = spread(jnp.where(place < size, part[CH + 1 : CH + 2], -1.0)) == step
    left = [jnp.where(hit, one, none)]
    left += [jnp.where(hit, spread(part[c : c + 1]), none) for c in range(CH)]
    receiver = spread(part[CH + 2 : CH + 3])
    right = [jnp.where(receiver == step + jnp.bfloat16(j), one, none) for j in range(0, HALF, BLOCK)]
    return contract_last(jnp.concatenate(left, axis=0), jnp.concatenate(right, axis=0))


def spot(b):
    rows = pl.ds(pl.multiple_of(b // HALVES * BLOCK, BLOCK), BLOCK)
    return rows, pl.ds(pl.multiple_of(b % HALVES * HALF, HALF), HALF)


def add_blocks(table_s, flat, buffers, later, packed, total, emit):
    sides = BLOCKS // SIDE

    def merge(i, q):
        b = jnp.minimum(i, sides - 1) * SIDE + q
        for r in range(GROUP):
            buffers[q][pl.ds(table_s[GROUP + r, b], COPY), :] = flat[pl.ds(table_s[r, b], COPY), :]
        later[q] = turned(0, LARGE, buffers[q])

    def fast(i, width):
        parts = [later[q, :, :width] for q in range(SIDE)]
        for q in range(SIDE):
            merge(i + 1, q)
            b = i * SIDE + q
            emit(b, products(parts[q], table_s[2 * GROUP + 1, b]))

    def slow(b):
        def run(r, target):
            source = table_s[r, b]
            count = table_s[r, b + 1] - source

            def piece(k, _):
                packed[pl.ds(target + 8 * k, 8), :] = flat[pl.ds(source + 8 * k, 8), :]
                return 0

            lax.fori_loop(0, (count + 7) // 8, piece, 0)
            return target + count

        lax.fori_loop(0, GROUP, run, 0)
        total[...] = jnp.zeros_like(total)
        size = table_s[2 * GROUP + 1, b]

        def piece(k, _):
            first = pl.multiple_of(k * LARGE, LARGE)
            total[...] += products(turned(first, LARGE, packed), size - first)
            return 0

        lax.fori_loop(0, (size + LARGE - 1) // LARGE, piece, 0)
        emit(b, total[...])

    def side(i, _):
        b = i * SIDE
        widest = table_s[2 * GROUP, b]
        largest = table_s[2 * GROUP + 1, b]
        for q in range(1, SIDE):
            widest = jnp.maximum(widest, table_s[2 * GROUP, b + q])
            largest = jnp.maximum(largest, table_s[2 * GROUP + 1, b + q])
        plain = widest <= COPY
        least = -1
        for width in WIDTHS:

            @pl.when(plain & (largest > least) & (largest <= width))
            def _(width=width):
                fast(i, width)

            least = width

        @pl.when(jnp.logical_not(plain) | (largest > LARGE))
        def _():
            for q in range(SIDE):
                merge(i + 1, q)
            lax.fori_loop(0, SIDE, lambda q, _: (slow(b + q), 0)[1], 0)

        return 0

    for q in range(SIDE):
        merge(jnp.int32(0), q)
    lax.fori_loop(0, sides, side, 0)


def grid_kernel(
    scale, row_block, lists_ref, out_ref, planes, flat, packed, keys, table, twice, total, result,
    table_s, sem, out_sems, *rest
):
    runs = lists_ref.shape[0]
    alone = runs == GROUP
    later, *buffers = rest[: SIDE + 1]
    grid = rest[SIDE + 1] if not alone else None

    def finish(sums, rows, lanes):
        inverse = 1.0 / jnp.maximum(sums(0), 1.0)
        for c in range(CH):
            planes[c, rows, lanes] = (sums(c + 1) * inverse).astype(jnp.bfloat16)

    def emit(b, sums):
        rows, lanes = spot(b)
        if alone:
            finish(lambda c: sums[c * BLOCK : (c + 1) * BLOCK], rows, lanes)
        else:
            for c in range(CH + 1):
                grid[c, rows, lanes] += sums[c * BLOCK : (c + 1) * BLOCK]

    def group(g, _):
        copy = make_table(g * GROUP, lists_ref, keys, table, table_s, sem)
        turn_runs(g * GROUP, lists_ref, flat)
        copy.wait()
        add_blocks(table_s, flat, buffers, later, packed, total, emit)
        return 0

    if alone:
        group(0, 0)
    else:
        grid[...] = jnp.zeros_like(grid)
        lax.fori_loop(0, runs // GROUP, group, 0)

        def divide(b, _):
            rows, lanes = spot(b)
            finish(lambda c: grid[c, rows, lanes], rows, lanes)
            return 0

        lax.fori_loop(0, BLOCKS, divide, 0)

    first_row = pl.multiple_of(lax.axis_index("tile") * row_block, row_block)

    def sent(f):
        return pltpu.make_async_copy(result.at[f], out_ref.at[f], out_sems.at[f])

    def frequency(f, slot):
        for part, p in enumerate((f, FB + f)):
            for i in range(0, NG, TURN):
                for j in range(0, NG, TURN):
                    across = jnp.transpose(planes[p, j : j + TURN, i : i + TURN])
                    twice[slot, part * NG + i : part * NG + i + TURN, j : j + TURN] = (
                        planes[p, i : i + TURN, j : j + TURN] + across
                    )
        real = twice[slot, pl.ds(first_row, row_block), :]
        imag = twice[slot, pl.ds(NG + first_row, row_block), :]
        own = jnp.concatenate(
            [jnp.concatenate([real, -imag], axis=1), jnp.concatenate([imag, real], axis=1)], axis=0
        )
        for half in range(NG // HALF):
            lanes = slice(half * HALF, (half + 1) * HALF)
            both = jnp.dot(own, twice[slot, :, lanes], preferred_element_type=jnp.float32)
            both = both * (0.25 * scale)
            result[f, 0, :, lanes] = both[:row_block]
            result[f, 1, :, lanes] = both[row_block:]
        sent(f).start()

    def some(i, _):
        for q in range(BESIDE):
            frequency(i * BESIDE + q, q)
        return 0

    lax.fori_loop(0, FB // BESIDE, some, 0)
    for f in range(FB):
        sent(f).wait()


def whole(space=pltpu.VMEM):
    return pl.BlockSpec(memory_space=space)


def per_device(raw_traces, bin_owner, bin_offset):
    band_count = lax.axis_size("band")
    tile_count = lax.axis_size("tile")
    length = bin_offset.shape[1]
    count = raw_traces.shape[1]
    cells_dev = NG * NG // tile_count
    row_block = NG // tile_count
    runs = band_count * tile_count
    params = pltpu.CompilerParams(vmem_limit_bytes=VMEM)

    own = pl.pallas_call(
        functools.partial(run_kernel, cells_dev),
        out_shape=jax.ShapeDtypeStruct((band_count, tile_count, ROWS, count), jnp.bfloat16),
        in_specs=[whole()] * 4,
        out_specs=whole(),
        compiler_params=params,
        name="own_run",
    )(
        jnp.asarray(twiddle_rows(band_count)),
        raw_traces,
        bin_owner.reshape(1, length),
        bin_offset,
    )
    lists = lax.all_to_all(
        own.reshape(runs, ROWS, count), ("band", "tile"), split_axis=0, concat_axis=0, tiled=True
    )

    traces = GROUP * count
    scratch = [
        pltpu.VMEM((CH, NG, NG), jnp.bfloat16),
        pltpu.VMEM((traces + COPY, 128), jnp.float32),
        pltpu.VMEM((traces + LARGE, 128), jnp.float32),
        pltpu.VMEM((GROUP, 128), jnp.float32),
        pltpu.VMEM((2 * GROUP + 8, 128), jnp.int32),
        pltpu.VMEM((BESIDE, 2 * NG, NG), jnp.bfloat16),
        pltpu.VMEM(((CH + 1) * BLOCK, HALF), jnp.float32),
        pltpu.VMEM((FB, 2, row_block, NG), jnp.float32),
        pltpu.SMEM((2 * GROUP + 8, 128), jnp.int32),
        pltpu.SemaphoreType.DMA,
        pltpu.SemaphoreType.DMA((FB,)),
    ]
    scratch.append(pltpu.VMEM((SIDE, ROWS, LARGE), jnp.float32))
    scratch += [pltpu.VMEM((LARGE + COPY, 128), jnp.float32)] * SIDE
    if runs != GROUP:
        scratch.append(pltpu.VMEM((CH + 1, NG, NG), jnp.float32))
    return pl.pallas_call(
        functools.partial(grid_kernel, 1.0 / math.sqrt(NG), row_block),
        out_shape=jax.ShapeDtypeStruct((FB, 2, row_block, NG), jnp.float32),
        in_specs=[whole()],
        out_specs=whole(pl.ANY),
        scratch_shapes=scratch,
        compiler_params=params,
        name="grid",
    )(lists)


def solution(mesh):
    return jax.shard_map(
        per_device,
        mesh=mesh,
        in_specs=(P("tile", "band", None), P("tile", None, None), P("tile", None)),
        out_specs=P("band", None, "tile", None),
        check_vma=False,
    )
```

```python
import functools
import math

import jax
import jax.numpy as jnp
import ml_dtypes
import numpy as np
from jax import lax
from jax.experimental import pallas as pl
from jax.experimental.pallas import tpu as pltpu
from jax.sharding import PartitionSpec as P

NG = 512
NT = 2048
FB = 10
CH = 2 * FB
ROWS = 24
BLOCK = 16
BLOCKS = NG // BLOCK
GROUP = 32
COPY = 32
WIDTHS = (128, 256, 384, 512, 640)
LARGE = WIDTHS[-1]
BESIDE = 5
SIDE = 4
TURN = 128
HALF = 256
VMEM = 56 * 1024 * 1024


def twiddle_rows(band_count):
    time_index = np.arange(NT)[None, None, :]
    freq_index = np.arange(band_count * FB).reshape(band_count, FB, 1) + 1
    angle = (time_index * freq_index % NT) * (2.0 * math.pi / NT)
    norm = 1.0 / math.sqrt(NT)
    table = np.zeros((band_count, ROWS, NT), np.float64)
    table[:, :FB] = np.cos(angle) * norm
    table[:, FB:CH] = -np.sin(angle) * norm
    return table.reshape(band_count * ROWS, NT).astype(ml_dtypes.bfloat16)


def contract_last(left, right):
    return lax.dot_general(
        left, right, (((1,), (1,)), ((), ())), preferred_element_type=jnp.float32
    )


def run_kernel(cells_dev, twiddle_ref, traces_ref, owner_ref, offset_ref, out_ref):
    bands, tiles, _, count = out_ref.shape
    lanes = pl.ds(pl.multiple_of(lax.axis_index("band") * count, count), count)
    cell = owner_ref[:, lanes] * cells_dev + offset_ref[:, lanes]
    order = cell * count + lax.broadcasted_iota(jnp.int32, (1, count), 1)
    rank = jnp.zeros((1, count), jnp.int32)
    starts = jnp.zeros((1, count), jnp.int32)
    limit = lax.broadcasted_iota(jnp.int32, (1, count), 1) * (BLOCK * NG * count)
    limit = jnp.minimum(limit, NG * NG * count)
    for first in range(0, count, 128):
        column = jnp.transpose(jnp.broadcast_to(order[:, first : first + 128], (128, 128)))
        column = jnp.concatenate([column] * (count // 128), axis=1)
        rank += jnp.sum((column < order).astype(jnp.int32), axis=0, keepdims=True)
        starts += jnp.sum((column < limit).astype(jnp.int32), axis=0, keepdims=True)
    target = lax.broadcasted_iota(jnp.int32, (count, count), 0)
    permute = (target == rank).astype(jnp.float32).astype(jnp.bfloat16)
    source = cell // NG
    receiver = cell % NG
    row = lax.broadcasted_iota(jnp.int32, (bands * ROWS, count), 0) % ROWS
    digits = jnp.where(row == CH + 1, source % BLOCK, 0)
    digits = jnp.where(row == CH + 2, receiver // HALF, digits)
    digits = jnp.where(row == CH + 3, receiver % HALF, digits)
    spectra = contract_last(twiddle_ref[...], traces_ref[0])
    packed = (spectra + digits.astype(jnp.float32)).astype(jnp.bfloat16)
    ordered = contract_last(packed, permute) + jnp.where(row == CH, starts, 0).astype(jnp.float32)
    for band in range(bands):
        part = ordered[band * ROWS : (band + 1) * ROWS].astype(jnp.bfloat16)
        for tile in range(tiles):
            out_ref[band, tile] = part


def make_table(first_run, lists_ref, keys, table, table_s, sem):
    length = lists_ref.shape[2]
    for r in range(GROUP):
        part = lists_ref[first_run + r].astype(jnp.float32)
        keys[r : r + 1, :] = part[CH : CH + 1, :128]
    starts = keys[...]
    lane = lax.broadcasted_iota(jnp.int32, (GROUP, 128), 1)
    sizes = jnp.where(lane < BLOCKS, pltpu.roll(starts, 127, 1) - starts, 0.0)
    earlier = lax.broadcasted_iota(jnp.int32, (GROUP, GROUP), 0) > lax.broadcasted_iota(
        jnp.int32, (GROUP, GROUP), 1
    )
    targets = jnp.dot(
        earlier.astype(jnp.float32).astype(jnp.bfloat16),
        sizes.astype(jnp.bfloat16),
        preferred_element_type=jnp.float32,
    )
    run = lax.broadcasted_iota(jnp.int32, (GROUP, 128), 0)
    table[:GROUP, :] = starts.astype(jnp.int32) + run * length
    table[GROUP : 2 * GROUP, :] = jnp.minimum(targets, float(LARGE)).astype(jnp.int32)
    widest = jnp.max(sizes, axis=0, keepdims=True)
    total = jnp.sum(sizes, axis=0, keepdims=True)
    last = lax.broadcasted_iota(jnp.int32, (8, 128), 0)
    table[2 * GROUP :, :] = jnp.where(last == 0, widest, total).astype(jnp.int32)
    copy = pltpu.make_async_copy(table, table_s, sem)
    copy.start()
    return copy


def turn_runs(first_run, lists_ref, flat):
    length = lists_ref.shape[2]
    for r in range(GROUP):
        part = lists_ref[first_run + r].astype(jnp.float32)
        for first in range(0, length, 128):
            at = r * length + first
            flat[at : at + 128, :ROWS] = jnp.transpose(part[:, first : first + 128])


def turned(first, width, packed):
    return jnp.concatenate(
        [jnp.transpose(packed[pl.ds(first + k, 128), :])[:ROWS] for k in range(0, width, 128)],
        axis=1,
    )


def products(part, size):
    width = part.shape[1]
    step = lax.broadcasted_iota(jnp.int32, (BLOCK, width), 0).astype(jnp.float32)
    step = step.astype(jnp.bfloat16)
    place = lax.broadcasted_iota(jnp.int32, (1, width), 1)
    one = jnp.ones((), jnp.bfloat16)
    none = jnp.zeros((), jnp.bfloat16)

    def spread(row):
        return jnp.broadcast_to(row, (BLOCK, width)).astype(jnp.bfloat16)

    hit = spread(jnp.where(place < size, part[CH + 1 : CH + 2], -1.0)) == step
    left = [jnp.where(hit, one, none)]
    left += [jnp.where(hit, spread(part[c : c + 1]), none) for c in range(CH)]
    left = jnp.concatenate(left, axis=0)
    for half in range(NG // HALF):
        low = spread(jnp.where(part[CH + 2 : CH + 3] == float(half), part[CH + 3 : CH + 4], -1.0))
        right = [
            jnp.where(low == step + jnp.bfloat16(j), one, none) for j in range(0, HALF, BLOCK)
        ]
        yield pl.ds(half * HALF, HALF), contract_last(left, jnp.concatenate(right, axis=0))


def block_rows(b):
    return pl.ds(pl.multiple_of(b * BLOCK, BLOCK), BLOCK)


def add_blocks(table_s, flat, buffers, later, packed, total, emit):
    sides = BLOCKS // SIDE

    def merge(i, q):
        b = jnp.minimum(i, sides - 1) * SIDE + q
        for r in range(GROUP):
            buffers[q][pl.ds(table_s[GROUP + r, b], COPY), :] = flat[pl.ds(table_s[r, b], COPY), :]
        later[q] = turned(0, LARGE, buffers[q])

    def fast(i, width):
        parts = [later[q, :, :width] for q in range(SIDE)]
        for q in range(SIDE):
            merge(i + 1, q)
            b = i * SIDE + q
            for lanes, sums in products(parts[q], table_s[2 * GROUP + 1, b]):
                emit(b, lanes, sums)

    def slow(b):
        def run(r, target):
            source = table_s[r, b]
            count = table_s[r, b + 1] - source

            def piece(k, _):
                packed[pl.ds(target + 8 * k, 8), :] = flat[pl.ds(source + 8 * k, 8), :]
                return 0

            lax.fori_loop(0, (count + 7) // 8, piece, 0)
            return target + count

        lax.fori_loop(0, GROUP, run, 0)
        total[...] = jnp.zeros_like(total)
        size = table_s[2 * GROUP + 1, b]

        def piece(k, _):
            first = pl.multiple_of(k * LARGE, LARGE)
            for lanes, sums in products(turned(first, LARGE, packed), size - first):
                total[:, lanes] += sums
            return 0

        lax.fori_loop(0, (size + LARGE - 1) // LARGE, piece, 0)
        for half in range(NG // HALF):
            lanes = pl.ds(half * HALF, HALF)
            emit(b, lanes, total[:, lanes])

    def side(i, _):
        b = i * SIDE
        widest = table_s[2 * GROUP, b]
        largest = table_s[2 * GROUP + 1, b]
        for q in range(1, SIDE):
            widest = jnp.maximum(widest, table_s[2 * GROUP, b + q])
            largest = jnp.maximum(largest, table_s[2 * GROUP + 1, b + q])
        plain = widest <= COPY
        least = -1
        for width in WIDTHS:

            @pl.when(plain & (largest > least) & (largest <= width))
            def _(width=width):
                fast(i, width)

            least = width

        @pl.when(jnp.logical_not(plain) | (largest > LARGE))
        def _():
            for q in range(SIDE):
                merge(i + 1, q)
            lax.fori_loop(0, SIDE, lambda q, _: (slow(b + q), 0)[1], 0)

        return 0

    for q in range(SIDE):
        merge(jnp.int32(0), q)
    lax.fori_loop(0, sides, side, 0)


def grid_kernel(
    scale, row_block, lists_ref, out_ref, planes, flat, packed, keys, table, twice, total, result,
    table_s, sem, out_sems, *rest
):
    runs = lists_ref.shape[0]
    alone = runs == GROUP
    later, *buffers = rest[: SIDE + 1]
    grid = rest[SIDE + 1] if not alone else None

    def finish(sums, rows, lanes):
        inverse = 1.0 / jnp.maximum(sums(0), 1.0)
        for c in range(CH):
            planes[c, rows, lanes] = (sums(c + 1) * inverse).astype(jnp.bfloat16)

    def emit(b, lanes, sums):
        rows = block_rows(b)
        if alone:
            finish(lambda c: sums[c * BLOCK : (c + 1) * BLOCK], rows, lanes)
        else:
            for c in range(CH + 1):
                grid[c, rows, lanes] += sums[c * BLOCK : (c + 1) * BLOCK]

    def group(g, _):
        copy = make_table(g * GROUP, lists_ref, keys, table, table_s, sem)
        turn_runs(g * GROUP, lists_ref, flat)
        copy.wait()
        add_blocks(table_s, flat, buffers, later, packed, total, emit)
        return 0

    if alone:
        group(0, 0)
    else:
        grid[...] = jnp.zeros_like(grid)
        lax.fori_loop(0, runs // GROUP, group, 0)

        def divide(b, _):
            rows = block_rows(b)
            finish(lambda c: grid[c, rows, :], rows, pl.ds(0, NG))
            return 0

        lax.fori_loop(0, BLOCKS, divide, 0)

    first_row = pl.multiple_of(lax.axis_index("tile") * row_block, row_block)

    def sent(f):
        return pltpu.make_async_copy(result.at[f], out_ref.at[f], out_sems.at[f])

    def frequency(f, slot):
        for part, p in enumerate((f, FB + f)):
            for i in range(0, NG, TURN):
                for j in range(0, NG, TURN):
                    across = jnp.transpose(planes[p, j : j + TURN, i : i + TURN])
                    twice[slot, part * NG + i : part * NG + i + TURN, j : j + TURN] = (
                        planes[p, i : i + TURN, j : j + TURN] + across
                    )
        real = twice[slot, pl.ds(first_row, row_block), :]
        imag = twice[slot, pl.ds(NG + first_row, row_block), :]
        own = jnp.concatenate(
            [jnp.concatenate([real, -imag], axis=1), jnp.concatenate([imag, real], axis=1)], axis=0
        )
        for half in range(NG // HALF):
            lanes = slice(half * HALF, (half + 1) * HALF)
            both = jnp.dot(own, twice[slot, :, lanes], preferred_element_type=jnp.float32)
            both = both * (0.25 * scale)
            result[f, 0, :, lanes] = both[:row_block]
            result[f, 1, :, lanes] = both[row_block:]
        sent(f).start()

    def some(i, _):
        for q in range(BESIDE):
            frequency(i * BESIDE + q, q)
        return 0

    lax.fori_loop(0, FB // BESIDE, some, 0)
    for f in range(FB):
        sent(f).wait()


def whole(space=pltpu.VMEM):
    return pl.BlockSpec(memory_space=space)


def per_device(raw_traces, bin_owner, bin_offset):
    band_count = lax.axis_size("band")
    tile_count = lax.axis_size("tile")
    length = bin_offset.shape[1]
    count = raw_traces.shape[1]
    cells_dev = NG * NG // tile_count
    row_block = NG // tile_count
    runs = band_count * tile_count
    params = pltpu.CompilerParams(vmem_limit_bytes=VMEM)

    own = pl.pallas_call(
        functools.partial(run_kernel, cells_dev),
        out_shape=jax.ShapeDtypeStruct((band_count, tile_count, ROWS, count), jnp.bfloat16),
        in_specs=[whole()] * 4,
        out_specs=whole(),
        compiler_params=params,
        name="own_run",
    )(
        jnp.asarray(twiddle_rows(band_count)),
        raw_traces,
        bin_owner.reshape(1, length),
        bin_offset,
    )
    lists = lax.all_to_all(
        own.reshape(runs, ROWS, count), ("band", "tile"), split_axis=0, concat_axis=0, tiled=True
    )

    traces = GROUP * count
    scratch = [
        pltpu.VMEM((CH, NG, NG), jnp.bfloat16),
        pltpu.VMEM((traces + COPY, 128), jnp.float32),
        pltpu.VMEM((traces + LARGE, 128), jnp.float32),
        pltpu.VMEM((GROUP, 128), jnp.float32),
        pltpu.VMEM((2 * GROUP + 8, 128), jnp.int32),
        pltpu.VMEM((BESIDE, 2 * NG, NG), jnp.bfloat16),
        pltpu.VMEM(((CH + 1) * BLOCK, NG), jnp.float32),
        pltpu.VMEM((FB, 2, row_block, NG), jnp.float32),
        pltpu.SMEM((2 * GROUP + 8, 128), jnp.int32),
        pltpu.SemaphoreType.DMA,
        pltpu.SemaphoreType.DMA((FB,)),
    ]
    scratch.append(pltpu.VMEM((SIDE, ROWS, LARGE), jnp.float32))
    scratch += [pltpu.VMEM((LARGE + COPY, 128), jnp.float32)] * SIDE
    if runs != GROUP:
        scratch.append(pltpu.VMEM((CH + 1, NG, NG), jnp.float32))
    return pl.pallas_call(
        functools.partial(grid_kernel, 1.0 / math.sqrt(NG), row_block),
        out_shape=jax.ShapeDtypeStruct((FB, 2, row_block, NG), jnp.float32),
        in_specs=[whole()],
        out_specs=whole(pl.ANY),
        scratch_shapes=scratch,
        compiler_params=params,
        name="grid",
    )(lists)


def solution(mesh):
    return jax.shard_map(
        per_device,
        mesh=mesh,
        in_specs=(P("tile", "band", None), P("tile", None, None), P("tile", None)),
        out_specs=P("band", None, "tile", None),
        check_vma=False,
    )
```

```python
import functools
import math

import jax
import jax.numpy as jnp
import ml_dtypes
import numpy as np
from jax import lax
from jax.experimental import pallas as pl
from jax.experimental.pallas import tpu as pltpu
from jax.sharding import PartitionSpec as P

NG = 512
NT = 2048
FB = 10
CH = 2 * FB
ROWS = 24
BLOCK = 16
BLOCKS = NG // BLOCK
GROUP = 32
COPY = 32
WIDTHS = (256, 512, 640)
LARGE = WIDTHS[-1]
BESIDE = 5
SIDE = 4
TURN = 128
HALF = 256
VMEM = 56 * 1024 * 1024


def twiddle_rows(band_count):
    time_index = np.arange(NT)[None, None, :]
    freq_index = np.arange(band_count * FB).reshape(band_count, FB, 1) + 1
    angle = (time_index * freq_index % NT) * (2.0 * math.pi / NT)
    norm = 1.0 / math.sqrt(NT)
    table = np.zeros((band_count, ROWS, NT), np.float64)
    table[:, :FB] = np.cos(angle) * norm
    table[:, FB:CH] = -np.sin(angle) * norm
    return table.reshape(band_count * ROWS, NT).astype(ml_dtypes.bfloat16)


def contract_last(left, right):
    return lax.dot_general(
        left, right, (((1,), (1,)), ((), ())), preferred_element_type=jnp.float32
    )


def run_kernel(cells_dev, twiddle_ref, traces_ref, owner_ref, offset_ref, out_ref):
    tiles, bands, _, count = out_ref.shape
    lanes = pl.ds(pl.multiple_of(lax.axis_index("band") * count, count), count)
    cell = owner_ref[:, lanes] * cells_dev + offset_ref[:, lanes]
    order = cell * count + lax.broadcasted_iota(jnp.int32, (1, count), 1)
    rank = jnp.zeros((1, count), jnp.int32)
    starts = jnp.zeros((1, count), jnp.int32)
    limit = lax.broadcasted_iota(jnp.int32, (1, count), 1) * (BLOCK * NG * count)
    limit = jnp.minimum(limit, NG * NG * count)
    for first in range(0, count, 128):
        column = jnp.transpose(jnp.broadcast_to(order[:, first : first + 128], (128, 128)))
        column = jnp.concatenate([column] * (count // 128), axis=1)
        rank += jnp.sum((column < order).astype(jnp.int32), axis=0, keepdims=True)
        starts += jnp.sum((column < limit).astype(jnp.int32), axis=0, keepdims=True)
    target = lax.broadcasted_iota(jnp.int32, (count, count), 0)
    permute = (target == rank).astype(jnp.float32).astype(jnp.bfloat16)
    source = cell // NG
    receiver = cell % NG
    row = lax.broadcasted_iota(jnp.int32, (bands * ROWS, count), 0) % ROWS
    digits = jnp.where(row == CH + 1, source % BLOCK, 0)
    digits = jnp.where(row == CH + 2, receiver // HALF, digits)
    digits = jnp.where(row == CH + 3, receiver % HALF, digits)
    spectra = contract_last(twiddle_ref[...], traces_ref[0])
    packed = (spectra + digits.astype(jnp.float32)).astype(jnp.bfloat16)
    ordered = contract_last(packed, permute) + jnp.where(row == CH, starts, 0).astype(jnp.float32)
    for band in range(bands):
        part = ordered[band * ROWS : (band + 1) * ROWS].astype(jnp.bfloat16)
        for tile in range(tiles):
            out_ref[tile, band] = part


def make_table(first_run, lists_ref, keys, table, table_s, sem):
    length = lists_ref.shape[2]
    for r in range(GROUP):
        part = lists_ref[first_run + r].astype(jnp.float32)
        keys[r : r + 1, :] = part[CH : CH + 1, :128]
    starts = keys[...]
    lane = lax.broadcasted_iota(jnp.int32, (GROUP, 128), 1)
    sizes = jnp.where(lane < BLOCKS, pltpu.roll(starts, 127, 1) - starts, 0.0)
    earlier = lax.broadcasted_iota(jnp.int32, (GROUP, GROUP), 0) > lax.broadcasted_iota(
        jnp.int32, (GROUP, GROUP), 1
    )
    targets = jnp.dot(
        earlier.astype(jnp.float32).astype(jnp.bfloat16),
        sizes.astype(jnp.bfloat16),
        preferred_element_type=jnp.float32,
    )
    run = lax.broadcasted_iota(jnp.int32, (GROUP, 128), 0)
    table[:GROUP, :] = starts.astype(jnp.int32) + run * length
    table[GROUP : 2 * GROUP, :] = jnp.minimum(targets, float(LARGE)).astype(jnp.int32)
    widest = jnp.max(sizes, axis=0, keepdims=True)
    total = jnp.sum(sizes, axis=0, keepdims=True)
    last = lax.broadcasted_iota(jnp.int32, (8, 128), 0)
    table[2 * GROUP :, :] = jnp.where(last == 0, widest, total).astype(jnp.int32)
    copy = pltpu.make_async_copy(table, table_s, sem)
    copy.start()
    return copy


def turn_runs(first_run, lists_ref, flat):
    length = lists_ref.shape[2]
    for r in range(GROUP):
        part = lists_ref[first_run + r].astype(jnp.float32)
        for first in range(0, length, 128):
            at = r * length + first
            flat[at : at + 128, :ROWS] = jnp.transpose(part[:, first : first + 128])


def turned(first, width, packed):
    return jnp.concatenate(
        [jnp.transpose(packed[pl.ds(first + k, 128), :])[:ROWS] for k in range(0, width, 128)],
        axis=1,
    )


def products(part, size):
    width = part.shape[1]
    step = lax.broadcasted_iota(jnp.int32, (BLOCK, width), 0).astype(jnp.float32)
    step = step.astype(jnp.bfloat16)
    place = lax.broadcasted_iota(jnp.int32, (1, width), 1)
    one = jnp.ones((), jnp.bfloat16)
    none = jnp.zeros((), jnp.bfloat16)

    def spread(row):
        return jnp.broadcast_to(row, (BLOCK, width)).astype(jnp.bfloat16)

    hit = spread(jnp.where(place < size, part[CH + 1 : CH + 2], -1.0)) == step
    left = [jnp.where(hit, one, none)]
    left += [jnp.where(hit, spread(part[c : c + 1]), none) for c in range(CH)]
    left = jnp.concatenate(left, axis=0)
    for half in range(NG // HALF):
        low = spread(jnp.where(part[CH + 2 : CH + 3] == float(half), part[CH + 3 : CH + 4], -1.0))
        right = [
            jnp.where(low == step + jnp.bfloat16(j), one, none) for j in range(0, HALF, BLOCK)
        ]
        yield pl.ds(half * HALF, HALF), contract_last(left, jnp.concatenate(right, axis=0))


def block_rows(b):
    return pl.ds(pl.multiple_of(b * BLOCK, BLOCK), BLOCK)


def add_blocks(table_s, flat, buffers, later, packed, total, emit):
    sides = BLOCKS // SIDE

    def merge(i, q):
        b = jnp.minimum(i, sides - 1) * SIDE + q
        for r in range(GROUP):
            buffers[q][pl.ds(table_s[GROUP + r, b], COPY), :] = flat[pl.ds(table_s[r, b], COPY), :]
        later[q] = turned(0, LARGE, buffers[q])

    def fast(i, width):
        parts = [later[q, :, :width] for q in range(SIDE)]
        for q in range(SIDE):
            merge(i + 1, q)
            b = i * SIDE + q
            for lanes, sums in products(parts[q], table_s[2 * GROUP + 1, b]):
                emit(b, lanes, sums)

    def slow(b):
        def run(r, target):
            source = table_s[r, b]
            count = table_s[r, b + 1] - source

            def piece(k, _):
                packed[pl.ds(target + 8 * k, 8), :] = flat[pl.ds(source + 8 * k, 8), :]
                return 0

            lax.fori_loop(0, (count + 7) // 8, piece, 0)
            return target + count

        lax.fori_loop(0, GROUP, run, 0)
        total[...] = jnp.zeros_like(total)
        size = table_s[2 * GROUP + 1, b]

        def piece(k, _):
            first = pl.multiple_of(k * LARGE, LARGE)
            for lanes, sums in products(turned(first, LARGE, packed), size - first):
                total[:, lanes] += sums
            return 0

        lax.fori_loop(0, (size + LARGE - 1) // LARGE, piece, 0)
        for half in range(NG // HALF):
            lanes = pl.ds(half * HALF, HALF)
            emit(b, lanes, total[:, lanes])

    def side(i, _):
        b = i * SIDE
        widest = table_s[2 * GROUP, b]
        largest = table_s[2 * GROUP + 1, b]
        for q in range(1, SIDE):
            widest = jnp.maximum(widest, table_s[2 * GROUP, b + q])
            largest = jnp.maximum(largest, table_s[2 * GROUP + 1, b + q])
        plain = widest <= COPY
        least = -1
        for width in WIDTHS:

            @pl.when(plain & (largest > least) & (largest <= width))
            def _(width=width):
                fast(i, width)

            least = width

        @pl.when(jnp.logical_not(plain) | (largest > LARGE))
        def _():
            for q in range(SIDE):
                merge(i + 1, q)
            lax.fori_loop(0, SIDE, lambda q, _: (slow(b + q), 0)[1], 0)

        return 0

    for q in range(SIDE):
        merge(jnp.int32(0), q)
    lax.fori_loop(0, sides, side, 0)


def grid_kernel(
    scale, row_block, lists_ref, out_ref, planes, flat, packed, keys, table, twice, total, result,
    table_s, sem, out_sems, *rest
):
    runs = lists_ref.shape[0]
    alone = runs == GROUP
    later, *buffers = rest[: SIDE + 1]
    grid = rest[SIDE + 1] if not alone else None

    def finish(sums, rows, lanes):
        inverse = 1.0 / jnp.maximum(sums(0), 1.0)
        for c in range(CH):
            planes[c, rows, lanes] = (sums(c + 1) * inverse).astype(jnp.bfloat16)

    def emit(b, lanes, sums):
        rows = block_rows(b)
        if alone:
            finish(lambda c: sums[c * BLOCK : (c + 1) * BLOCK], rows, lanes)
        else:
            for c in range(CH + 1):
                grid[c, rows, lanes] += sums[c * BLOCK : (c + 1) * BLOCK]

    def group(g, _):
        copy = make_table(g * GROUP, lists_ref, keys, table, table_s, sem)
        turn_runs(g * GROUP, lists_ref, flat)
        copy.wait()
        add_blocks(table_s, flat, buffers, later, packed, total, emit)
        return 0

    if alone:
        group(0, 0)
    else:
        grid[...] = jnp.zeros_like(grid)
        lax.fori_loop(0, runs // GROUP, group, 0)

        def divide(b, _):
            rows = block_rows(b)
            finish(lambda c: grid[c, rows, :], rows, pl.ds(0, NG))
            return 0

        lax.fori_loop(0, BLOCKS, divide, 0)

    first_row = pl.multiple_of(lax.axis_index("tile") * row_block, row_block)

    def sent(f):
        return pltpu.make_async_copy(result.at[f], out_ref.at[f], out_sems.at[f])

    def frequency(f, slot):
        for part, p in enumerate((f, FB + f)):
            for i in range(0, NG, TURN):
                for j in range(0, NG, TURN):
                    across = jnp.transpose(planes[p, j : j + TURN, i : i + TURN])
                    twice[slot, part * NG + i : part * NG + i + TURN, j : j + TURN] = (
                        planes[p, i : i + TURN, j : j + TURN] + across
                    )
        real = twice[slot, pl.ds(first_row, row_block), :]
        imag = twice[slot, pl.ds(NG + first_row, row_block), :]
        own = jnp.concatenate(
            [jnp.concatenate([real, -imag], axis=1), jnp.concatenate([imag, real], axis=1)], axis=0
        )
        for half in range(NG // HALF):
            lanes = slice(half * HALF, (half + 1) * HALF)
            both = jnp.dot(own, twice[slot, :, lanes], preferred_element_type=jnp.float32)
            both = both * (0.25 * scale)
            result[f, 0, :, lanes] = both[:row_block]
            result[f, 1, :, lanes] = both[row_block:]
        sent(f).start()

    def some(i, _):
        for q in range(BESIDE):
            frequency(i * BESIDE + q, q)
        return 0

    lax.fori_loop(0, FB // BESIDE, some, 0)
    for f in range(FB):
        sent(f).wait()


def whole(space=pltpu.VMEM):
    return pl.BlockSpec(memory_space=space)


def per_device(raw_traces, bin_owner, bin_offset):
    band_count = lax.axis_size("band")
    tile_count = lax.axis_size("tile")
    length = bin_offset.shape[1]
    count = raw_traces.shape[1]
    cells_dev = NG * NG // tile_count
    row_block = NG // tile_count
    runs = band_count * tile_count
    params = pltpu.CompilerParams(vmem_limit_bytes=VMEM)

    own = pl.pallas_call(
        functools.partial(run_kernel, cells_dev),
        out_shape=jax.ShapeDtypeStruct((tile_count, band_count, ROWS, count), jnp.bfloat16),
        in_specs=[whole()] * 4,
        out_specs=whole(),
        compiler_params=params,
        name="own_run",
    )(
        jnp.asarray(twiddle_rows(band_count)),
        raw_traces,
        bin_owner.reshape(1, length),
        bin_offset,
    )
    lists = lax.all_to_all(
        own.reshape(runs, ROWS, count), ("tile", "band"), split_axis=0, concat_axis=0, tiled=True
    )

    traces = GROUP * count
    scratch = [
        pltpu.VMEM((CH, NG, NG), jnp.bfloat16),
        pltpu.VMEM((traces + COPY, 128), jnp.float32),
        pltpu.VMEM((traces + LARGE, 128), jnp.float32),
        pltpu.VMEM((GROUP, 128), jnp.float32),
        pltpu.VMEM((2 * GROUP + 8, 128), jnp.int32),
        pltpu.VMEM((BESIDE, 2 * NG, NG), jnp.bfloat16),
        pltpu.VMEM(((CH + 1) * BLOCK, NG), jnp.float32),
        pltpu.VMEM((FB, 2, row_block, NG), jnp.float32),
        pltpu.SMEM((2 * GROUP + 8, 128), jnp.int32),
        pltpu.SemaphoreType.DMA,
        pltpu.SemaphoreType.DMA((FB,)),
    ]
    scratch.append(pltpu.VMEM((SIDE, ROWS, LARGE), jnp.float32))
    scratch += [pltpu.VMEM((LARGE + COPY, 128), jnp.float32)] * SIDE
    if runs != GROUP:
        scratch.append(pltpu.VMEM((CH + 1, NG, NG), jnp.float32))
    return pl.pallas_call(
        functools.partial(grid_kernel, 1.0 / math.sqrt(NG), row_block),
        out_shape=jax.ShapeDtypeStruct((FB, 2, row_block, NG), jnp.float32),
        in_specs=[whole()],
        out_specs=whole(pl.ANY),
        scratch_shapes=scratch,
        compiler_params=params,
        name="grid",
    )(lists)


def solution(mesh):
    return jax.shard_map(
        per_device,
        mesh=mesh,
        in_specs=(P("tile", "band", None), P("tile", None, None), P("tile", None)),
        out_specs=P("band", None, "tile", None),
        check_vma=False,
    )
```

```python
import functools
import math

import jax
import jax.numpy as jnp
import ml_dtypes
import numpy as np
from jax import lax
from jax.experimental import pallas as pl
from jax.experimental.pallas import tpu as pltpu
from jax.sharding import PartitionSpec as P

NG = 512
NT = 2048
FB = 10
CH = 2 * FB
ROWS = 24
BLOCK = 16
BLOCKS = NG // BLOCK
GROUP = 32
COPY = 32
NARROW = 16
WIDTHS = (256, 512, 640)
LARGE = WIDTHS[-1]
BESIDE = 5
SIDE = 4
TURN = 128
HALF = 256
VMEM = 56 * 1024 * 1024


def twiddle_rows(band_count):
    time_index = np.arange(NT)[None, None, :]
    freq_index = np.arange(band_count * FB).reshape(band_count, FB, 1) + 1
    angle = (time_index * freq_index % NT) * (2.0 * math.pi / NT)
    norm = 1.0 / math.sqrt(NT)
    table = np.zeros((band_count, ROWS, NT), np.float64)
    table[:, :FB] = np.cos(angle) * norm
    table[:, FB:CH] = -np.sin(angle) * norm
    return table.reshape(band_count * ROWS, NT).astype(ml_dtypes.bfloat16)


def contract_last(left, right):
    return lax.dot_general(
        left, right, (((1,), (1,)), ((), ())), preferred_element_type=jnp.float32
    )


def run_kernel(cells_dev, twiddle_ref, traces_ref, owner_ref, offset_ref, out_ref):
    tiles, bands, _, count = out_ref.shape
    lanes = pl.ds(pl.multiple_of(lax.axis_index("band") * count, count), count)
    cell = owner_ref[:, lanes] * cells_dev + offset_ref[:, lanes]
    order = cell * count + lax.broadcasted_iota(jnp.int32, (1, count), 1)
    rank = jnp.zeros((1, count), jnp.int32)
    starts = jnp.zeros((1, count), jnp.int32)
    limit = lax.broadcasted_iota(jnp.int32, (1, count), 1) * (BLOCK * NG * count)
    limit = jnp.minimum(limit, NG * NG * count)
    for first in range(0, count, 128):
        column = jnp.transpose(jnp.broadcast_to(order[:, first : first + 128], (128, 128)))
        column = jnp.concatenate([column] * (count // 128), axis=1)
        rank += jnp.sum((column < order).astype(jnp.int32), axis=0, keepdims=True)
        starts += jnp.sum((column < limit).astype(jnp.int32), axis=0, keepdims=True)
    target = lax.broadcasted_iota(jnp.int32, (count, count), 0)
    permute = (target == rank).astype(jnp.float32).astype(jnp.bfloat16)
    source = cell // NG
    receiver = cell % NG
    row = lax.broadcasted_iota(jnp.int32, (bands * ROWS, count), 0) % ROWS
    digits = jnp.where(row == CH + 1, source % BLOCK, 0)
    digits = jnp.where(row == CH + 2, receiver // HALF, digits)
    digits = jnp.where(row == CH + 3, receiver % HALF, digits)
    spectra = contract_last(twiddle_ref[...], traces_ref[0])
    packed = (spectra + digits.astype(jnp.float32)).astype(jnp.bfloat16)
    ordered = contract_last(packed, permute) + jnp.where(row == CH, starts, 0).astype(jnp.float32)
    for band in range(bands):
        part = ordered[band * ROWS : (band + 1) * ROWS].astype(jnp.bfloat16)
        for tile in range(tiles):
            out_ref[tile, band] = part


def make_table(first_run, lists_ref, keys, table, table_s, sem):
    length = lists_ref.shape[2]
    for r in range(GROUP):
        part = lists_ref[first_run + r].astype(jnp.float32)
        keys[r : r + 1, :] = part[CH : CH + 1, :128]
    starts = keys[...]
    lane = lax.broadcasted_iota(jnp.int32, (GROUP, 128), 1)
    sizes = jnp.where(lane < BLOCKS, pltpu.roll(starts, 127, 1) - starts, 0.0)
    earlier = lax.broadcasted_iota(jnp.int32, (GROUP, GROUP), 0) > lax.broadcasted_iota(
        jnp.int32, (GROUP, GROUP), 1
    )
    targets = jnp.dot(
        earlier.astype(jnp.float32).astype(jnp.bfloat16),
        sizes.astype(jnp.bfloat16),
        preferred_element_type=jnp.float32,
    )
    run = lax.broadcasted_iota(jnp.int32, (GROUP, 128), 0)
    table[:GROUP, :] = starts.astype(jnp.int32) + run * length
    table[GROUP : 2 * GROUP, :] = jnp.minimum(targets, float(LARGE)).astype(jnp.int32)
    widest = jnp.max(sizes, axis=0, keepdims=True)
    total = jnp.sum(sizes, axis=0, keepdims=True)
    last = lax.broadcasted_iota(jnp.int32, (8, 128), 0)
    table[2 * GROUP :, :] = jnp.where(last == 0, widest, total).astype(jnp.int32)
    copy = pltpu.make_async_copy(table, table_s, sem)
    copy.start()
    return copy


def turn_runs(first_run, lists_ref, flat):
    length = lists_ref.shape[2]
    for r in range(GROUP):
        part = lists_ref[first_run + r].astype(jnp.float32)
        for first in range(0, length, 128):
            at = r * length + first
            flat[at : at + 128, :ROWS] = jnp.transpose(part[:, first : first + 128])


def turned(first, width, packed):
    return jnp.concatenate(
        [jnp.transpose(packed[pl.ds(first + k, 128), :])[:ROWS] for k in range(0, width, 128)],
        axis=1,
    )


def products(part, size):
    width = part.shape[1]
    step = lax.broadcasted_iota(jnp.int32, (BLOCK, width), 0).astype(jnp.float32)
    step = step.astype(jnp.bfloat16)
    place = lax.broadcasted_iota(jnp.int32, (1, width), 1)
    one = jnp.ones((), jnp.bfloat16)
    none = jnp.zeros((), jnp.bfloat16)

    def spread(row):
        return jnp.broadcast_to(row, (BLOCK, width)).astype(jnp.bfloat16)

    hit = spread(jnp.where(place < size, part[CH + 1 : CH + 2], -1.0)) == step
    left = [jnp.where(hit, one, none)]
    left += [jnp.where(hit, spread(part[c : c + 1]), none) for c in range(CH)]
    left = jnp.concatenate(left, axis=0)
    for half in range(NG // HALF):
        low = spread(jnp.where(part[CH + 2 : CH + 3] == float(half), part[CH + 3 : CH + 4], -1.0))
        right = [
            jnp.where(low == step + jnp.bfloat16(j), one, none) for j in range(0, HALF, BLOCK)
        ]
        yield pl.ds(half * HALF, HALF), contract_last(left, jnp.concatenate(right, axis=0))


def block_rows(b):
    return pl.ds(pl.multiple_of(b * BLOCK, BLOCK), BLOCK)


def add_blocks(table_s, flat, buffers, later, packed, total, emit):
    sides = BLOCKS // SIDE

    def merge(i, q, rows):
        b = jnp.minimum(i, sides - 1) * SIDE + q
        for r in range(GROUP):
            buffers[q][pl.ds(table_s[GROUP + r, b], rows), :] = flat[pl.ds(table_s[r, b], rows), :]
        later[q] = turned(0, LARGE, buffers[q])

    def most(i, row):
        b = jnp.minimum(i, sides - 1) * SIDE
        found = table_s[row, b]
        for q in range(1, SIDE):
            found = jnp.maximum(found, table_s[row, b + q])
        return found

    def fast(i, width, rows):
        parts = [later[q, :, :width] for q in range(SIDE)]
        for q in range(SIDE):
            merge(i + 1, q, rows)
            b = i * SIDE + q
            for lanes, sums in products(parts[q], table_s[2 * GROUP + 1, b]):
                emit(b, lanes, sums)

    def slow(b):
        def run(r, target):
            source = table_s[r, b]
            count = table_s[r, b + 1] - source

            def piece(k, _):
                packed[pl.ds(target + 8 * k, 8), :] = flat[pl.ds(source + 8 * k, 8), :]
                return 0

            lax.fori_loop(0, (count + 7) // 8, piece, 0)
            return target + count

        lax.fori_loop(0, GROUP, run, 0)
        total[...] = jnp.zeros_like(total)
        size = table_s[2 * GROUP + 1, b]

        def piece(k, _):
            first = pl.multiple_of(k * LARGE, LARGE)
            for lanes, sums in products(turned(first, LARGE, packed), size - first):
                total[:, lanes] += sums
            return 0

        lax.fori_loop(0, (size + LARGE - 1) // LARGE, piece, 0)
        for half in range(NG // HALF):
            lanes = pl.ds(half * HALF, HALF)
            emit(b, lanes, total[:, lanes])

    def side(i, _):
        largest = most(i, 2 * GROUP + 1)
        plain = (most(i, 2 * GROUP) <= COPY) & (largest <= LARGE)
        ahead = most(i + 1, 2 * GROUP) <= NARROW
        least = -1
        for width in WIDTHS:
            for rows, fits in ((NARROW, ahead), (COPY, jnp.logical_not(ahead))):

                @pl.when(plain & (largest > least) & (largest <= width) & fits)
                def _(width=width, rows=rows):
                    fast(i, width, rows)

            least = width

        @pl.when(jnp.logical_not(plain))
        def _():
            for q in range(SIDE):
                merge(i + 1, q, COPY)
            lax.fori_loop(0, SIDE, lambda q, _: (slow(i * SIDE + q), 0)[1], 0)

        return 0

    for q in range(SIDE):
        merge(jnp.int32(0), q, COPY)
    lax.fori_loop(0, sides, side, 0)


def grid_kernel(
    scale, row_block, lists_ref, out_ref, planes, flat, packed, keys, table, twice, total, result,
    table_s, sem, out_sems, *rest
):
    runs = lists_ref.shape[0]
    alone = runs == GROUP
    later, *buffers = rest[: SIDE + 1]
    grid = rest[SIDE + 1] if not alone else None

    def finish(sums, rows, lanes):
        inverse = 1.0 / jnp.maximum(sums(0), 1.0)
        for c in range(CH):
            planes[c, rows, lanes] = (sums(c + 1) * inverse).astype(jnp.bfloat16)

    def emit(b, lanes, sums):
        rows = block_rows(b)
        if alone:
            finish(lambda c: sums[c * BLOCK : (c + 1) * BLOCK], rows, lanes)
        else:
            for c in range(CH + 1):
                grid[c, rows, lanes] += sums[c * BLOCK : (c + 1) * BLOCK]

    def group(g, _):
        copy = make_table(g * GROUP, lists_ref, keys, table, table_s, sem)
        turn_runs(g * GROUP, lists_ref, flat)
        copy.wait()
        add_blocks(table_s, flat, buffers, later, packed, total, emit)
        return 0

    if alone:
        group(0, 0)
    else:
        grid[...] = jnp.zeros_like(grid)
        lax.fori_loop(0, runs // GROUP, group, 0)

        def divide(b, _):
            rows = block_rows(b)
            finish(lambda c: grid[c, rows, :], rows, pl.ds(0, NG))
            return 0

        lax.fori_loop(0, BLOCKS, divide, 0)

    first_row = pl.multiple_of(lax.axis_index("tile") * row_block, row_block)

    def sent(f):
        return pltpu.make_async_copy(result.at[f], out_ref.at[f], out_sems.at[f])

    def frequency(f, slot):
        for part, p in enumerate((f, FB + f)):
            for i in range(0, NG, TURN):
                for j in range(0, NG, TURN):
                    across = jnp.transpose(planes[p, j : j + TURN, i : i + TURN])
                    twice[slot, part * NG + i : part * NG + i + TURN, j : j + TURN] = (
                        planes[p, i : i + TURN, j : j + TURN] + across
                    )
        real = twice[slot, pl.ds(first_row, row_block), :]
        imag = twice[slot, pl.ds(NG + first_row, row_block), :]
        own = jnp.concatenate(
            [jnp.concatenate([real, -imag], axis=1), jnp.concatenate([imag, real], axis=1)], axis=0
        )
        for half in range(NG // HALF):
            lanes = slice(half * HALF, (half + 1) * HALF)
            both = jnp.dot(own, twice[slot, :, lanes], preferred_element_type=jnp.float32)
            both = both * (0.25 * scale)
            result[f, 0, :, lanes] = both[:row_block]
            result[f, 1, :, lanes] = both[row_block:]
        sent(f).start()

    def some(i, _):
        for q in range(BESIDE):
            frequency(i * BESIDE + q, q)
        return 0

    lax.fori_loop(0, FB // BESIDE, some, 0)
    for f in range(FB):
        sent(f).wait()


def whole(space=pltpu.VMEM):
    return pl.BlockSpec(memory_space=space)


def per_device(raw_traces, bin_owner, bin_offset):
    band_count = lax.axis_size("band")
    tile_count = lax.axis_size("tile")
    length = bin_offset.shape[1]
    count = raw_traces.shape[1]
    cells_dev = NG * NG // tile_count
    row_block = NG // tile_count
    runs = band_count * tile_count
    params = pltpu.CompilerParams(vmem_limit_bytes=VMEM)

    own = pl.pallas_call(
        functools.partial(run_kernel, cells_dev),
        out_shape=jax.ShapeDtypeStruct((tile_count, band_count, ROWS, count), jnp.bfloat16),
        in_specs=[whole()] * 4,
        out_specs=whole(),
        compiler_params=params,
        name="own_run",
    )(
        jnp.asarray(twiddle_rows(band_count)),
        raw_traces,
        bin_owner.reshape(1, length),
        bin_offset,
    )
    lists = lax.all_to_all(
        own.reshape(runs, ROWS, count), ("tile", "band"), split_axis=0, concat_axis=0, tiled=True
    )

    traces = GROUP * count
    scratch = [
        pltpu.VMEM((CH, NG, NG), jnp.bfloat16),
        pltpu.VMEM((traces + COPY, 128), jnp.float32),
        pltpu.VMEM((traces + LARGE, 128), jnp.float32),
        pltpu.VMEM((GROUP, 128), jnp.float32),
        pltpu.VMEM((2 * GROUP + 8, 128), jnp.int32),
        pltpu.VMEM((BESIDE, 2 * NG, NG), jnp.bfloat16),
        pltpu.VMEM(((CH + 1) * BLOCK, NG), jnp.float32),
        pltpu.VMEM((FB, 2, row_block, NG), jnp.float32),
        pltpu.SMEM((2 * GROUP + 8, 128), jnp.int32),
        pltpu.SemaphoreType.DMA,
        pltpu.SemaphoreType.DMA((FB,)),
    ]
    scratch.append(pltpu.VMEM((SIDE, ROWS, LARGE), jnp.float32))
    scratch += [pltpu.VMEM((LARGE + COPY, 128), jnp.float32)] * SIDE
    if runs != GROUP:
        scratch.append(pltpu.VMEM((CH + 1, NG, NG), jnp.float32))
    return pl.pallas_call(
        functools.partial(grid_kernel, 1.0 / math.sqrt(NG), row_block),
        out_shape=jax.ShapeDtypeStruct((FB, 2, row_block, NG), jnp.float32),
        in_specs=[whole()],
        out_specs=whole(pl.ANY),
        scratch_shapes=scratch,
        compiler_params=params,
        name="grid",
    )(lists)


def solution(mesh):
    return jax.shard_map(
        per_device,
        mesh=mesh,
        in_specs=(P("tile", "band", None), P("tile", None, None), P("tile", None)),
        out_specs=P("band", None, "tile", None),
        check_vma=False,
    )
```

```python
import functools
import math

import jax
import jax.numpy as jnp
import ml_dtypes
import numpy as np
from jax import lax
from jax.experimental import pallas as pl
from jax.experimental.pallas import tpu as pltpu
from jax.sharding import PartitionSpec as P

NG = 512
NT = 2048
FB = 10
CH = 2 * FB
ROWS = 24
BLOCK = 16
BLOCKS = NG // BLOCK
GROUP = 32
TURNED = 8
COPY = 32
WIDTHS = (256, 512, 640)
LARGE = WIDTHS[-1]
BESIDE = 2
SIDE = 4
TURN = 128
HALF = 256
VMEM = 56 * 1024 * 1024


def twiddle_rows(band_count):
    time_index = np.arange(NT)[None, None, :]
    freq_index = np.arange(band_count * FB).reshape(band_count, FB, 1) + 1
    angle = (time_index * freq_index % NT) * (2.0 * math.pi / NT)
    norm = 1.0 / math.sqrt(NT)
    table = np.zeros((band_count, ROWS, NT), np.float64)
    table[:, :FB] = np.cos(angle) * norm
    table[:, FB:CH] = -np.sin(angle) * norm
    return table.reshape(band_count * ROWS, NT).astype(ml_dtypes.bfloat16)


def contract_last(left, right):
    return lax.dot_general(
        left, right, (((1,), (1,)), ((), ())), preferred_element_type=jnp.float32
    )


def run_kernel(cells_dev, twiddle_ref, traces_ref, owner_ref, offset_ref, out_ref):
    tiles, bands, _, count = out_ref.shape
    lanes = pl.ds(pl.multiple_of(lax.axis_index("band") * count, count), count)
    cell = owner_ref[:, lanes] * cells_dev + offset_ref[:, lanes]
    order = cell * count + lax.broadcasted_iota(jnp.int32, (1, count), 1)
    rank = jnp.zeros((1, count), jnp.int32)
    starts = jnp.zeros((1, count), jnp.int32)
    limit = lax.broadcasted_iota(jnp.int32, (1, count), 1) * (BLOCK * NG * count)
    limit = jnp.minimum(limit, NG * NG * count)
    for first in range(0, count, 128):
        column = jnp.transpose(jnp.broadcast_to(order[:, first : first + 128], (128, 128)))
        column = jnp.concatenate([column] * (count // 128), axis=1)
        rank += jnp.sum((column < order).astype(jnp.int32), axis=0, keepdims=True)
        starts += jnp.sum((column < limit).astype(jnp.int32), axis=0, keepdims=True)
    target = lax.broadcasted_iota(jnp.int32, (count, count), 0)
    permute = (target == rank).astype(jnp.float32).astype(jnp.bfloat16)
    source = cell // NG
    receiver = cell % NG
    row = lax.broadcasted_iota(jnp.int32, (bands * ROWS, count), 0) % ROWS
    digits = jnp.where(row == CH + 1, source % BLOCK, 0)
    digits = jnp.where(row == CH + 2, receiver // HALF, digits)
    digits = jnp.where(row == CH + 3, receiver % HALF, digits)
    spectra = contract_last(twiddle_ref[...], traces_ref[0])
    packed = (spectra + digits.astype(jnp.float32)).astype(jnp.bfloat16)
    ordered = contract_last(packed, permute) + jnp.where(row == CH, starts, 0).astype(jnp.float32)
    for band in range(bands):
        part = ordered[band * ROWS : (band + 1) * ROWS].astype(jnp.bfloat16)
        for tile in range(tiles):
            out_ref[tile, band] = part


def make_table(first_run, lists_ref, keys, table, table_s, sem):
    length = lists_ref.shape[2]
    for r in range(GROUP):
        part = lists_ref[first_run + r].astype(jnp.float32)
        keys[r : r + 1, :] = part[CH : CH + 1, :128]
    starts = keys[...]
    lane = lax.broadcasted_iota(jnp.int32, (GROUP, 128), 1)
    sizes = jnp.where(lane < BLOCKS, pltpu.roll(starts, 127, 1) - starts, 0.0)
    earlier = lax.broadcasted_iota(jnp.int32, (GROUP, GROUP), 0) > lax.broadcasted_iota(
        jnp.int32, (GROUP, GROUP), 1
    )
    targets = jnp.dot(
        earlier.astype(jnp.float32).astype(jnp.bfloat16),
        sizes.astype(jnp.bfloat16),
        preferred_element_type=jnp.float32,
    )
    run = lax.broadcasted_iota(jnp.int32, (GROUP, 128), 0)
    table[:GROUP, :] = starts.astype(jnp.int32) + run * length
    table[GROUP : 2 * GROUP, :] = jnp.minimum(targets, float(LARGE)).astype(jnp.int32)
    widest = jnp.max(sizes, axis=0, keepdims=True)
    total = jnp.sum(sizes, axis=0, keepdims=True)
    last = lax.broadcasted_iota(jnp.int32, (8, 128), 0)
    table[2 * GROUP :, :] = jnp.where(last == 0, widest, total).astype(jnp.int32)
    copy = pltpu.make_async_copy(table, table_s, sem)
    copy.start()
    return copy


def turn_runs(first_run, lists_ref, flat):
    length = lists_ref.shape[2]

    def some(i, _):
        for k in range(TURNED):
            r = i * TURNED + k
            part = lists_ref[first_run + r].astype(jnp.float32)
            for first in range(0, length, 128):
                at = pl.multiple_of(r * length + first, 128)
                flat[pl.ds(at, 128), :ROWS] = jnp.transpose(part[:, first : first + 128])
        return 0

    lax.fori_loop(0, GROUP // TURNED, some, 0)


def turned(first, width, packed):
    return jnp.concatenate(
        [jnp.transpose(packed[pl.ds(first + k, 128), :])[:ROWS] for k in range(0, width, 128)],
        axis=1,
    )


def products(part, size):
    width = part.shape[1]
    step = lax.broadcasted_iota(jnp.int32, (BLOCK, width), 0).astype(jnp.float32)
    step = step.astype(jnp.bfloat16)
    place = lax.broadcasted_iota(jnp.int32, (1, width), 1)
    one = jnp.ones((), jnp.bfloat16)
    none = jnp.zeros((), jnp.bfloat16)

    def spread(row):
        return jnp.broadcast_to(row, (BLOCK, width)).astype(jnp.bfloat16)

    hit = spread(jnp.where(place < size, part[CH + 1 : CH + 2], -1.0)) == step
    left = [jnp.where(hit, one, none)]
    left += [jnp.where(hit, spread(part[c : c + 1]), none) for c in range(CH)]
    left = jnp.concatenate(left, axis=0)
    for half in range(NG // HALF):
        low = spread(jnp.where(part[CH + 2 : CH + 3] == float(half), part[CH + 3 : CH + 4], -1.0))
        right = [
            jnp.where(low == step + jnp.bfloat16(j), one, none) for j in range(0, HALF, BLOCK)
        ]
        yield pl.ds(half * HALF, HALF), contract_last(left, jnp.concatenate(right, axis=0))


def block_rows(b):
    return pl.ds(pl.multiple_of(b * BLOCK, BLOCK), BLOCK)


def add_blocks(table_s, flat, buffers, later, packed, total, emit):
    sides = BLOCKS // SIDE

    def merge(i, q):
        b = jnp.minimum(i, sides - 1) * SIDE + q
        for r in range(GROUP):
            buffers[q][pl.ds(table_s[GROUP + r, b], COPY), :] = flat[pl.ds(table_s[r, b], COPY), :]
        later[q] = turned(0, LARGE, buffers[q])

    def fast(i, width):
        parts = [later[q, :, :width] for q in range(SIDE)]
        for q in range(SIDE):
            merge(i + 1, q)
            b = i * SIDE + q
            for lanes, sums in products(parts[q], table_s[2 * GROUP + 1, b]):
                emit(b, lanes, sums)

    def slow(b):
        def run(r, target):
            source = table_s[r, b]
            count = table_s[r, b + 1] - source

            def piece(k, _):
                packed[pl.ds(target + 8 * k, 8), :] = flat[pl.ds(source + 8 * k, 8), :]
                return 0

            lax.fori_loop(0, (count + 7) // 8, piece, 0)
            return target + count

        lax.fori_loop(0, GROUP, run, 0)
        total[...] = jnp.zeros_like(total)
        size = table_s[2 * GROUP + 1, b]

        def piece(k, _):
            first = pl.multiple_of(k * LARGE, LARGE)
            for lanes, sums in products(turned(first, LARGE, packed), size - first):
                total[:, lanes] += sums
            return 0

        lax.fori_loop(0, (size + LARGE - 1) // LARGE, piece, 0)
        for half in range(NG // HALF):
            lanes = pl.ds(half * HALF, HALF)
            emit(b, lanes, total[:, lanes])

    def side(i, _):
        b = i * SIDE
        widest = table_s[2 * GROUP, b]
        largest = table_s[2 * GROUP + 1, b]
        for q in range(1, SIDE):
            widest = jnp.maximum(widest, table_s[2 * GROUP, b + q])
            largest = jnp.maximum(largest, table_s[2 * GROUP + 1, b + q])
        plain = widest <= COPY
        least = -1
        for width in WIDTHS:

            @pl.when(plain & (largest > least) & (largest <= width))
            def _(width=width):
                fast(i, width)

            least = width

        @pl.when(jnp.logical_not(plain) | (largest > LARGE))
        def _():
            for q in range(SIDE):
                merge(i + 1, q)
            lax.fori_loop(0, SIDE, lambda q, _: (slow(b + q), 0)[1], 0)

        return 0

    for q in range(SIDE):
        merge(jnp.int32(0), q)
    lax.fori_loop(0, sides, side, 0)


def grid_kernel(
    scale, row_block, lists_ref, out_ref, planes, flat, packed, keys, table, twice, total, result,
    table_s, sem, out_sems, *rest
):
    runs = lists_ref.shape[0]
    alone = runs == GROUP
    later, *buffers = rest[: SIDE + 1]
    grid = rest[SIDE + 1] if not alone else None

    def finish(sums, rows, lanes):
        inverse = 1.0 / jnp.maximum(sums(0), 1.0)
        for c in range(CH):
            planes[c, rows, lanes] = (sums(c + 1) * inverse).astype(jnp.bfloat16)

    def emit(b, lanes, sums):
        rows = block_rows(b)
        if alone:
            finish(lambda c: sums[c * BLOCK : (c + 1) * BLOCK], rows, lanes)
        else:
            for c in range(CH + 1):
                grid[c, rows, lanes] += sums[c * BLOCK : (c + 1) * BLOCK]

    def group(g, _):
        copy = make_table(g * GROUP, lists_ref, keys, table, table_s, sem)
        turn_runs(g * GROUP, lists_ref, flat)
        copy.wait()
        add_blocks(table_s, flat, buffers, later, packed, total, emit)
        return 0

    if alone:
        group(0, 0)
    else:
        grid[...] = jnp.zeros_like(grid)
        lax.fori_loop(0, runs // GROUP, group, 0)

        def divide(b, _):
            rows = block_rows(b)
            finish(lambda c: grid[c, rows, :], rows, pl.ds(0, NG))
            return 0

        lax.fori_loop(0, BLOCKS, divide, 0)

    first_row = pl.multiple_of(lax.axis_index("tile") * row_block, row_block)

    def sent(f):
        return pltpu.make_async_copy(result.at[f], out_ref.at[f], out_sems.at[f])

    def frequency(f, slot):
        for part, p in enumerate((f, FB + f)):
            for i in range(0, NG, TURN):
                for j in range(0, NG, TURN):
                    across = jnp.transpose(planes[p, j : j + TURN, i : i + TURN])
                    twice[slot, part * NG + i : part * NG + i + TURN, j : j + TURN] = (
                        planes[p, i : i + TURN, j : j + TURN] + across
                    )
        real = twice[slot, pl.ds(first_row, row_block), :]
        imag = twice[slot, pl.ds(NG + first_row, row_block), :]
        own = jnp.concatenate(
            [jnp.concatenate([real, -imag], axis=1), jnp.concatenate([imag, real], axis=1)], axis=0
        )
        for half in range(NG // HALF):
            lanes = slice(half * HALF, (half + 1) * HALF)
            both = jnp.dot(own, twice[slot, :, lanes], preferred_element_type=jnp.float32)
            both = both * (0.25 * scale)
            result[f, 0, :, lanes] = both[:row_block]
            result[f, 1, :, lanes] = both[row_block:]
        sent(f).start()

    def some(i, _):
        for q in range(BESIDE):
            frequency(i * BESIDE + q, q)
        return 0

    lax.fori_loop(0, FB // BESIDE, some, 0)
    for f in range(FB):
        sent(f).wait()


def whole(space=pltpu.VMEM):
    return pl.BlockSpec(memory_space=space)


def per_device(raw_traces, bin_owner, bin_offset):
    band_count = lax.axis_size("band")
    tile_count = lax.axis_size("tile")
    length = bin_offset.shape[1]
    count = raw_traces.shape[1]
    cells_dev = NG * NG // tile_count
    row_block = NG // tile_count
    runs = band_count * tile_count
    params = pltpu.CompilerParams(vmem_limit_bytes=VMEM)

    own = pl.pallas_call(
        functools.partial(run_kernel, cells_dev),
        out_shape=jax.ShapeDtypeStruct((tile_count, band_count, ROWS, count), jnp.bfloat16),
        in_specs=[whole()] * 4,
        out_specs=whole(),
        compiler_params=params,
        name="own_run",
    )(
        jnp.asarray(twiddle_rows(band_count)),
        raw_traces,
        bin_owner.reshape(1, length),
        bin_offset,
    )
    lists = lax.all_to_all(
        own.reshape(runs, ROWS, count), ("tile", "band"), split_axis=0, concat_axis=0, tiled=True
    )

    traces = GROUP * count
    scratch = [
        pltpu.VMEM((CH, NG, NG), jnp.bfloat16),
        pltpu.VMEM((traces + COPY, 128), jnp.float32),
        pltpu.VMEM((traces + LARGE, 128), jnp.float32),
        pltpu.VMEM((GROUP, 128), jnp.float32),
        pltpu.VMEM((2 * GROUP + 8, 128), jnp.int32),
        pltpu.VMEM((BESIDE, 2 * NG, NG), jnp.bfloat16),
        pltpu.VMEM(((CH + 1) * BLOCK, NG), jnp.float32),
        pltpu.VMEM((FB, 2, row_block, NG), jnp.float32),
        pltpu.SMEM((2 * GROUP + 8, 128), jnp.int32),
        pltpu.SemaphoreType.DMA,
        pltpu.SemaphoreType.DMA((FB,)),
    ]
    scratch.append(pltpu.VMEM((SIDE, ROWS, LARGE), jnp.float32))
    scratch += [pltpu.VMEM((LARGE + COPY, 128), jnp.float32)] * SIDE
    if runs != GROUP:
        scratch.append(pltpu.VMEM((CH + 1, NG, NG), jnp.float32))
    return pl.pallas_call(
        functools.partial(grid_kernel, 1.0 / math.sqrt(NG), row_block),
        out_shape=jax.ShapeDtypeStruct((FB, 2, row_block, NG), jnp.float32),
        in_specs=[whole()],
        out_specs=whole(pl.ANY),
        scratch_shapes=scratch,
        compiler_params=params,
        name="grid",
    )(lists)


def solution(mesh):
    return jax.shard_map(
        per_device,
        mesh=mesh,
        in_specs=(P("tile", "band", None), P("tile", None, None), P("tile", None)),
        out_specs=P("band", None, "tile", None),
        check_vma=False,
    )
```

```python
import functools
import math

import jax
import jax.numpy as jnp
import ml_dtypes
import numpy as np
from jax import lax
from jax.experimental import pallas as pl
from jax.experimental.pallas import tpu as pltpu
from jax.sharding import PartitionSpec as P

NG = 512
NT = 2048
FB = 10
CH = 2 * FB
ROWS = 24
BLOCK = 16
BLOCKS = NG // BLOCK
GROUP = 32
COPY = 32
WIDTHS = (256, 512, 640)
LARGE = WIDTHS[-1]
BESIDE = 5
SIDE = 4
TURN = 128
HALF = 256
VMEM = 56 * 1024 * 1024


def twiddle_rows(band_count):
    time_index = np.arange(NT)[None, None, :]
    freq_index = np.arange(band_count * FB).reshape(band_count, FB, 1) + 1
    angle = (time_index * freq_index % NT) * (2.0 * math.pi / NT)
    norm = 1.0 / math.sqrt(NT)
    table = np.zeros((band_count, ROWS, NT), np.float64)
    table[:, :FB] = np.cos(angle) * norm
    table[:, FB:CH] = -np.sin(angle) * norm
    return table.reshape(band_count * ROWS, NT).astype(ml_dtypes.bfloat16)


def contract_last(left, right):
    return lax.dot_general(
        left, right, (((1,), (1,)), ((), ())), preferred_element_type=jnp.float32
    )


def run_kernel(cells_dev, twiddle_ref, traces_ref, owner_ref, offset_ref, out_ref):
    tiles, bands, _, count = out_ref.shape
    lanes = pl.ds(pl.multiple_of(lax.axis_index("band") * count, count), count)
    cell = owner_ref[:, lanes] * cells_dev + offset_ref[:, lanes]
    order = cell * count + lax.broadcasted_iota(jnp.int32, (1, count), 1)
    rank = jnp.zeros((1, count), jnp.int32)
    starts = jnp.zeros((1, count), jnp.int32)
    limit = lax.broadcasted_iota(jnp.int32, (1, count), 1) * (BLOCK * NG * count)
    limit = jnp.minimum(limit, NG * NG * count)
    for first in range(0, count, 128):
        column = jnp.transpose(jnp.broadcast_to(order[:, first : first + 128], (128, 128)))
        column = jnp.concatenate([column] * (count // 128), axis=1)
        rank += jnp.sum((column < order).astype(jnp.int32), axis=0, keepdims=True)
        starts += jnp.sum((column < limit).astype(jnp.int32), axis=0, keepdims=True)
    target = lax.broadcasted_iota(jnp.int32, (count, count), 0)
    permute = (target == rank).astype(jnp.float32).astype(jnp.bfloat16)
    source = cell // NG
    receiver = cell % NG
    row = lax.broadcasted_iota(jnp.int32, (bands * ROWS, count), 0) % ROWS
    digits = jnp.where(row == CH + 1, source % BLOCK, 0)
    digits = jnp.where(row == CH + 2, receiver // HALF, digits)
    digits = jnp.where(row == CH + 3, receiver % HALF, digits)
    spectra = contract_last(twiddle_ref[...], traces_ref[0])
    packed = (spectra + digits.astype(jnp.float32)).astype(jnp.bfloat16)
    ordered = contract_last(packed, permute) + jnp.where(row == CH, starts, 0).astype(jnp.float32)
    for band in range(bands):
        part = ordered[band * ROWS : (band + 1) * ROWS].astype(jnp.bfloat16)
        for tile in range(tiles):
            out_ref[tile, band] = part


def make_table(first_run, lists_ref, keys, table, table_s, sem):
    length = lists_ref.shape[2]
    for r in range(GROUP):
        part = lists_ref[first_run + r].astype(jnp.float32)
        keys[r : r + 1, :] = part[CH : CH + 1, :128]
    starts = keys[...]
    lane = lax.broadcasted_iota(jnp.int32, (GROUP, 128), 1)
    sizes = jnp.where(lane < BLOCKS, pltpu.roll(starts, 127, 1) - starts, 0.0)
    earlier = lax.broadcasted_iota(jnp.int32, (GROUP, GROUP), 0) > lax.broadcasted_iota(
        jnp.int32, (GROUP, GROUP), 1
    )
    targets = jnp.dot(
        earlier.astype(jnp.float32).astype(jnp.bfloat16),
        sizes.astype(jnp.bfloat16),
        preferred_element_type=jnp.float32,
    )
    run = lax.broadcasted_iota(jnp.int32, (GROUP, 128), 0)
    table[:GROUP, :] = starts.astype(jnp.int32) + run * length
    table[GROUP : 2 * GROUP, :] = jnp.minimum(targets, float(LARGE)).astype(jnp.int32)
    widest = jnp.max(sizes, axis=0, keepdims=True)
    total = jnp.sum(sizes, axis=0, keepdims=True)
    last = lax.broadcasted_iota(jnp.int32, (8, 128), 0)
    table[2 * GROUP :, :] = jnp.where(last == 0, widest, total).astype(jnp.int32)
    copy = pltpu.make_async_copy(table, table_s, sem)
    copy.start()
    return copy


def turn_runs(first_run, lists_ref, flat):
    length = lists_ref.shape[2]
    for r in range(GROUP):
        part = lists_ref[first_run + r].astype(jnp.float32)
        for first in range(0, length, 128):
            at = r * length + first
            flat[at : at + 128, :ROWS] = jnp.transpose(part[:, first : first + 128])


def turned(first, width, packed):
    return jnp.concatenate(
        [jnp.transpose(packed[pl.ds(first + k, 128), :])[:ROWS] for k in range(0, width, 128)],
        axis=1,
    )


def products(row_of, width, size):
    step = lax.broadcasted_iota(jnp.int32, (BLOCK, width), 0).astype(jnp.float32)
    step = step.astype(jnp.bfloat16)
    place = lax.broadcasted_iota(jnp.int32, (1, width), 1)
    one = jnp.ones((), jnp.bfloat16)
    none = jnp.zeros((), jnp.bfloat16)

    def spread(row):
        return jnp.broadcast_to(row, (BLOCK, width)).astype(jnp.bfloat16)

    hit = spread(jnp.where(place < size, row_of(CH + 1), -1.0)) == step
    left = [jnp.where(hit, one, none)]
    left += [jnp.where(hit, spread(row_of(c)), none) for c in range(CH)]
    left = jnp.concatenate(left, axis=0)
    which, place = row_of(CH + 2), row_of(CH + 3)
    for half in range(NG // HALF):
        low = spread(jnp.where(which == float(half), place, -1.0))
        right = [
            jnp.where(low == step + jnp.bfloat16(j), one, none) for j in range(0, HALF, BLOCK)
        ]
        yield pl.ds(half * HALF, HALF), contract_last(left, jnp.concatenate(right, axis=0))


def block_rows(b):
    return pl.ds(pl.multiple_of(b * BLOCK, BLOCK), BLOCK)


def add_blocks(table_s, flat, buffers, later, packed, total, emit):
    sides = BLOCKS // SIDE

    def merge(i, q):
        b = jnp.minimum(i, sides - 1) * SIDE + q
        for r in range(GROUP):
            buffers[q][pl.ds(table_s[GROUP + r, b], COPY), :] = flat[pl.ds(table_s[r, b], COPY), :]
        later[q] = turned(0, LARGE, buffers[q])

    def fast(i, width):
        for q in range(SIDE):
            b = i * SIDE + q
            block = functools.partial(lambda q, c: later[q, c : c + 1, :width], q)
            for lanes, sums in products(block, width, table_s[2 * GROUP + 1, b]):
                emit(b, lanes, sums)
            merge(i + 1, q)

    def slow(b):
        def run(r, target):
            source = table_s[r, b]
            count = table_s[r, b + 1] - source

            def piece(k, _):
                packed[pl.ds(target + 8 * k, 8), :] = flat[pl.ds(source + 8 * k, 8), :]
                return 0

            lax.fori_loop(0, (count + 7) // 8, piece, 0)
            return target + count

        lax.fori_loop(0, GROUP, run, 0)
        total[...] = jnp.zeros_like(total)
        size = table_s[2 * GROUP + 1, b]

        def piece(k, _):
            first = pl.multiple_of(k * LARGE, LARGE)
            part = turned(first, LARGE, packed)
            for lanes, sums in products(lambda c: part[c : c + 1], LARGE, size - first):
                total[:, lanes] += sums
            return 0

        lax.fori_loop(0, (size + LARGE - 1) // LARGE, piece, 0)
        for half in range(NG // HALF):
            lanes = pl.ds(half * HALF, HALF)
            emit(b, lanes, total[:, lanes])

    def side(i, _):
        b = i * SIDE
        widest = table_s[2 * GROUP, b]
        largest = table_s[2 * GROUP + 1, b]
        for q in range(1, SIDE):
            widest = jnp.maximum(widest, table_s[2 * GROUP, b + q])
            largest = jnp.maximum(largest, table_s[2 * GROUP + 1, b + q])
        plain = widest <= COPY
        least = -1
        for width in WIDTHS:

            @pl.when(plain & (largest > least) & (largest <= width))
            def _(width=width):
                fast(i, width)

            least = width

        @pl.when(jnp.logical_not(plain) | (largest > LARGE))
        def _():
            for q in range(SIDE):
                merge(i + 1, q)
            lax.fori_loop(0, SIDE, lambda q, _: (slow(b + q), 0)[1], 0)

        return 0

    for q in range(SIDE):
        merge(jnp.int32(0), q)
    lax.fori_loop(0, sides, side, 0)


def grid_kernel(
    scale, row_block, lists_ref, out_ref, planes, flat, packed, keys, table, twice, total, result,
    table_s, sem, out_sems, *rest
):
    runs = lists_ref.shape[0]
    alone = runs == GROUP
    later, *buffers = rest[: SIDE + 1]
    grid = rest[SIDE + 1] if not alone else None

    def finish(sums, rows, lanes):
        inverse = 1.0 / jnp.maximum(sums(0), 1.0)
        for c in range(CH):
            planes[c, rows, lanes] = (sums(c + 1) * inverse).astype(jnp.bfloat16)

    def emit(b, lanes, sums):
        rows = block_rows(b)
        if alone:
            finish(lambda c: sums[c * BLOCK : (c + 1) * BLOCK], rows, lanes)
        else:
            for c in range(CH + 1):
                grid[c, rows, lanes] += sums[c * BLOCK : (c + 1) * BLOCK]

    def group(g, _):
        copy = make_table(g * GROUP, lists_ref, keys, table, table_s, sem)
        turn_runs(g * GROUP, lists_ref, flat)
        copy.wait()
        add_blocks(table_s, flat, buffers, later, packed, total, emit)
        return 0

    if alone:
        group(0, 0)
    else:
        grid[...] = jnp.zeros_like(grid)
        lax.fori_loop(0, runs // GROUP, group, 0)

        def divide(b, _):
            rows = block_rows(b)
            finish(lambda c: grid[c, rows, :], rows, pl.ds(0, NG))
            return 0

        lax.fori_loop(0, BLOCKS, divide, 0)

    first_row = pl.multiple_of(lax.axis_index("tile") * row_block, row_block)

    def sent(f):
        return pltpu.make_async_copy(result.at[f], out_ref.at[f], out_sems.at[f])

    def frequency(f, slot):
        for part, p in enumerate((f, FB + f)):
            for i in range(0, NG, TURN):
                for j in range(0, NG, TURN):
                    across = jnp.transpose(planes[p, j : j + TURN, i : i + TURN])
                    twice[slot, part * NG + i : part * NG + i + TURN, j : j + TURN] = (
                        planes[p, i : i + TURN, j : j + TURN] + across
                    )
        real = twice[slot, pl.ds(first_row, row_block), :]
        imag = twice[slot, pl.ds(NG + first_row, row_block), :]
        own = jnp.concatenate(
            [jnp.concatenate([real, -imag], axis=1), jnp.concatenate([imag, real], axis=1)], axis=0
        )
        for half in range(NG // HALF):
            lanes = slice(half * HALF, (half + 1) * HALF)
            both = jnp.dot(own, twice[slot, :, lanes], preferred_element_type=jnp.float32)
            both = both * (0.25 * scale)
            result[f, 0, :, lanes] = both[:row_block]
            result[f, 1, :, lanes] = both[row_block:]
        sent(f).start()

    def some(i, _):
        for q in range(BESIDE):
            frequency(i * BESIDE + q, q)
        return 0

    lax.fori_loop(0, FB // BESIDE, some, 0)
    for f in range(FB):
        sent(f).wait()


def whole(space=pltpu.VMEM):
    return pl.BlockSpec(memory_space=space)


def per_device(raw_traces, bin_owner, bin_offset):
    band_count = lax.axis_size("band")
    tile_count = lax.axis_size("tile")
    length = bin_offset.shape[1]
    count = raw_traces.shape[1]
    cells_dev = NG * NG // tile_count
    row_block = NG // tile_count
    runs = band_count * tile_count
    params = pltpu.CompilerParams(vmem_limit_bytes=VMEM)

    own = pl.pallas_call(
        functools.partial(run_kernel, cells_dev),
        out_shape=jax.ShapeDtypeStruct((tile_count, band_count, ROWS, count), jnp.bfloat16),
        in_specs=[whole()] * 4,
        out_specs=whole(),
        compiler_params=params,
        name="own_run",
    )(
        jnp.asarray(twiddle_rows(band_count)),
        raw_traces,
        bin_owner.reshape(1, length),
        bin_offset,
    )
    lists = lax.all_to_all(
        own.reshape(runs, ROWS, count), ("tile", "band"), split_axis=0, concat_axis=0, tiled=True
    )

    traces = GROUP * count
    scratch = [
        pltpu.VMEM((CH, NG, NG), jnp.bfloat16),
        pltpu.VMEM((traces + COPY, 128), jnp.float32),
        pltpu.VMEM((traces + LARGE, 128), jnp.float32),
        pltpu.VMEM((GROUP, 128), jnp.float32),
        pltpu.VMEM((2 * GROUP + 8, 128), jnp.int32),
        pltpu.VMEM((BESIDE, 2 * NG, NG), jnp.bfloat16),
        pltpu.VMEM(((CH + 1) * BLOCK, NG), jnp.float32),
        pltpu.VMEM((FB, 2, row_block, NG), jnp.float32),
        pltpu.SMEM((2 * GROUP + 8, 128), jnp.int32),
        pltpu.SemaphoreType.DMA,
        pltpu.SemaphoreType.DMA((FB,)),
    ]
    scratch.append(pltpu.VMEM((SIDE, ROWS, LARGE), jnp.float32))
    scratch += [pltpu.VMEM((LARGE + COPY, 128), jnp.float32)] * SIDE
    if runs != GROUP:
        scratch.append(pltpu.VMEM((CH + 1, NG, NG), jnp.float32))
    return pl.pallas_call(
        functools.partial(grid_kernel, 1.0 / math.sqrt(NG), row_block),
        out_shape=jax.ShapeDtypeStruct((FB, 2, row_block, NG), jnp.float32),
        in_specs=[whole()],
        out_specs=whole(pl.ANY),
        scratch_shapes=scratch,
        compiler_params=params,
        name="grid",
    )(lists)


def solution(mesh):
    return jax.shard_map(
        per_device,
        mesh=mesh,
        in_specs=(P("tile", "band", None), P("tile", None, None), P("tile", None)),
        out_specs=P("band", None, "tile", None),
        check_vma=False,
    )
```

```python
import functools
import math

import jax
import jax.numpy as jnp
import ml_dtypes
import numpy as np
from jax import lax
from jax.experimental import pallas as pl
from jax.experimental.pallas import tpu as pltpu
from jax.sharding import PartitionSpec as P

NG = 512
NT = 2048
FB = 10
CH = 2 * FB
ROWS = 24
BLOCK = 16
BLOCKS = NG // BLOCK
GROUP = 32
COPY = 32
WIDTHS = (256, 512, 640)
LARGE = WIDTHS[-1]
BESIDE = 5
SIDE = 4
TURN = 128
HALF = 256
VMEM = 56 * 1024 * 1024


def twiddle_rows(band_count):
    time_index = np.arange(NT)[None, None, :]
    freq_index = np.arange(band_count * FB).reshape(band_count, FB, 1) + 1
    angle = (time_index * freq_index % NT) * (2.0 * math.pi / NT)
    norm = 1.0 / math.sqrt(NT)
    table = np.zeros((band_count, ROWS, NT), np.float64)
    table[:, :FB] = np.cos(angle) * norm
    table[:, FB:CH] = -np.sin(angle) * norm
    return table.reshape(band_count * ROWS, NT).astype(ml_dtypes.bfloat16)


def contract_last(left, right):
    return lax.dot_general(
        left, right, (((1,), (1,)), ((), ())), preferred_element_type=jnp.float32
    )


def run_kernel(cells_dev, twiddle_ref, traces_ref, owner_ref, offset_ref, out_ref):
    tiles, bands, _, count = out_ref.shape
    lanes = pl.ds(pl.multiple_of(lax.axis_index("band") * count, count), count)
    cell = owner_ref[:, lanes] * cells_dev + offset_ref[:, lanes]
    order = cell * count + lax.broadcasted_iota(jnp.int32, (1, count), 1)
    rank = jnp.zeros((1, count), jnp.int32)
    starts = jnp.zeros((1, count), jnp.int32)
    limit = lax.broadcasted_iota(jnp.int32, (1, count), 1) * (BLOCK * NG * count)
    limit = jnp.minimum(limit, NG * NG * count)
    for first in range(0, count, 128):
        column = jnp.transpose(jnp.broadcast_to(order[:, first : first + 128], (128, 128)))
        column = jnp.concatenate([column] * (count // 128), axis=1)
        rank += jnp.sum((column < order).astype(jnp.int32), axis=0, keepdims=True)
        starts += jnp.sum((column < limit).astype(jnp.int32), axis=0, keepdims=True)
    target = lax.broadcasted_iota(jnp.int32, (count, count), 0)
    permute = (target == rank).astype(jnp.float32).astype(jnp.bfloat16)
    source = cell // NG
    receiver = cell % NG
    row = lax.broadcasted_iota(jnp.int32, (bands * ROWS, count), 0) % ROWS
    digits = jnp.where(row == CH + 1, source % BLOCK, 0)
    digits = jnp.where(row == CH + 2, receiver // HALF, digits)
    digits = jnp.where(row == CH + 3, receiver % HALF, digits)
    spectra = contract_last(twiddle_ref[...], traces_ref[0])
    packed = (spectra + digits.astype(jnp.float32)).astype(jnp.bfloat16)
    ordered = contract_last(packed, permute) + jnp.where(row == CH, starts, 0).astype(jnp.float32)
    for band in range(bands):
        part = ordered[band * ROWS : (band + 1) * ROWS].astype(jnp.bfloat16)
        for tile in range(tiles):
            out_ref[tile, band] = part


def make_table(first_run, lists_ref, keys, table, table_s, sem):
    length = lists_ref.shape[2]
    for r in range(GROUP):
        part = lists_ref[first_run + r].astype(jnp.float32)
        keys[r : r + 1, :] = part[CH : CH + 1, :128]
    starts = keys[...]
    lane = lax.broadcasted_iota(jnp.int32, (GROUP, 128), 1)
    sizes = jnp.where(lane < BLOCKS, pltpu.roll(starts, 127, 1) - starts, 0.0)
    earlier = lax.broadcasted_iota(jnp.int32, (GROUP, GROUP), 0) > lax.broadcasted_iota(
        jnp.int32, (GROUP, GROUP), 1
    )
    targets = jnp.dot(
        earlier.astype(jnp.float32).astype(jnp.bfloat16),
        sizes.astype(jnp.bfloat16),
        preferred_element_type=jnp.float32,
    )
    run = lax.broadcasted_iota(jnp.int32, (GROUP, 128), 0)
    table[:GROUP, :] = starts.astype(jnp.int32) + run * length
    table[GROUP : 2 * GROUP, :] = jnp.minimum(targets, float(LARGE)).astype(jnp.int32)
    widest = jnp.max(sizes, axis=0, keepdims=True)
    total = jnp.sum(sizes, axis=0, keepdims=True)
    last = lax.broadcasted_iota(jnp.int32, (8, 128), 0)
    table[2 * GROUP :, :] = jnp.where(last == 0, widest, total).astype(jnp.int32)
    copy = pltpu.make_async_copy(table, table_s, sem)
    copy.start()
    return copy


def turn_runs(first_run, lists_ref, flat):
    length = lists_ref.shape[2]
    for r in range(GROUP):
        part = lists_ref[first_run + r].astype(jnp.float32)
        for first in range(0, length, 128):
            at = r * length + first
            flat[at : at + 128, :ROWS] = jnp.transpose(part[:, first : first + 128])


def turned(first, width, packed):
    return jnp.concatenate(
        [jnp.transpose(packed[pl.ds(first + k, 128), :])[:ROWS] for k in range(0, width, 128)],
        axis=1,
    )


def products(part, size):
    width = part.shape[1]
    step = lax.broadcasted_iota(jnp.int32, (BLOCK, width), 0).astype(jnp.float32)
    step = step.astype(jnp.bfloat16)
    place = lax.broadcasted_iota(jnp.int32, (1, width), 1)
    one = jnp.ones((), jnp.bfloat16)
    none = jnp.zeros((), jnp.bfloat16)

    def spread(row):
        return jnp.broadcast_to(row, (BLOCK, width)).astype(jnp.bfloat16)

    hit = spread(jnp.where(place < size, part[CH + 1 : CH + 2], -1.0)) == step
    left = [jnp.where(hit, one, none)]
    left += [jnp.where(hit, spread(part[c : c + 1]), none) for c in range(CH)]
    left = jnp.concatenate(left, axis=0)
    for half in range(NG // HALF):
        low = spread(jnp.where(part[CH + 2 : CH + 3] == float(half), part[CH + 3 : CH + 4], -1.0))
        right = [
            jnp.where(low == step + jnp.bfloat16(j), one, none) for j in range(0, HALF, BLOCK)
        ]
        yield pl.ds(half * HALF, HALF), contract_last(left, jnp.concatenate(right, axis=0))


def block_rows(b):
    return pl.ds(pl.multiple_of(b * BLOCK, BLOCK), BLOCK)


def add_blocks(table_s, flat, buffers, later, packed, total, emit):
    sides = BLOCKS // SIDE

    def merge(i, q):
        b = jnp.minimum(i, sides - 1) * SIDE + q
        for r in range(GROUP):
            buffers[q][pl.ds(table_s[GROUP + r, b], COPY), :] = flat[pl.ds(table_s[r, b], COPY), :]
        later[q] = turned(0, LARGE, buffers[q])

    def fast(i, width):
        parts = [later[q, :, :width] for q in range(SIDE)]
        for q in range(SIDE):
            merge(i + 1, q)
            b = i * SIDE + q
            for lanes, sums in products(parts[q], table_s[2 * GROUP + 1, b]):
                emit(b, lanes, sums)

    def slow(b):
        def run(r, target):
            source = table_s[r, b]
            count = table_s[r, b + 1] - source

            def piece(k, _):
                packed[pl.ds(target + 8 * k, 8), :] = flat[pl.ds(source + 8 * k, 8), :]
                return 0

            lax.fori_loop(0, (count + 7) // 8, piece, 0)
            return target + count

        lax.fori_loop(0, GROUP, run, 0)
        total[...] = jnp.zeros_like(total)
        size = table_s[2 * GROUP + 1, b]

        def piece(k, _):
            first = pl.multiple_of(k * LARGE, LARGE)
            for lanes, sums in products(turned(first, LARGE, packed), size - first):
                total[:, lanes] += sums
            return 0

        lax.fori_loop(0, (size + LARGE - 1) // LARGE, piece, 0)
        for half in range(NG // HALF):
            lanes = pl.ds(half * HALF, HALF)
            emit(b, lanes, total[:, lanes])

    def side(i, _):
        b = i * SIDE
        widest = table_s[2 * GROUP, b]
        largest = table_s[2 * GROUP + 1, b]
        for q in range(1, SIDE):
            widest = jnp.maximum(widest, table_s[2 * GROUP, b + q])
            largest = jnp.maximum(largest, table_s[2 * GROUP + 1, b + q])
        plain = widest <= COPY
        least = -1
        for width in WIDTHS:

            @pl.when(plain & (largest > least) & (largest <= width))
            def _(width=width):
                fast(i, width)

            least = width

        @pl.when(jnp.logical_not(plain) | (largest > LARGE))
        def _():
            for q in range(SIDE):
                merge(i + 1, q)
            lax.fori_loop(0, SIDE, lambda q, _: (slow(b + q), 0)[1], 0)

        return 0

    for q in range(SIDE):
        merge(jnp.int32(0), q)
    lax.fori_loop(0, sides, side, 0)


def grid_kernel(
    scale, row_block, lists_ref, out_ref, planes, flat, packed, keys, table, twice, total, result,
    table_s, sem, out_sems, *rest
):
    runs = lists_ref.shape[0]
    alone = runs == GROUP
    later, *buffers = rest[: SIDE + 1]
    grid = rest[SIDE + 1] if not alone else None

    def finish(sums, rows, lanes):
        inverse = 1.0 / jnp.maximum(sums(0), 1.0)
        for c in range(CH):
            planes[c, rows, lanes] = (sums(c + 1) * inverse).astype(jnp.bfloat16)

    def emit(b, lanes, sums):
        rows = block_rows(b)
        if alone:
            finish(lambda c: sums[c * BLOCK : (c + 1) * BLOCK], rows, lanes)
        else:
            for c in range(CH + 1):
                grid[c, rows, lanes] += sums[c * BLOCK : (c + 1) * BLOCK]

    def group(g, _):
        copy = make_table(g * GROUP, lists_ref, keys, table, table_s, sem)
        turn_runs(g * GROUP, lists_ref, flat)
        copy.wait()
        add_blocks(table_s, flat, buffers, later, packed, total, emit)
        return 0

    if alone:
        group(0, 0)
    else:
        grid[...] = jnp.zeros_like(grid)
        lax.fori_loop(0, runs // GROUP, group, 0)

        def divide(b, _):
            rows = block_rows(b)
            finish(lambda c: grid[c, rows, :], rows, pl.ds(0, NG))
            return 0

        lax.fori_loop(0, BLOCKS, divide, 0)

    first_row = pl.multiple_of(lax.axis_index("tile") * row_block, row_block)

    def sent(f):
        return pltpu.make_async_copy(result.at[f], out_ref.at[f], out_sems.at[f])

    def form(f, slot):
        for part, p in enumerate((f, FB + f)):
            for i in range(0, NG, TURN):
                for j in range(0, NG, TURN):
                    across = jnp.transpose(planes[p, j : j + TURN, i : i + TURN])
                    twice[slot, part * NG + i : part * NG + i + TURN, j : j + TURN] = (
                        planes[p, i : i + TURN, j : j + TURN] + across
                    )

    def multiply(f, slot):
        real = twice[slot, pl.ds(first_row, row_block), :]
        imag = twice[slot, pl.ds(NG + first_row, row_block), :]
        own = jnp.concatenate(
            [jnp.concatenate([real, -imag], axis=1), jnp.concatenate([imag, real], axis=1)], axis=0
        )
        for half in range(NG // HALF):
            lanes = slice(half * HALF, (half + 1) * HALF)
            both = jnp.dot(own, twice[slot, :, lanes], preferred_element_type=jnp.float32)
            both = both * (0.25 * scale)
            result[f, 0, :, lanes] = both[:row_block]
            result[f, 1, :, lanes] = both[row_block:]
        sent(f).start()

    def some(i, _):
        form(i * BESIDE, 0)
        for q in range(BESIDE):
            if q + 1 < BESIDE:
                form(i * BESIDE + q + 1, q + 1)
            multiply(i * BESIDE + q, q)
        return 0

    lax.fori_loop(0, FB // BESIDE, some, 0)
    for f in range(FB):
        sent(f).wait()


def whole(space=pltpu.VMEM):
    return pl.BlockSpec(memory_space=space)


def per_device(raw_traces, bin_owner, bin_offset):
    band_count = lax.axis_size("band")
    tile_count = lax.axis_size("tile")
    length = bin_offset.shape[1]
    count = raw_traces.shape[1]
    cells_dev = NG * NG // tile_count
    row_block = NG // tile_count
    runs = band_count * tile_count
    params = pltpu.CompilerParams(vmem_limit_bytes=VMEM)

    own = pl.pallas_call(
        functools.partial(run_kernel, cells_dev),
        out_shape=jax.ShapeDtypeStruct((tile_count, band_count, ROWS, count), jnp.bfloat16),
        in_specs=[whole()] * 4,
        out_specs=whole(),
        compiler_params=params,
        name="own_run",
    )(
        jnp.asarray(twiddle_rows(band_count)),
        raw_traces,
        bin_owner.reshape(1, length),
        bin_offset,
    )
    lists = lax.all_to_all(
        own.reshape(runs, ROWS, count), ("tile", "band"), split_axis=0, concat_axis=0, tiled=True
    )

    traces = GROUP * count
    scratch = [
        pltpu.VMEM((CH, NG, NG), jnp.bfloat16),
        pltpu.VMEM((traces + COPY, 128), jnp.float32),
        pltpu.VMEM((traces + LARGE, 128), jnp.float32),
        pltpu.VMEM((GROUP, 128), jnp.float32),
        pltpu.VMEM((2 * GROUP + 8, 128), jnp.int32),
        pltpu.VMEM((BESIDE, 2 * NG, NG), jnp.bfloat16),
        pltpu.VMEM(((CH + 1) * BLOCK, NG), jnp.float32),
        pltpu.VMEM((FB, 2, row_block, NG), jnp.float32),
        pltpu.SMEM((2 * GROUP + 8, 128), jnp.int32),
        pltpu.SemaphoreType.DMA,
        pltpu.SemaphoreType.DMA((FB,)),
    ]
    scratch.append(pltpu.VMEM((SIDE, ROWS, LARGE), jnp.float32))
    scratch += [pltpu.VMEM((LARGE + COPY, 128), jnp.float32)] * SIDE
    if runs != GROUP:
        scratch.append(pltpu.VMEM((CH + 1, NG, NG), jnp.float32))
    return pl.pallas_call(
        functools.partial(grid_kernel, 1.0 / math.sqrt(NG), row_block),
        out_shape=jax.ShapeDtypeStruct((FB, 2, row_block, NG), jnp.float32),
        in_specs=[whole()],
        out_specs=whole(pl.ANY),
        scratch_shapes=scratch,
        compiler_params=params,
        name="grid",
    )(lists)


def solution(mesh):
    return jax.shard_map(
        per_device,
        mesh=mesh,
        in_specs=(P("tile", "band", None), P("tile", None, None), P("tile", None)),
        out_specs=P("band", None, "tile", None),
        check_vma=False,
    )
```

```python
import functools
import math

import jax
import jax.numpy as jnp
import ml_dtypes
import numpy as np
from jax import lax
from jax.experimental import pallas as pl
from jax.experimental.pallas import tpu as pltpu
from jax.sharding import PartitionSpec as P

NG = 512
NT = 2048
FB = 10
CH = 2 * FB
ROWS = 24
BLOCK = 16
BLOCKS = NG // BLOCK
GROUP = 32
COPY = 32
WIDTHS = (256, 512, 640)
LARGE = WIDTHS[-1]
BESIDE = 10
SLOTS = 5
SIDE = 4
TURN = 128
HALF = 256
VMEM = 56 * 1024 * 1024


def twiddle_columns(band_count):
    time_index = np.arange(NT)[:, None, None]
    freq_index = np.arange(band_count * FB).reshape(1, band_count, FB) + 1
    angle = (time_index * freq_index % NT) * (2.0 * math.pi / NT)
    norm = 1.0 / math.sqrt(NT)
    table = np.zeros((NT, band_count, ROWS), np.float64)
    table[:, :, :FB] = np.cos(angle) * norm
    table[:, :, FB:CH] = -np.sin(angle) * norm
    table = table.reshape(NT, band_count * ROWS)
    table = np.pad(table, ((0, 0), (0, -band_count * ROWS % 128)))
    return table.astype(ml_dtypes.bfloat16)


def contract_last(left, right):
    return lax.dot_general(
        left, right, (((1,), (1,)), ((), ())), preferred_element_type=jnp.float32
    )


def run_kernel(cells_dev, twiddle_ref, traces_ref, owner_ref, offset_ref, out_ref):
    tiles, bands, _, count = out_ref.shape
    lanes = pl.ds(pl.multiple_of(lax.axis_index("band") * count, count), count)
    cell = owner_ref[:, lanes] * cells_dev + offset_ref[:, lanes]
    order = cell * count + lax.broadcasted_iota(jnp.int32, (1, count), 1)
    rank = jnp.zeros((1, count), jnp.int32)
    starts = jnp.zeros((1, count), jnp.int32)
    limit = lax.broadcasted_iota(jnp.int32, (1, count), 1) * (BLOCK * NG * count)
    limit = jnp.minimum(limit, NG * NG * count)
    for first in range(0, count, 128):
        column = jnp.transpose(jnp.broadcast_to(order[:, first : first + 128], (128, 128)))
        column = jnp.concatenate([column] * (count // 128), axis=1)
        rank += jnp.sum((column < order).astype(jnp.int32), axis=0, keepdims=True)
        starts += jnp.sum((column < limit).astype(jnp.int32), axis=0, keepdims=True)
    target = lax.broadcasted_iota(jnp.int32, (count, count), 0)
    permute = (target == rank).astype(jnp.float32).astype(jnp.bfloat16)
    source = cell // NG
    receiver = cell % NG
    row = lax.broadcasted_iota(jnp.int32, (bands * ROWS, count), 0) % ROWS
    digits = jnp.where(row == CH + 1, source % BLOCK, 0)
    digits = jnp.where(row == CH + 2, receiver // HALF, digits)
    digits = jnp.where(row == CH + 3, receiver % HALF, digits)
    spectra = jnp.dot(traces_ref[0], twiddle_ref[...], preferred_element_type=jnp.float32)
    spectra = jnp.transpose(spectra)[: bands * ROWS]
    packed = (spectra + digits.astype(jnp.float32)).astype(jnp.bfloat16)
    ordered = contract_last(packed, permute) + jnp.where(row == CH, starts, 0).astype(jnp.float32)
    for band in range(bands):
        part = ordered[band * ROWS : (band + 1) * ROWS].astype(jnp.bfloat16)
        for tile in range(tiles):
            out_ref[tile, band] = part


def make_table(first_run, lists_ref, keys, table, table_s, sem):
    length = lists_ref.shape[2]
    for r in range(GROUP):
        part = lists_ref[first_run + r].astype(jnp.float32)
        keys[r : r + 1, :] = part[CH : CH + 1, :128]
    starts = keys[...]
    lane = lax.broadcasted_iota(jnp.int32, (GROUP, 128), 1)
    sizes = jnp.where(lane < BLOCKS, pltpu.roll(starts, 127, 1) - starts, 0.0)
    earlier = lax.broadcasted_iota(jnp.int32, (GROUP, GROUP), 0) > lax.broadcasted_iota(
        jnp.int32, (GROUP, GROUP), 1
    )
    targets = jnp.dot(
        earlier.astype(jnp.float32).astype(jnp.bfloat16),
        sizes.astype(jnp.bfloat16),
        preferred_element_type=jnp.float32,
    )
    run = lax.broadcasted_iota(jnp.int32, (GROUP, 128), 0)
    table[:GROUP, :] = starts.astype(jnp.int32) + run * length
    table[GROUP : 2 * GROUP, :] = jnp.minimum(targets, float(LARGE)).astype(jnp.int32)
    widest = jnp.max(sizes, axis=0, keepdims=True)
    total = jnp.sum(sizes, axis=0, keepdims=True)
    last = lax.broadcasted_iota(jnp.int32, (8, 128), 0)
    table[2 * GROUP :, :] = jnp.where(last == 0, widest, total).astype(jnp.int32)
    copy = pltpu.make_async_copy(table, table_s, sem)
    copy.start()
    return copy


def turn_runs(first_run, lists_ref, flat):
    length = lists_ref.shape[2]
    for r in range(GROUP):
        part = lists_ref[first_run + r].astype(jnp.float32)
        for first in range(0, length, 128):
            at = r * length + first
            flat[at : at + 128, :ROWS] = jnp.transpose(part[:, first : first + 128])


def turned(first, width, packed):
    return jnp.concatenate(
        [jnp.transpose(packed[pl.ds(first + k, 128), :])[:ROWS] for k in range(0, width, 128)],
        axis=1,
    )


def products(part, size):
    width = part.shape[1]
    step = lax.broadcasted_iota(jnp.int32, (BLOCK, width), 0).astype(jnp.float32)
    step = step.astype(jnp.bfloat16)
    place = lax.broadcasted_iota(jnp.int32, (1, width), 1)
    one = jnp.ones((), jnp.bfloat16)
    none = jnp.zeros((), jnp.bfloat16)

    def spread(row):
        return jnp.broadcast_to(row, (BLOCK, width)).astype(jnp.bfloat16)

    hit = spread(jnp.where(place < size, part[CH + 1 : CH + 2], -1.0)) == step
    left = [jnp.where(hit, one, none)]
    left += [jnp.where(hit, spread(part[c : c + 1]), none) for c in range(CH)]
    left = jnp.concatenate(left, axis=0)
    for half in range(NG // HALF):
        low = spread(jnp.where(part[CH + 2 : CH + 3] == float(half), part[CH + 3 : CH + 4], -1.0))
        right = [
            jnp.where(low == step + jnp.bfloat16(j), one, none) for j in range(0, HALF, BLOCK)
        ]
        yield pl.ds(half * HALF, HALF), contract_last(left, jnp.concatenate(right, axis=0))


def block_rows(b):
    return pl.ds(pl.multiple_of(b * BLOCK, BLOCK), BLOCK)


def add_blocks(table_s, flat, buffers, later, packed, total, emit):
    sides = BLOCKS // SIDE

    def merge(i, q):
        b = jnp.minimum(i, sides - 1) * SIDE + q
        for r in range(GROUP):
            buffers[q][pl.ds(table_s[GROUP + r, b], COPY), :] = flat[pl.ds(table_s[r, b], COPY), :]
        later[q] = turned(0, LARGE, buffers[q])

    def fast(i, width):
        parts = [later[q, :, :width] for q in range(SIDE)]
        for q in range(SIDE):
            merge(i + 1, q)
            b = i * SIDE + q
            for lanes, sums in products(parts[q], table_s[2 * GROUP + 1, b]):
                emit(b, lanes, sums)

    def slow(b):
        def run(r, target):
            source = table_s[r, b]
            count = table_s[r, b + 1] - source

            def piece(k, _):
                packed[pl.ds(target + 8 * k, 8), :] = flat[pl.ds(source + 8 * k, 8), :]
                return 0

            lax.fori_loop(0, (count + 7) // 8, piece, 0)
            return target + count

        lax.fori_loop(0, GROUP, run, 0)
        total[...] = jnp.zeros_like(total)
        size = table_s[2 * GROUP + 1, b]

        def piece(k, _):
            first = pl.multiple_of(k * LARGE, LARGE)
            for lanes, sums in products(turned(first, LARGE, packed), size - first):
                total[:, lanes] += sums
            return 0

        lax.fori_loop(0, (size + LARGE - 1) // LARGE, piece, 0)
        for half in range(NG // HALF):
            lanes = pl.ds(half * HALF, HALF)
            emit(b, lanes, total[:, lanes])

    def side(i, _):
        b = i * SIDE
        widest = table_s[2 * GROUP, b]
        largest = table_s[2 * GROUP + 1, b]
        for q in range(1, SIDE):
            widest = jnp.maximum(widest, table_s[2 * GROUP, b + q])
            largest = jnp.maximum(largest, table_s[2 * GROUP + 1, b + q])
        plain = widest <= COPY
        least = -1
        for width in WIDTHS:

            @pl.when(plain & (largest > least) & (largest <= width))
            def _(width=width):
                fast(i, width)

            least = width

        @pl.when(jnp.logical_not(plain) | (largest > LARGE))
        def _():
            for q in range(SIDE):
                merge(i + 1, q)
            lax.fori_loop(0, SIDE, lambda q, _: (slow(b + q), 0)[1], 0)

        return 0

    for q in range(SIDE):
        merge(jnp.int32(0), q)
    lax.fori_loop(0, sides, side, 0)


def grid_kernel(
    scale, row_block, lists_ref, out_ref, planes, flat, packed, keys, table, twice, total, result,
    table_s, sem, out_sems, *rest
):
    runs = lists_ref.shape[0]
    alone = runs == GROUP
    later, *buffers = rest[: SIDE + 1]
    grid = rest[SIDE + 1] if not alone else None

    def finish(sums, rows, lanes):
        inverse = 1.0 / jnp.maximum(sums(0), 1.0)
        for c in range(CH):
            planes[c, rows, lanes] = (sums(c + 1) * inverse).astype(jnp.bfloat16)

    def emit(b, lanes, sums):
        rows = block_rows(b)
        if alone:
            finish(lambda c: sums[c * BLOCK : (c + 1) * BLOCK], rows, lanes)
        else:
            for c in range(CH + 1):
                grid[c, rows, lanes] += sums[c * BLOCK : (c + 1) * BLOCK]

    def group(g, _):
        copy = make_table(g * GROUP, lists_ref, keys, table, table_s, sem)
        turn_runs(g * GROUP, lists_ref, flat)
        copy.wait()
        add_blocks(table_s, flat, buffers, later, packed, total, emit)
        return 0

    if alone:
        group(0, 0)
    else:
        grid[...] = jnp.zeros_like(grid)
        lax.fori_loop(0, runs // GROUP, group, 0)

        def divide(b, _):
            rows = block_rows(b)
            finish(lambda c: grid[c, rows, :], rows, pl.ds(0, NG))
            return 0

        lax.fori_loop(0, BLOCKS, divide, 0)

    first_row = pl.multiple_of(lax.axis_index("tile") * row_block, row_block)

    def sent(f):
        return pltpu.make_async_copy(result.at[f], out_ref.at[f], out_sems.at[f])

    def frequency(f, slot):
        for part, p in enumerate((f, FB + f)):
            for i in range(0, NG, TURN):
                for j in range(0, NG, TURN):
                    across = jnp.transpose(planes[p, j : j + TURN, i : i + TURN])
                    twice[slot, part * NG + i : part * NG + i + TURN, j : j + TURN] = (
                        planes[p, i : i + TURN, j : j + TURN] + across
                    )
        real = twice[slot, pl.ds(first_row, row_block), :]
        imag = twice[slot, pl.ds(NG + first_row, row_block), :]
        own = jnp.concatenate(
            [jnp.concatenate([real, -imag], axis=1), jnp.concatenate([imag, real], axis=1)], axis=0
        )
        for half in range(NG // HALF):
            lanes = slice(half * HALF, (half + 1) * HALF)
            both = jnp.dot(own, twice[slot, :, lanes], preferred_element_type=jnp.float32)
            both = both * (0.25 * scale)
            result[f, 0, :, lanes] = both[:row_block]
            result[f, 1, :, lanes] = both[row_block:]
        sent(f).start()

    def some(i, _):
        for q in range(BESIDE):
            frequency(i * BESIDE + q, q % SLOTS)
        return 0

    lax.fori_loop(0, FB // BESIDE, some, 0)
    for f in range(FB):
        sent(f).wait()


def whole(space=pltpu.VMEM):
    return pl.BlockSpec(memory_space=space)


def per_device(raw_traces, bin_owner, bin_offset):
    band_count = lax.axis_size("band")
    tile_count = lax.axis_size("tile")
    length = bin_offset.shape[1]
    count = raw_traces.shape[1]
    cells_dev = NG * NG // tile_count
    row_block = NG // tile_count
    runs = band_count * tile_count
    params = pltpu.CompilerParams(vmem_limit_bytes=VMEM)

    own = pl.pallas_call(
        functools.partial(run_kernel, cells_dev),
        out_shape=jax.ShapeDtypeStruct((tile_count, band_count, ROWS, count), jnp.bfloat16),
        in_specs=[whole()] * 4,
        out_specs=whole(),
        compiler_params=params,
        name="own_run",
    )(
        jnp.asarray(twiddle_columns(band_count)),
        raw_traces,
        bin_owner.reshape(1, length),
        bin_offset,
    )
    lists = lax.all_to_all(
        own.reshape(runs, ROWS, count), ("tile", "band"), split_axis=0, concat_axis=0, tiled=True
    )

    traces = GROUP * count
    scratch = [
        pltpu.VMEM((CH, NG, NG), jnp.bfloat16),
        pltpu.VMEM((traces + COPY, 128), jnp.float32),
        pltpu.VMEM((traces + LARGE, 128), jnp.float32),
        pltpu.VMEM((GROUP, 128), jnp.float32),
        pltpu.VMEM((2 * GROUP + 8, 128), jnp.int32),
        pltpu.VMEM((SLOTS, 2 * NG, NG), jnp.bfloat16),
        pltpu.VMEM(((CH + 1) * BLOCK, NG), jnp.float32),
        pltpu.VMEM((FB, 2, row_block, NG), jnp.float32),
        pltpu.SMEM((2 * GROUP + 8, 128), jnp.int32),
        pltpu.SemaphoreType.DMA,
        pltpu.SemaphoreType.DMA((FB,)),
    ]
    scratch.append(pltpu.VMEM((SIDE, ROWS, LARGE), jnp.float32))
    scratch += [pltpu.VMEM((LARGE + COPY, 128), jnp.float32)] * SIDE
    if runs != GROUP:
        scratch.append(pltpu.VMEM((CH + 1, NG, NG), jnp.float32))
    return pl.pallas_call(
        functools.partial(grid_kernel, 1.0 / math.sqrt(NG), row_block),
        out_shape=jax.ShapeDtypeStruct((FB, 2, row_block, NG), jnp.float32),
        in_specs=[whole()],
        out_specs=whole(pl.ANY),
        scratch_shapes=scratch,
        compiler_params=params,
        name="grid",
    )(lists)


def solution(mesh):
    return jax.shard_map(
        per_device,
        mesh=mesh,
        in_specs=(P("tile", "band", None), P("tile", None, None), P("tile", None)),
        out_specs=P("band", None, "tile", None),
        check_vma=False,
    )
```

```python
import functools
import math

import jax
import jax.numpy as jnp
import ml_dtypes
import numpy as np
from jax import lax
from jax.experimental import pallas as pl
from jax.experimental.pallas import tpu as pltpu
from jax.sharding import PartitionSpec as P

NG = 512
NT = 2048
FB = 10
CH = 2 * FB
ROWS = 24
BLOCK = 16
BLOCKS = NG // BLOCK
GROUP = 32
COPY = 32
WIDTHS = (256, 512, 640)
LARGE = WIDTHS[-1]
BESIDE = 10
SLOTS = 5
SIDE = 4
TURN = 128
HALF = 256
VMEM = 56 * 1024 * 1024


def twiddle_rows(band_count):
    time_index = np.arange(NT)[None, None, :]
    freq_index = np.arange(band_count * FB).reshape(band_count, FB, 1) + 1
    angle = (time_index * freq_index % NT) * (2.0 * math.pi / NT)
    norm = 1.0 / math.sqrt(NT)
    table = np.zeros((band_count, ROWS, NT), np.float64)
    table[:, :FB] = np.cos(angle) * norm
    table[:, FB:CH] = -np.sin(angle) * norm
    return table.reshape(band_count * ROWS, NT).astype(ml_dtypes.bfloat16)


def contract_last(left, right):
    return lax.dot_general(
        left, right, (((1,), (1,)), ((), ())), preferred_element_type=jnp.float32
    )


def run_kernel(cells_dev, twiddle_ref, traces_ref, owner_ref, offset_ref, out_ref):
    tiles, bands, _, count = out_ref.shape
    lanes = pl.ds(pl.multiple_of(lax.axis_index("band") * count, count), count)
    cell = owner_ref[:, lanes] * cells_dev + offset_ref[:, lanes]
    order = cell * count + lax.broadcasted_iota(jnp.int32, (1, count), 1)
    rank = jnp.zeros((1, count), jnp.int32)
    starts = jnp.zeros((1, count), jnp.int32)
    limit = lax.broadcasted_iota(jnp.int32, (1, count), 1) * (BLOCK * NG * count)
    limit = jnp.minimum(limit, NG * NG * count)
    for first in range(0, count, 128):
        column = jnp.transpose(jnp.broadcast_to(order[:, first : first + 128], (128, 128)))
        column = jnp.concatenate([column] * (count // 128), axis=1)
        rank += jnp.sum((column < order).astype(jnp.int32), axis=0, keepdims=True)
        starts += jnp.sum((column < limit).astype(jnp.int32), axis=0, keepdims=True)
    target = lax.broadcasted_iota(jnp.int32, (count, count), 0)
    permute = (target == rank).astype(jnp.float32).astype(jnp.bfloat16)
    source = cell // NG
    receiver = cell % NG
    row = lax.broadcasted_iota(jnp.int32, (bands * ROWS, count), 0) % ROWS
    digits = jnp.where(row == CH + 1, source % BLOCK, 0)
    digits = jnp.where(row == CH + 2, receiver // HALF, digits)
    digits = jnp.where(row == CH + 3, receiver % HALF, digits)
    spectra = contract_last(twiddle_ref[...], traces_ref[0])
    packed = (spectra + digits.astype(jnp.float32)).astype(jnp.bfloat16)
    ordered = contract_last(packed, permute) + jnp.where(row == CH, starts, 0).astype(jnp.float32)
    for band in range(bands):
        part = ordered[band * ROWS : (band + 1) * ROWS].astype(jnp.bfloat16)
        for tile in range(tiles):
            out_ref[tile, band] = part


def make_table(first_run, lists_ref, keys, table, table_s, sem):
    length = lists_ref.shape[2]
    for r in range(GROUP):
        part = lists_ref[first_run + r].astype(jnp.float32)
        keys[r : r + 1, :] = part[CH : CH + 1, :128]
    starts = keys[...]
    lane = lax.broadcasted_iota(jnp.int32, (GROUP, 128), 1)
    sizes = jnp.where(lane < BLOCKS, pltpu.roll(starts, 127, 1) - starts, 0.0)
    earlier = lax.broadcasted_iota(jnp.int32, (GROUP, GROUP), 0) > lax.broadcasted_iota(
        jnp.int32, (GROUP, GROUP), 1
    )
    targets = jnp.dot(
        earlier.astype(jnp.float32).astype(jnp.bfloat16),
        sizes.astype(jnp.bfloat16),
        preferred_element_type=jnp.float32,
    )
    run = lax.broadcasted_iota(jnp.int32, (GROUP, 128), 0)
    table[:GROUP, :] = starts.astype(jnp.int32) + run * length
    table[GROUP : 2 * GROUP, :] = jnp.minimum(targets, float(LARGE)).astype(jnp.int32)
    widest = jnp.max(sizes, axis=0, keepdims=True)
    total = jnp.sum(sizes, axis=0, keepdims=True)
    last = lax.broadcasted_iota(jnp.int32, (8, 128), 0)
    table[2 * GROUP :, :] = jnp.where(last == 0, widest, total).astype(jnp.int32)
    copy = pltpu.make_async_copy(table, table_s, sem)
    copy.start()
    return copy


def turn_runs(first_run, lists_ref, flat):
    length = lists_ref.shape[2]
    for r in range(GROUP):
        part = lists_ref[first_run + r].astype(jnp.float32)
        for first in range(0, length, 128):
            at = r * length + first
            flat[at : at + 128, :ROWS] = jnp.transpose(part[:, first : first + 128])


def turned(first, width, packed):
    return jnp.concatenate(
        [jnp.transpose(packed[pl.ds(first + k, 128), :])[:ROWS] for k in range(0, width, 128)],
        axis=1,
    )


def products(part, size):
    width = part.shape[1]
    step = lax.broadcasted_iota(jnp.int32, (BLOCK, width), 0).astype(jnp.float32)
    step = step.astype(jnp.bfloat16)
    place = lax.broadcasted_iota(jnp.int32, (1, width), 1)
    one = jnp.ones((), jnp.bfloat16)
    none = jnp.zeros((), jnp.bfloat16)

    def spread(row):
        return jnp.broadcast_to(row, (BLOCK, width)).astype(jnp.bfloat16)

    hit = spread(jnp.where(place < size, part[CH + 1 : CH + 2], -1.0)) == step
    left = [jnp.where(hit, one, none)]
    left += [jnp.where(hit, spread(part[c : c + 1]), none) for c in range(CH)]
    left = jnp.concatenate(left, axis=0)
    for half in range(NG // HALF):
        low = spread(jnp.where(part[CH + 2 : CH + 3] == float(half), part[CH + 3 : CH + 4], -1.0))
        right = [
            jnp.where(low == step + jnp.bfloat16(j), one, none) for j in range(0, HALF, BLOCK)
        ]
        yield pl.ds(half * HALF, HALF), contract_last(left, jnp.concatenate(right, axis=0))


def block_rows(b):
    return pl.ds(pl.multiple_of(b * BLOCK, BLOCK), BLOCK)


def add_blocks(table_s, flat, buffers, later, packed, total, emit):
    sides = BLOCKS // SIDE

    def merge(i, q):
        b = jnp.minimum(i, sides - 1) * SIDE + q
        for r in range(GROUP):
            buffers[q][pl.ds(table_s[GROUP + r, b], COPY), :] = flat[pl.ds(table_s[r, b], COPY), :]
        later[q] = turned(0, LARGE, buffers[q])

    def fast(i, width):
        parts = [later[q, :, :width] for q in range(SIDE)]
        for q in range(SIDE):
            merge(i + 1, q)
            b = i * SIDE + q
            for lanes, sums in products(parts[q], table_s[2 * GROUP + 1, b]):
                emit(b, lanes, sums)

    def slow(b):
        def run(r, target):
            source = table_s[r, b]
            count = table_s[r, b + 1] - source

            def piece(k, _):
                packed[pl.ds(target + 8 * k, 8), :] = flat[pl.ds(source + 8 * k, 8), :]
                return 0

            lax.fori_loop(0, (count + 7) // 8, piece, 0)
            return target + count

        lax.fori_loop(0, GROUP, run, 0)
        total[...] = jnp.zeros_like(total)
        size = table_s[2 * GROUP + 1, b]

        def piece(k, _):
            first = pl.multiple_of(k * LARGE, LARGE)
            for lanes, sums in products(turned(first, LARGE, packed), size - first):
                total[:, lanes] += sums
            return 0

        lax.fori_loop(0, (size + LARGE - 1) // LARGE, piece, 0)
        for half in range(NG // HALF):
            lanes = pl.ds(half * HALF, HALF)
            emit(b, lanes, total[:, lanes])

    def side(i, _):
        b = i * SIDE
        widest = table_s[2 * GROUP, b]
        largest = table_s[2 * GROUP + 1, b]
        for q in range(1, SIDE):
            widest = jnp.maximum(widest, table_s[2 * GROUP, b + q])
            largest = jnp.maximum(largest, table_s[2 * GROUP + 1, b + q])
        plain = widest <= COPY
        least = -1
        for width in WIDTHS:

            @pl.when(plain & (largest > least) & (largest <= width))
            def _(width=width):
                fast(i, width)

            least = width

        @pl.when(jnp.logical_not(plain) | (largest > LARGE))
        def _():
            for q in range(SIDE):
                merge(i + 1, q)
            lax.fori_loop(0, SIDE, lambda q, _: (slow(b + q), 0)[1], 0)

        return 0

    for q in range(SIDE):
        merge(jnp.int32(0), q)
    lax.fori_loop(0, sides, side, 0)


def grid_kernel(
    scale, row_block, lists_ref, out_ref, planes, flat, packed, keys, table, twice, total, result,
    table_s, sem, out_sems, *rest
):
    runs = lists_ref.shape[0]
    alone = runs == GROUP
    later, *buffers = rest[: SIDE + 1]
    grid = rest[SIDE + 1] if not alone else None

    def finish(sums, rows, lanes):
        inverse = 1.0 / jnp.maximum(sums(0), 1.0)
        for c in range(CH):
            planes[c, rows, lanes] = (sums(c + 1) * inverse).astype(jnp.bfloat16)

    def emit(b, lanes, sums):
        rows = block_rows(b)
        if alone:
            finish(lambda c: sums[c * BLOCK : (c + 1) * BLOCK], rows, lanes)
        else:
            for c in range(CH + 1):
                grid[c, rows, lanes] += sums[c * BLOCK : (c + 1) * BLOCK]

    def group(g, _):
        copy = make_table(g * GROUP, lists_ref, keys, table, table_s, sem)
        turn_runs(g * GROUP, lists_ref, flat)
        copy.wait()
        add_blocks(table_s, flat, buffers, later, packed, total, emit)
        return 0

    if alone:
        group(0, 0)
    else:
        grid[...] = jnp.zeros_like(grid)
        lax.fori_loop(0, runs // GROUP, group, 0)

        def divide(b, _):
            rows = block_rows(b)
            finish(lambda c: grid[c, rows, :], rows, pl.ds(0, NG))
            return 0

        lax.fori_loop(0, BLOCKS, divide, 0)

    first_row = pl.multiple_of(lax.axis_index("tile") * row_block, row_block)

    def sent(f):
        return pltpu.make_async_copy(result.at[f], out_ref.at[f], out_sems.at[f])

    def frequency(f, slot):
        for part, p in enumerate((f, FB + f)):
            for i in range(0, NG, TURN):
                for j in range(0, NG, TURN):
                    across = jnp.transpose(planes[p, j : j + TURN, i : i + TURN])
                    twice[slot, part * NG + i : part * NG + i + TURN, j : j + TURN] = (
                        planes[p, i : i + TURN, j : j + TURN] + across
                    )
        real = twice[slot, pl.ds(first_row, row_block), :]
        imag = twice[slot, pl.ds(NG + first_row, row_block), :]
        own = jnp.concatenate(
            [jnp.concatenate([real, -imag], axis=1), jnp.concatenate([imag, real], axis=1)], axis=0
        )
        for half in range(NG // HALF):
            lanes = slice(half * HALF, (half + 1) * HALF)
            both = jnp.dot(own, twice[slot, :, lanes], preferred_element_type=jnp.float32)
            both = both * (0.25 * scale)
            result[f, 0, :, lanes] = both[:row_block]
            result[f, 1, :, lanes] = both[row_block:]
        sent(f).start()

    def some(i, _):
        for q in range(BESIDE):
            frequency(i * BESIDE + q, q % SLOTS)
        return 0

    lax.fori_loop(0, FB // BESIDE, some, 0)
    for f in range(FB):
        sent(f).wait()


def whole(space=pltpu.VMEM):
    return pl.BlockSpec(memory_space=space)


def per_device(raw_traces, bin_owner, bin_offset):
    band_count = lax.axis_size("band")
    tile_count = lax.axis_size("tile")
    length = bin_offset.shape[1]
    count = raw_traces.shape[1]
    cells_dev = NG * NG // tile_count
    row_block = NG // tile_count
    runs = band_count * tile_count
    params = pltpu.CompilerParams(vmem_limit_bytes=VMEM)

    own = pl.pallas_call(
        functools.partial(run_kernel, cells_dev),
        out_shape=jax.ShapeDtypeStruct((tile_count, band_count, ROWS, count), jnp.bfloat16),
        in_specs=[whole()] * 4,
        out_specs=whole(),
        compiler_params=params,
        name="own_run",
    )(
        jnp.asarray(twiddle_rows(band_count)),
        raw_traces,
        bin_owner.reshape(1, length),
        bin_offset,
    )
    lists = lax.all_to_all(
        own.reshape(runs, ROWS, count), ("tile", "band"), split_axis=0, concat_axis=0, tiled=True
    )

    traces = GROUP * count
    scratch = [
        pltpu.VMEM((CH, NG, NG), jnp.bfloat16),
        pltpu.VMEM((traces + COPY, 128), jnp.float32),
        pltpu.VMEM((traces + LARGE, 128), jnp.float32),
        pltpu.VMEM((GROUP, 128), jnp.float32),
        pltpu.VMEM((2 * GROUP + 8, 128), jnp.int32),
        pltpu.VMEM((SLOTS, 2 * NG, NG), jnp.bfloat16),
        pltpu.VMEM(((CH + 1) * BLOCK, NG), jnp.float32),
        pltpu.VMEM((FB, 2, row_block, NG), jnp.float32),
        pltpu.SMEM((2 * GROUP + 8, 128), jnp.int32),
        pltpu.SemaphoreType.DMA,
        pltpu.SemaphoreType.DMA((FB,)),
    ]
    scratch.append(pltpu.VMEM((SIDE, ROWS, LARGE), jnp.float32))
    scratch += [pltpu.VMEM((LARGE + COPY, 128), jnp.float32)] * SIDE
    if runs != GROUP:
        scratch.append(pltpu.VMEM((CH + 1, NG, NG), jnp.float32))
    return pl.pallas_call(
        functools.partial(grid_kernel, 1.0 / math.sqrt(NG), row_block),
        out_shape=jax.ShapeDtypeStruct((FB, 2, row_block, NG), jnp.float32),
        in_specs=[whole()],
        out_specs=whole(pl.ANY),
        scratch_shapes=scratch,
        compiler_params=params,
        name="grid",
    )(lists)


def solution(mesh):
    return jax.shard_map(
        per_device,
        mesh=mesh,
        in_specs=(P("tile", "band", None), P("tile", None, None), P("tile", None)),
        out_specs=P("band", None, "tile", None),
        check_vma=False,
    )
```

```python
import functools
import math

import jax
import jax.numpy as jnp
import ml_dtypes
import numpy as np
from jax import lax
from jax.experimental import pallas as pl
from jax.experimental.pallas import tpu as pltpu
from jax.sharding import PartitionSpec as P

NG = 512
NT = 2048
FB = 10
CH = 2 * FB
ROWS = 24
BLOCK = 16
BLOCKS = NG // BLOCK
GROUP = 32
COPY = 32
WIDTHS = (256, 512, 640)
LARGE = WIDTHS[-1]
BESIDE = 5
SIDE = 4
TURN = 256
HALF = 256
VMEM = 56 * 1024 * 1024


def twiddle_rows(band_count):
    time_index = np.arange(NT)[None, None, :]
    freq_index = np.arange(band_count * FB).reshape(band_count, FB, 1) + 1
    angle = (time_index * freq_index % NT) * (2.0 * math.pi / NT)
    norm = 1.0 / math.sqrt(NT)
    table = np.zeros((band_count, ROWS, NT), np.float64)
    table[:, :FB] = np.cos(angle) * norm
    table[:, FB:CH] = -np.sin(angle) * norm
    return table.reshape(band_count * ROWS, NT).astype(ml_dtypes.bfloat16)


def contract_last(left, right):
    return lax.dot_general(
        left, right, (((1,), (1,)), ((), ())), preferred_element_type=jnp.float32
    )


def run_kernel(cells_dev, twiddle_ref, traces_ref, owner_ref, offset_ref, out_ref):
    tiles, bands, _, count = out_ref.shape
    lanes = pl.ds(pl.multiple_of(lax.axis_index("band") * count, count), count)
    cell = owner_ref[:, lanes] * cells_dev + offset_ref[:, lanes]
    order = cell * count + lax.broadcasted_iota(jnp.int32, (1, count), 1)
    rank = jnp.zeros((1, count), jnp.int32)
    starts = jnp.zeros((1, count), jnp.int32)
    limit = lax.broadcasted_iota(jnp.int32, (1, count), 1) * (BLOCK * NG * count)
    limit = jnp.minimum(limit, NG * NG * count)
    for first in range(0, count, 128):
        column = jnp.transpose(jnp.broadcast_to(order[:, first : first + 128], (128, 128)))
        column = jnp.concatenate([column] * (count // 128), axis=1)
        rank += jnp.sum((column < order).astype(jnp.int32), axis=0, keepdims=True)
        starts += jnp.sum((column < limit).astype(jnp.int32), axis=0, keepdims=True)
    target = lax.broadcasted_iota(jnp.int32, (count, count), 0)
    permute = (target == rank).astype(jnp.float32).astype(jnp.bfloat16)
    source = cell // NG
    receiver = cell % NG
    row = lax.broadcasted_iota(jnp.int32, (bands * ROWS, count), 0) % ROWS
    digits = jnp.where(row == CH + 1, source % BLOCK, 0)
    digits = jnp.where(row == CH + 2, receiver // HALF, digits)
    digits = jnp.where(row == CH + 3, receiver % HALF, digits)
    spectra = contract_last(twiddle_ref[...], traces_ref[0])
    packed = (spectra + digits.astype(jnp.float32)).astype(jnp.bfloat16)
    ordered = contract_last(packed, permute) + jnp.where(row == CH, starts, 0).astype(jnp.float32)
    for band in range(bands):
        part = ordered[band * ROWS : (band + 1) * ROWS].astype(jnp.bfloat16)
        for tile in range(tiles):
            out_ref[tile, band] = part


def make_table(first_run, lists_ref, keys, table, table_s, sem):
    length = lists_ref.shape[2]
    for r in range(GROUP):
        part = lists_ref[first_run + r].astype(jnp.float32)
        keys[r : r + 1, :] = part[CH : CH + 1, :128]
    starts = keys[...]
    lane = lax.broadcasted_iota(jnp.int32, (GROUP, 128), 1)
    sizes = jnp.where(lane < BLOCKS, pltpu.roll(starts, 127, 1) - starts, 0.0)
    earlier = lax.broadcasted_iota(jnp.int32, (GROUP, GROUP), 0) > lax.broadcasted_iota(
        jnp.int32, (GROUP, GROUP), 1
    )
    targets = jnp.dot(
        earlier.astype(jnp.float32).astype(jnp.bfloat16),
        sizes.astype(jnp.bfloat16),
        preferred_element_type=jnp.float32,
    )
    run = lax.broadcasted_iota(jnp.int32, (GROUP, 128), 0)
    table[:GROUP, :] = starts.astype(jnp.int32) + run * length
    table[GROUP : 2 * GROUP, :] = jnp.minimum(targets, float(LARGE)).astype(jnp.int32)
    widest = jnp.max(sizes, axis=0, keepdims=True)
    total = jnp.sum(sizes, axis=0, keepdims=True)
    last = lax.broadcasted_iota(jnp.int32, (8, 128), 0)
    table[2 * GROUP :, :] = jnp.where(last == 0, widest, total).astype(jnp.int32)
    copy = pltpu.make_async_copy(table, table_s, sem)
    copy.start()
    return copy


def turn_runs(first_run, lists_ref, flat):
    length = lists_ref.shape[2]
    for r in range(GROUP):
        part = lists_ref[first_run + r].astype(jnp.float32)
        for first in range(0, length, 128):
            at = r * length + first
            flat[at : at + 128, :ROWS] = jnp.transpose(part[:, first : first + 128])


def turned(first, width, packed):
    return jnp.concatenate(
        [jnp.transpose(packed[pl.ds(first + k, 128), :])[:ROWS] for k in range(0, width, 128)],
        axis=1,
    )


def products(part, size):
    width = part.shape[1]
    step = lax.broadcasted_iota(jnp.int32, (BLOCK, width), 0).astype(jnp.float32)
    step = step.astype(jnp.bfloat16)
    place = lax.broadcasted_iota(jnp.int32, (1, width), 1)
    one = jnp.ones((), jnp.bfloat16)
    none = jnp.zeros((), jnp.bfloat16)

    def spread(row):
        return jnp.broadcast_to(row, (BLOCK, width)).astype(jnp.bfloat16)

    hit = spread(jnp.where(place < size, part[CH + 1 : CH + 2], -1.0)) == step
    left = [jnp.where(hit, one, none)]
    left += [jnp.where(hit, spread(part[c : c + 1]), none) for c in range(CH)]
    left = jnp.concatenate(left, axis=0)
    for half in range(NG // HALF):
        low = spread(jnp.where(part[CH + 2 : CH + 3] == float(half), part[CH + 3 : CH + 4], -1.0))
        right = [
            jnp.where(low == step + jnp.bfloat16(j), one, none) for j in range(0, HALF, BLOCK)
        ]
        yield pl.ds(half * HALF, HALF), contract_last(left, jnp.concatenate(right, axis=0))


def block_rows(b):
    return pl.ds(pl.multiple_of(b * BLOCK, BLOCK), BLOCK)


def add_blocks(table_s, flat, buffers, later, packed, total, emit):
    sides = BLOCKS // SIDE

    def merge(i, q):
        b = jnp.minimum(i, sides - 1) * SIDE + q
        for r in range(GROUP):
            buffers[q][pl.ds(table_s[GROUP + r, b], COPY), :] = flat[pl.ds(table_s[r, b], COPY), :]
        later[q] = turned(0, LARGE, buffers[q])

    def fast(i, width):
        parts = [later[q, :, :width] for q in range(SIDE)]
        for q in range(SIDE):
            merge(i + 1, q)
            b = i * SIDE + q
            for lanes, sums in products(parts[q], table_s[2 * GROUP + 1, b]):
                emit(b, lanes, sums)

    def slow(b):
        def run(r, target):
            source = table_s[r, b]
            count = table_s[r, b + 1] - source

            def piece(k, _):
                packed[pl.ds(target + 8 * k, 8), :] = flat[pl.ds(source + 8 * k, 8), :]
                return 0

            lax.fori_loop(0, (count + 7) // 8, piece, 0)
            return target + count

        lax.fori_loop(0, GROUP, run, 0)
        total[...] = jnp.zeros_like(total)
        size = table_s[2 * GROUP + 1, b]

        def piece(k, _):
            first = pl.multiple_of(k * LARGE, LARGE)
            for lanes, sums in products(turned(first, LARGE, packed), size - first):
                total[:, lanes] += sums
            return 0

        lax.fori_loop(0, (size + LARGE - 1) // LARGE, piece, 0)
        for half in range(NG // HALF):
            lanes = pl.ds(half * HALF, HALF)
            emit(b, lanes, total[:, lanes])

    def side(i, _):
        b = i * SIDE
        widest = table_s[2 * GROUP, b]
        largest = table_s[2 * GROUP + 1, b]
        for q in range(1, SIDE):
            widest = jnp.maximum(widest, table_s[2 * GROUP, b + q])
            largest = jnp.maximum(largest, table_s[2 * GROUP + 1, b + q])
        plain = widest <= COPY
        least = -1
        for width in WIDTHS:

            @pl.when(plain & (largest > least) & (largest <= width))
            def _(width=width):
                fast(i, width)

            least = width

        @pl.when(jnp.logical_not(plain) | (largest > LARGE))
        def _():
            for q in range(SIDE):
                merge(i + 1, q)
            lax.fori_loop(0, SIDE, lambda q, _: (slow(b + q), 0)[1], 0)

        return 0

    for q in range(SIDE):
        merge(jnp.int32(0), q)
    lax.fori_loop(0, sides, side, 0)


def grid_kernel(
    scale, row_block, lists_ref, out_ref, planes, flat, packed, keys, table, twice, total, result,
    table_s, sem, out_sems, *rest
):
    runs = lists_ref.shape[0]
    alone = runs == GROUP
    later, *buffers = rest[: SIDE + 1]
    grid = rest[SIDE + 1] if not alone else None

    def finish(sums, rows, lanes):
        inverse = 1.0 / jnp.maximum(sums(0), 1.0)
        for c in range(CH):
            planes[c, rows, lanes] = (sums(c + 1) * inverse).astype(jnp.bfloat16)

    def emit(b, lanes, sums):
        rows = block_rows(b)
        if alone:
            finish(lambda c: sums[c * BLOCK : (c + 1) * BLOCK], rows, lanes)
        else:
            for c in range(CH + 1):
                grid[c, rows, lanes] += sums[c * BLOCK : (c + 1) * BLOCK]

    def group(g, _):
        copy = make_table(g * GROUP, lists_ref, keys, table, table_s, sem)
        turn_runs(g * GROUP, lists_ref, flat)
        copy.wait()
        add_blocks(table_s, flat, buffers, later, packed, total, emit)
        return 0

    if alone:
        group(0, 0)
    else:
        grid[...] = jnp.zeros_like(grid)
        lax.fori_loop(0, runs // GROUP, group, 0)

        def divide(b, _):
            rows = block_rows(b)
            finish(lambda c: grid[c, rows, :], rows, pl.ds(0, NG))
            return 0

        lax.fori_loop(0, BLOCKS, divide, 0)

    first_row = pl.multiple_of(lax.axis_index("tile") * row_block, row_block)

    def sent(f):
        return pltpu.make_async_copy(result.at[f], out_ref.at[f], out_sems.at[f])

    def frequency(f, slot):
        for part, p in enumerate((f, FB + f)):
            for i in range(0, NG, TURN):
                for j in range(0, NG, TURN):
                    across = jnp.transpose(planes[p, j : j + TURN, i : i + TURN])
                    twice[slot, part * NG + i : part * NG + i + TURN, j : j + TURN] = (
                        planes[p, i : i + TURN, j : j + TURN] + across
                    )
        real = twice[slot, pl.ds(first_row, row_block), :]
        imag = twice[slot, pl.ds(NG + first_row, row_block), :]
        own = jnp.concatenate(
            [jnp.concatenate([real, -imag], axis=1), jnp.concatenate([imag, real], axis=1)], axis=0
        )
        for half in range(NG // HALF):
            lanes = slice(half * HALF, (half + 1) * HALF)
            both = jnp.dot(own, twice[slot, :, lanes], preferred_element_type=jnp.float32)
            both = both * (0.25 * scale)
            result[f, 0, :, lanes] = both[:row_block]
            result[f, 1, :, lanes] = both[row_block:]
        sent(f).start()

    def some(i, _):
        for q in range(BESIDE):
            frequency(i * BESIDE + q, q)
        return 0

    lax.fori_loop(0, FB // BESIDE, some, 0)
    for f in range(FB):
        sent(f).wait()


def whole(space=pltpu.VMEM):
    return pl.BlockSpec(memory_space=space)


def per_device(raw_traces, bin_owner, bin_offset):
    band_count = lax.axis_size("band")
    tile_count = lax.axis_size("tile")
    length = bin_offset.shape[1]
    count = raw_traces.shape[1]
    cells_dev = NG * NG // tile_count
    row_block = NG // tile_count
    runs = band_count * tile_count
    params = pltpu.CompilerParams(vmem_limit_bytes=VMEM)

    own = pl.pallas_call(
        functools.partial(run_kernel, cells_dev),
        out_shape=jax.ShapeDtypeStruct((tile_count, band_count, ROWS, count), jnp.bfloat16),
        in_specs=[whole()] * 4,
        out_specs=whole(),
        compiler_params=params,
        name="own_run",
    )(
        jnp.asarray(twiddle_rows(band_count)),
        raw_traces,
        bin_owner.reshape(1, length),
        bin_offset,
    )
    lists = lax.all_to_all(
        own.reshape(runs, ROWS, count), ("tile", "band"), split_axis=0, concat_axis=0, tiled=True
    )

    traces = GROUP * count
    scratch = [
        pltpu.VMEM((CH, NG, NG), jnp.bfloat16),
        pltpu.VMEM((traces + COPY, 128), jnp.float32),
        pltpu.VMEM((traces + LARGE, 128), jnp.float32),
        pltpu.VMEM((GROUP, 128), jnp.float32),
        pltpu.VMEM((2 * GROUP + 8, 128), jnp.int32),
        pltpu.VMEM((BESIDE, 2 * NG, NG), jnp.bfloat16),
        pltpu.VMEM(((CH + 1) * BLOCK, NG), jnp.float32),
        pltpu.VMEM((FB, 2, row_block, NG), jnp.float32),
        pltpu.SMEM((2 * GROUP + 8, 128), jnp.int32),
        pltpu.SemaphoreType.DMA,
        pltpu.SemaphoreType.DMA((FB,)),
    ]
    scratch.append(pltpu.VMEM((SIDE, ROWS, LARGE), jnp.float32))
    scratch += [pltpu.VMEM((LARGE + COPY, 128), jnp.float32)] * SIDE
    if runs != GROUP:
        scratch.append(pltpu.VMEM((CH + 1, NG, NG), jnp.float32))
    return pl.pallas_call(
        functools.partial(grid_kernel, 1.0 / math.sqrt(NG), row_block),
        out_shape=jax.ShapeDtypeStruct((FB, 2, row_block, NG), jnp.float32),
        in_specs=[whole()],
        out_specs=whole(pl.ANY),
        scratch_shapes=scratch,
        compiler_params=params,
        name="grid",
    )(lists)


def solution(mesh):
    return jax.shard_map(
        per_device,
        mesh=mesh,
        in_specs=(P("tile", "band", None), P("tile", None, None), P("tile", None)),
        out_specs=P("band", None, "tile", None),
        check_vma=False,
    )
```
